128 devices in a mesh: shots: 32 (over y, z, core), depth: 4 (over x).
Axes of the slice: x: 4, y: 4, z: 4, core: 2. Of those that a mesh axis runs over, the one named last changes fastest.
Arguments:
- partials: float32 [512, 32, 4096], P('shots', 'depth'), may hold values from -6 to 6
- aperture: int32 [512], P('shots'), may hold values from -1 to 127, as said below
- owner_map: int32 [128], replicated, may hold values from 0 to 127, as said below
- dip_class: int32 [128], replicated, may hold values from 0 to 7
Outputs:
- smoothed: float32 [128, 32, 4096], P('shots', 'depth')
The draws below stay inside these ranges and needn't reach their ends.
Inputs may be any that keep to these rules, and one draw needn't show every extreme that they name: `aperture`: ids within one shot group are distinct; at most 1 of a group's bricks have storage rows r with the same r div 4, and some group reaches 1; some group fills all 16 slots; empty slots come after live ones. `owner_map`: A permutation of the bricks.
All inputs are finite; a program needn't handle non-finite values.
Results may differ from the reference program's by a relative error of at most 0.0003.
Values sent between devices are 32-bit elements; how exact they have to be, the bound alone decides.
No kernel may reach another device: no remote copies, remote signals or barrier semaphores. Data moves between devices by JAX's collectives and lax.ppermute only.
A program may use at most 128 MiB of HBM per device.

```python
import math
import jax
import jax.numpy as jnp
from jax import lax

BY = 64
B_DEV = 4
APER = 16
ITERS = 3
DIPS = 8
BXY = 4096
NZ = 32
NBRICK = 128
CAP = 1
N_SHOTS = 32


def shared_layout(key):
    perm_key, start_key, active_key, chosen_key, offset_key = jax.random.split(key, 5)
    owner_map = jax.random.permutation(perm_key, NBRICK).astype(jnp.int32)
    slot_brick = jnp.argsort(owner_map).astype(jnp.int32)
    senders = jnp.arange(N_SHOTS, dtype=jnp.int32)
    starting = jax.random.randint(start_key, (N_SHOTS,), 0, max(N_SHOTS // 4, 1), dtype=jnp.int32)
    offsets = jax.random.randint(offset_key, (N_SHOTS,), 0, B_DEV, dtype=jnp.int32)
    active_count = jax.random.randint(active_key, (N_SHOTS,), APER // 2, APER + 1, dtype=jnp.int32)
    chosen = jax.random.randint(chosen_key, (), 0, N_SHOTS, dtype=jnp.int32)
    active_count = jnp.where(senders == chosen, APER, active_count)
    slots = jnp.arange(APER, dtype=jnp.int32)
    owners = (starting[:, None] + slots[None, :] // CAP) % N_SHOTS
    within = (offsets[:, None] + slots[None, :] % CAP) % B_DEV
    bricks = slot_brick[owners * B_DEV + within]
    aperture = jnp.where(slots[None, :] < active_count[:, None], bricks, -1).reshape(-1).astype(jnp.int32)
    return (owner_map, aperture)


def draw_owner_map(key, part):
    return shared_layout(key)[0]


def draw_aperture(key, part):
    return shared_layout(key)[1]


def set_ends(values, stream_key, least, top_value):
    shape = values.shape
    place = [jax.random.randint(jax.random.fold_in(stream_key, axis), (), 0, shape[axis]) for axis in range(len(shape))]
    values = values.at[tuple(place)].set(least)
    longest = shape.index(max(shape))
    place[longest] = (place[longest] + 1) % shape[longest]
    return values.at[tuple(place)].set(top_value)


def shard_levels(key, shape, cuts, least, high):
    factor_of = 1.0
    for position, shards_of in cuts:
        draws = jax.random.uniform(jax.random.fold_in(jax.random.fold_in(key, 6), position), (shards_of,), jnp.float32, least / len(cuts), high / len(cuts))
        factor_of = factor_of * jnp.repeat(jnp.exp(draws), shape[position] // shards_of).reshape((-1,) + (1,) * (len(shape) - 1 - position))
    return factor_of


def centred(stream_key, shape, scale, limit, pieces=(), kind=jnp.bfloat16):
    entries = jax.random.normal(stream_key, shape, jnp.float32) * scale
    if len(pieces) > 0:
        entries = shard_levels(stream_key, shape, pieces, -0.22, 0.18) * entries
    return jnp.clip(entries, min=-limit, max=limit).astype(kind)


def setup_inputs(seed: int = 0) -> dict:
    streams_of = jax.random.split(jax.random.key(seed), 5)
    return {
        "partials": centred(streams_of[0], (N_SHOTS * APER, NZ, BXY), 1.0, 6.0, ((0, 32), (1, 4)), jnp.float32),
        "aperture": draw_aperture(jax.random.fold_in(streams_of[4], 71), 0),
        "owner_map": draw_owner_map(jax.random.fold_in(streams_of[4], 71), 0),
        "dip_class": set_ends(jax.random.randint(streams_of[3], (NBRICK,), 0, DIPS), jax.random.fold_in(streams_of[3], 1), 0, DIPS - 1).astype(jnp.int32),
    }


smoothing_rate = 0.15
tiny_value = 1e-6


def shifted(volume, step_x, step_y, row_width):
    count = volume.shape[-1]
    margin = row_width + 1
    padded = jnp.pad(volume, [(0, 0)] * (volume.ndim - 1) + [(margin, margin)])
    begin = margin + step_x * row_width + step_y
    moved = lax.slice_in_dim(padded, begin, begin + count, axis=volume.ndim - 1)
    column = jnp.arange(count) % row_width + step_y
    return jnp.where((column >= 0) & (column < row_width), moved, jnp.float32(0.0))


def smooth_x(volume, row_width):
    return (shifted(volume, -1, 0, row_width) + 2.0 * volume + shifted(volume, 1, 0, row_width)) * 0.25


def smooth_y(volume, row_width):
    return (shifted(volume, 0, -1, row_width) + 2.0 * volume + shifted(volume, 0, 1, row_width)) * 0.25


def derive_x(volume, row_width):
    return (shifted(volume, 1, 0, row_width) - shifted(volume, -1, 0, row_width)) * 0.5


def derive_y(volume, row_width):
    return (shifted(volume, 0, 1, row_width) - shifted(volume, 0, -1, row_width)) * 0.5


def depth_slice(extended, start, axis):
    length = extended.shape[axis] - 2
    return lax.slice_in_dim(extended, start, start + length, axis=axis)


def gradient_products(extended, row_width):
    lower_plane = depth_slice(extended, 0, 1)
    centre = depth_slice(extended, 1, 1)
    upper_plane = depth_slice(extended, 2, 1)
    along_depth = (lower_plane + 2.0 * centre + upper_plane) * 0.25
    grad_z = smooth_x(smooth_y((upper_plane - lower_plane) * 0.5, row_width), row_width)
    grad_x = smooth_y(derive_x(along_depth, row_width), row_width)
    grad_y = smooth_x(derive_y(along_depth, row_width), row_width)
    return jnp.stack([grad_z * grad_z, grad_x * grad_x, grad_y * grad_y, grad_z * grad_x, grad_z * grad_y, grad_x * grad_y])


def brick_normal(classes):
    tilt_angle = 0.2 + 0.1 * (classes % 4).astype(jnp.float32)
    azimuth = 0.3 + (math.pi / 2.0) * (classes // 4).astype(jnp.float32)
    norm_z = jnp.cos(tilt_angle)[:, None, None]
    norm_x = (jnp.sin(tilt_angle) * jnp.cos(azimuth))[:, None, None]
    norm_y = (jnp.sin(tilt_angle) * jnp.sin(azimuth))[:, None, None]
    return norm_z, norm_x, norm_y


def smooth_update(extended, tensor_ext, normal, row_width):
    tensor = (depth_slice(tensor_ext, 0, 2) + 2.0 * depth_slice(tensor_ext, 1, 2) + depth_slice(tensor_ext, 2, 2)) * 0.25
    tensor = smooth_x(smooth_y(tensor, row_width), row_width)
    lower_plane = depth_slice(extended, 0, 1)
    centre = depth_slice(extended, 1, 1)
    upper_plane = depth_slice(extended, 2, 1)
    second_zz = upper_plane + lower_plane - 2.0 * centre
    second_xx = shifted(centre, 1, 0, row_width) + shifted(centre, -1, 0, row_width) - 2.0 * centre
    second_yy = shifted(centre, 0, 1, row_width) + shifted(centre, 0, -1, row_width) - 2.0 * centre
    second_zx = (derive_x(upper_plane, row_width) - derive_x(lower_plane, row_width)) * 0.5
    second_zy = (derive_y(upper_plane, row_width) - derive_y(lower_plane, row_width)) * 0.5
    second_xy = derive_y(derive_x(centre, row_width), row_width)
    norm_z, norm_x, norm_y = normal
    curvature = (norm_z * norm_z * second_zz + norm_x * norm_x * second_xx + norm_y * norm_y * second_yy
                 + 2.0 * norm_z * norm_x * second_zx + 2.0 * norm_z * norm_y * second_zy + 2.0 * norm_x * norm_y * second_xy)
    aligned = (norm_z * norm_z * tensor[0] + norm_x * norm_x * tensor[1] + norm_y * norm_y * tensor[2]
               + 2.0 * norm_z * norm_x * tensor[3] + 2.0 * norm_z * norm_y * tensor[4] + 2.0 * norm_x * norm_y * tensor[5])
    weight = aligned / (tensor[0] + tensor[1] + tensor[2] + tiny_value)
    return centre + smoothing_rate * weight * (second_zz + second_xx + second_yy - curvature)


def reference(partials, aperture, owner_map, dip_class):
    safe_ids = jnp.where(aperture >= 0, aperture, NBRICK).astype(jnp.int32)
    by_brick = jax.ops.segment_sum(partials, safe_ids, num_segments=NBRICK + 1)[:NBRICK]
    slot_brick = jnp.argsort(owner_map).astype(jnp.int32)
    migrated = by_brick[slot_brick]
    classes = dip_class[slot_brick]

    def one_brick(pair):
        volume, klass = pair
        migrate = volume[None]
        normal = brick_normal(klass.reshape(1))
        for sweep in range(ITERS):
            extended = jnp.pad(migrate, ((0, 0), (1, 1), (0, 0)))
            products = gradient_products(extended, BY)
            tensor_ext = jnp.pad(products, ((0, 0), (0, 0), (1, 1), (0, 0)))
            migrate = smooth_update(extended, tensor_ext, normal, BY)
        return migrate[0]

    return lax.map(one_brick, (migrated, classes))
```

```python
import math

import jax
import jax.numpy as jnp
from jax import lax
from jax.experimental import pallas as pl
from jax.experimental.pallas import tpu as pltpu
from jax.sharding import PartitionSpec as P

STEPS = 16
HALO = 6
PLANES = 8
DEEP = PLANES + 2 * HALO
ITERS = 3
RATE = 0.15
TINY = 1e-6
TILES = 32


def lanes():
    return lax.broadcasted_iota(jnp.int32, (8, 128), 1)


def rows():
    return lax.broadcasted_iota(jnp.int32, (8, 128), 0)


def pack_kernel(aperture, owner_map, partials, out, slot_of, place_of):
    step = pl.program_id(0)
    owners = slot_of.shape[0]
    slots = partials.shape[0]
    per_step = out.shape[0]

    @pl.when(step == 0)
    def _():
        for owner in range(owners):
            slot_of[owner] = -1
        for slot in range(slots):
            brick = aperture[slot]

            @pl.when(brick >= 0)
            def _():
                row = owner_map[brick]
                slot_of[row // 4] = slot
                place_of[row // 4] = row % 4

    for j in range(per_step):
        owner = step * per_step + j
        slot = slot_of[owner]

        @pl.when(slot >= 0)
        def _():
            for tile in range(TILES):
                out[j, (tile % 8) * 4 + tile // 8] = partials[slot, :, tile * 128 : tile * 128 + 128]
            out[j, TILES] = jnp.full((8, 128), place_of[owner], jnp.int32).astype(jnp.float32)

        @pl.when(slot < 0)
        def _():
            for tile in range(TILES):
                out[j, tile] = jnp.zeros((8, 128), jnp.float32)
            out[j, TILES] = jnp.full((8, 128), -1.0, jnp.float32)


def pack(aperture, owner_map, partials, owners):
    slots, planes, columns = partials.shape
    per_step = 4
    return pl.pallas_call(
        pack_kernel,
        grid=(owners // per_step,),
        in_specs=[
            pl.BlockSpec(memory_space=pltpu.SMEM),
            pl.BlockSpec(memory_space=pltpu.SMEM),
            pl.BlockSpec((slots, planes, columns), lambda i: (0, 0, 0)),
        ],
        out_specs=pl.BlockSpec((per_step, TILES + 1, 8, 128), lambda i: (i, 0, 0, 0)),
        out_shape=jax.ShapeDtypeStruct((owners, TILES + 1, 8, 128), jnp.float32),
        scratch_shapes=[pltpu.SMEM((owners,), jnp.int32), pltpu.SMEM((owners,), jnp.int32)],
        compiler_params=pltpu.CompilerParams(vmem_limit_bytes=24 << 20),
        name="pack_blocks",
    )(aperture, owner_map, partials)


def merge_kernel(blocks, places, out):
    step = pl.program_id(0)
    senders = blocks.shape[0]
    low = lanes() < 64
    for half in range(2):

        def add(sender, sums):
            place = places[sender, 0]
            hits = [place == float(b) for b in range(4)]
            new = []
            for quarter in range(4):
                block = blocks[sender, half * 4 + quarter]
                for b in range(4):
                    new.append(sums[quarter * 4 + b] + jnp.where(hits[b], block, 0.0))
            return tuple(new)

        zero = jnp.zeros((8, 128), jnp.float32)
        sums = lax.fori_loop(0, senders, add, (zero,) * 16, unroll=4)
        for b in range(4):
            for upper in range(2):
                even = sums[(2 * upper) * 4 + b]
                odd = sums[(2 * upper + 1) * 4 + b]
                first = jnp.where(low, even, pltpu.roll(odd, 64, 1))
                second = jnp.where(low, pltpu.roll(even, 64, 1), odd)
                base = (step * 2 + half) * 16 + b * 2 + upper
                out[pl.ds(base, 8, stride=128), :] = first
                out[pl.ds(base + 8, 8, stride=128), :] = second


def merge(received):
    senders = received.shape[0]
    return pl.pallas_call(
        merge_kernel,
        grid=(4,),
        in_specs=[
            pl.BlockSpec((senders, 8, 8, 128), lambda i: (0, i, 0, 0)),
            pl.BlockSpec((senders, 1, 8, 128), lambda i: (0, TILES, 0, 0)),
        ],
        out_specs=pl.BlockSpec((PLANES * STEPS * 8, 128), lambda i: (0, 0)),
        out_shape=jax.ShapeDtypeStruct((PLANES * STEPS * 8, 128), jnp.float32),
        compiler_params=pltpu.CompilerParams(vmem_limit_bytes=24 << 20),
        name="merge_blocks",
    )(received, received)


def set_edges(field, plane, first, last):
    left_half = lanes() < 64
    lower_row = rows() % 2 == 0
    turned = pltpu.roll(last, 64, 1)
    below = jnp.where(lower_row, 0.0, pltpu.roll(turned, 1, 0))
    field[plane, 0] = jnp.where(left_half, below, turned)
    turned = pltpu.roll(first, 64, 1)
    above = jnp.where(lower_row, pltpu.roll(turned, 7, 0), 0.0)
    field[plane, STEPS + 1] = jnp.where(left_half, turned, above)


def smooth_kernel(bounds, coefs, lower, own, upper, out, image, other, along, total, final):
    column = lanes() % 64
    first_y = column == 0
    last_y = column == 63

    def after(f):
        return jnp.where(last_y, 0.0, pltpu.roll(f, 127, 1))

    def before(f):
        return jnp.where(first_y, 0.0, pltpu.roll(f, 1, 1))

    def blur_y(f):
        pair = f + after(f)
        return pair + jnp.where(first_y, f, pltpu.roll(pair, 1, 1))

    zero = jnp.zeros((8, 128), jnp.float32)
    for plane in (HALO - 1, HALO + PLANES):
        for step in range(STEPS + 2):
            other[plane, step] = zero
            along[plane, step] = zero
            total[plane, step] = zero

    def load(source, count, offset):
        @pl.loop(0, count)
        def _(plane):
            cells = [source[plane, step] for step in range(STEPS)]
            for step in range(STEPS):
                image[plane + offset, step + 1] = cells[step]
            set_edges(image, plane + offset, cells[0], cells[-1])

    load(lower, HALO, 0)
    load(own, PLANES, HALO)
    load(upper, HALO, HALO + PLANES)

    first_plane = bounds[0]
    end_plane = bounds[1]

    for sweep in range(ITERS):
        source = image if sweep % 2 == 0 else other
        target = other if sweep % 2 == 0 else image
        margin = 2 * sweep + 1

        @pl.loop(jnp.maximum(margin, first_plane), jnp.minimum(DEEP - margin, end_plane))
        def _(plane):
            norm_z, norm_x, norm_y = coefs[0], coefs[1], coefs[2]

            def depth_pair(step):
                low, mid, high = source[plane - 1, step], source[plane, step], source[plane + 1, step]
                return (low + mid) + (mid + high), high - low

            blurred, slopes = {}, {}
            blurred[0], slopes[0] = depth_pair(0)
            blurred[1], slopes[1] = depth_pair(1)
            slope_pair = slopes[0] + slopes[1]
            blur_pair = blurred[0] + blurred[1]
            ends = []
            for step in range(1, STEPS + 1):
                blurred[step + 1], slopes[step + 1] = depth_pair(step + 1)
                next_slope = slopes[step] + slopes[step + 1]
                next_blur = blurred[step] + blurred[step + 1]
                grad_z = blur_y(slope_pair + next_slope)
                grad_x = blur_y(blurred[step + 1] - blurred[step - 1])
                wide = blur_pair + next_blur
                grad_y = after(wide) - before(wide)
                slope_pair, blur_pair = next_slope, next_blur
                aligned = norm_z * grad_z + norm_x * grad_x + norm_y * grad_y
                aligned = aligned * aligned
                whole = grad_z * grad_z + grad_x * grad_x + grad_y * grad_y
                along[plane, step] = aligned
                total[plane, step] = whole
                if step in (1, STEPS):
                    ends.append((aligned, whole))
            set_edges(along, plane, ends[0][0], ends[1][0])
            set_edges(total, plane, ends[0][1], ends[1][1])

        margin += 1

        @pl.loop(jnp.maximum(margin, first_plane), jnp.minimum(DEEP - margin, end_plane))
        def _(plane):
            c_mid, c_zz, c_xx, c_yy, c_zx, c_zy, c_xy = [coefs[3 + i] for i in range(7)]

            def blur_z(field, step):
                low, mid, high = field[plane - 1, step], field[plane, step], field[plane + 1, step]
                return (low + mid) + (mid + high)

            def both(step):
                return blur_z(along, step), blur_z(total, step)

            def depth(step):
                return source[plane - 1, step], source[plane + 1, step]

            a_now, t_now = both(0)
            a_next, t_next = both(1)
            a_pair, t_pair = a_now + a_next, t_now + t_next
            low, high = depth(0)
            slope_before = high - low
            low, high = depth(1)
            slope, stack = high - low, high + low
            u_before, u_now = source[plane, 0], source[plane, 1]
            ends = []
            for step in range(1, STEPS + 1):
                a_now, t_now = a_next, t_next
                a_next, t_next = both(step + 1)
                a_new, t_new = a_now + a_next, t_now + t_next
                aligned = blur_y(a_pair + a_new)
                whole = blur_y(t_pair + t_new)
                a_pair, t_pair = a_new, t_new
                weight = aligned / (whole + jnp.float32(TINY * 65536.0))
                low, high = depth(step + 1)
                slope_after, stack_after = high - low, high + low
                u_after = source[plane, step + 1]
                side = u_after - u_before
                skew = c_zy * slope + c_xy * side
                level = c_yy * u_now
                change = (
                    c_mid * u_now
                    + c_zz * stack
                    + c_xx * (u_after + u_before)
                    + c_zx * (slope_after - slope_before)
                    + after(level + skew)
                    + before(level - skew)
                )
                new = u_now + weight * change
                slope_before, slope, stack = slope, slope_after, stack_after
                u_before, u_now = u_now, u_after
                if sweep == ITERS - 1:
                    base = pl.multiple_of((plane - HALO) * 128, 128) + (step - 1) * 8
                    final[pl.ds(base, 8), :] = new
                else:
                    target[plane, step] = new
                    if step in (1, STEPS):
                        ends.append(new)
            if sweep < ITERS - 1:
                set_edges(target, plane, ends[0], ends[1])

    low_half = lanes() < 64
    for b in range(4):
        for upper_half in range(2):
            for k in range(8):
                base = k * 16 + b * 2 + upper_half
                first = final[pl.ds(base, 8, stride=128), :]
                second = final[pl.ds(base + 8, 8, stride=128), :]
                tile = upper_half * 16 + k
                out[b, :, tile * 128 : tile * 128 + 128] = jnp.where(low_half, first, pltpu.roll(second, 64, 1))
                tile += 8
                out[b, :, tile * 128 : tile * 128 + 128] = jnp.where(low_half, pltpu.roll(first, 64, 1), second)


def smooth(bounds, coefs, lower, own, upper, interpret=False):
    field = pltpu.VMEM((DEEP, STEPS + 2, 8, 128), jnp.float32)
    vmem = pl.BlockSpec(memory_space=pltpu.VMEM)
    return pl.pallas_call(
        smooth_kernel,
        in_specs=[pl.BlockSpec(memory_space=pltpu.SMEM), vmem, vmem, vmem, vmem],
        out_specs=vmem,
        out_shape=jax.ShapeDtypeStruct((4, PLANES, STEPS * 256), jnp.float32),
        scratch_shapes=[field, field, field, field, pltpu.VMEM((PLANES * STEPS * 8, 128), jnp.float32)],
        compiler_params=pltpu.CompilerParams(vmem_limit_bytes=32 << 20),
        name="smooth_image",
        interpret=interpret,
    )(bounds, coefs, lower, own, upper)


def coefficients(classes):
    tilt = 0.2 + 0.1 * (classes % 4).astype(jnp.float32)
    azimuth = 0.3 + math.pi / 2.0 * (classes // 4).astype(jnp.float32)
    norm_z = jnp.cos(tilt)
    norm_x = jnp.sin(tilt) * jnp.cos(azimuth)
    norm_y = jnp.sin(tilt) * jnp.sin(azimuth)
    c_zz = RATE * (1.0 - norm_z * norm_z)
    c_xx = RATE * (1.0 - norm_x * norm_x)
    c_yy = RATE * (1.0 - norm_y * norm_y)
    cross = -0.5 * RATE
    values = jnp.stack(
        [
            norm_z,
            norm_x,
            norm_y,
            -2.0 * (c_zz + c_xx + c_yy),
            c_zz,
            c_xx,
            c_yy,
            cross * norm_z * norm_x,
            cross * norm_z * norm_y,
            cross * norm_x * norm_y,
        ]
    )
    return jnp.broadcast_to(jnp.repeat(values, 2, axis=1)[:, :, None], (10, 8, 128))


def local(partials, aperture, owner_map, dip_class):
    senders = lax.axis_size("shots")
    owned = owner_map.shape[0] // senders
    sent = pack(aperture, owner_map, partials, senders)
    received = lax.all_to_all(sent, "shots", 0, 0, tiled=True)
    image = merge(received).reshape(PLANES, STEPS, 8, 128)
    depth_count = lax.axis_size("depth")
    lower = lax.ppermute(image[PLANES - HALO :], "depth", [(i, i + 1) for i in range(depth_count - 1)])
    upper = lax.ppermute(image[:HALO], "depth", [(i + 1, i) for i in range(depth_count - 1)])
    mine = lax.axis_index("shots") * owned + jnp.arange(owned)
    classes = jnp.sum(jnp.where(owner_map[None, :] == mine[:, None], dip_class[None, :], 0), axis=1)
    place = lax.axis_index("depth")
    bounds = jnp.stack([HALO - place * PLANES, HALO + (depth_count - place) * PLANES]).astype(jnp.int32)
    return smooth(bounds, coefficients(classes), lower, image, upper)


def solution(mesh):
    placed = (P("shots", "depth", None), P("shots"), P(), P())
    return jax.shard_map(
        local, mesh=mesh, in_specs=placed, out_specs=P("shots", "depth", None), check_vma=False
    )
```

```python
import math

import jax
import jax.numpy as jnp
from jax import lax
from jax.experimental import pallas as pl
from jax.experimental.pallas import tpu as pltpu
from jax.sharding import PartitionSpec as P

STEPS = 16
HALO = 6
PLANES = 8
DEEP = PLANES + 2 * HALO
ITERS = 3
RATE = 0.15
TINY = 1e-6
TILES = 32
GROUP = 2


def lanes():
    return lax.broadcasted_iota(jnp.int32, (8, 128), 1)


def rows():
    return lax.broadcasted_iota(jnp.int32, (8, 128), 0)


def pack_kernel(aperture, owner_map, partials, out, slot_of, place_of):
    step = pl.program_id(0)
    owners = slot_of.shape[0]
    slots = partials.shape[0]
    per_step = out.shape[0]

    @pl.when(step == 0)
    def _():
        for owner in range(owners):
            slot_of[owner] = -1
        for slot in range(slots):
            brick = aperture[slot]

            @pl.when(brick >= 0)
            def _():
                row = owner_map[brick]
                slot_of[row // 4] = slot
                place_of[row // 4] = row % 4

    for j in range(per_step):
        owner = step * per_step + j
        slot = slot_of[owner]

        @pl.when(slot >= 0)
        def _():
            for tile in range(TILES):
                out[j, (tile % 8) * 4 + tile // 8] = partials[slot, :, tile * 128 : tile * 128 + 128]
            out[j, TILES] = jnp.full((8, 128), place_of[owner], jnp.int32).astype(jnp.float32)

        @pl.when(slot < 0)
        def _():
            for tile in range(TILES):
                out[j, tile] = jnp.zeros((8, 128), jnp.float32)
            out[j, TILES] = jnp.full((8, 128), -1.0, jnp.float32)


def pack(aperture, owner_map, partials, owners):
    slots, planes, columns = partials.shape
    per_step = 4
    return pl.pallas_call(
        pack_kernel,
        grid=(owners // per_step,),
        in_specs=[
            pl.BlockSpec(memory_space=pltpu.SMEM),
            pl.BlockSpec(memory_space=pltpu.SMEM),
            pl.BlockSpec((slots, planes, columns), lambda i: (0, 0, 0)),
        ],
        out_specs=pl.BlockSpec((per_step, TILES + 1, 8, 128), lambda i: (i, 0, 0, 0)),
        out_shape=jax.ShapeDtypeStruct((owners, TILES + 1, 8, 128), jnp.float32),
        scratch_shapes=[pltpu.SMEM((owners,), jnp.int32), pltpu.SMEM((owners,), jnp.int32)],
        compiler_params=pltpu.CompilerParams(vmem_limit_bytes=24 << 20),
        name="pack_blocks",
    )(aperture, owner_map, partials)


def merge_kernel(blocks, places, out):
    step = pl.program_id(0)
    senders = blocks.shape[0]
    low = lanes() < 64
    for half in range(2):

        def add(sender, sums):
            place = places[sender, 0]
            hits = [place == float(b) for b in range(4)]
            new = []
            for quarter in range(4):
                block = blocks[sender, half * 4 + quarter]
                for b in range(4):
                    new.append(sums[quarter * 4 + b] + jnp.where(hits[b], block, 0.0))
            return tuple(new)

        zero = jnp.zeros((8, 128), jnp.float32)
        sums = lax.fori_loop(0, senders, add, (zero,) * 16, unroll=4)
        for b in range(4):
            for upper in range(2):
                even = sums[(2 * upper) * 4 + b]
                odd = sums[(2 * upper + 1) * 4 + b]
                first = jnp.where(low, even, pltpu.roll(odd, 64, 1))
                second = jnp.where(low, pltpu.roll(even, 64, 1), odd)
                base = (step * 2 + half) * 16 + b * 2 + upper
                out[pl.ds(base, 8, stride=128), :] = first
                out[pl.ds(base + 8, 8, stride=128), :] = second


def merge(received):
    senders = received.shape[0]
    return pl.pallas_call(
        merge_kernel,
        grid=(4,),
        in_specs=[
            pl.BlockSpec((senders, 8, 8, 128), lambda i: (0, i, 0, 0)),
            pl.BlockSpec((senders, 1, 8, 128), lambda i: (0, TILES, 0, 0)),
        ],
        out_specs=pl.BlockSpec((PLANES * STEPS * 8, 128), lambda i: (0, 0)),
        out_shape=jax.ShapeDtypeStruct((PLANES * STEPS * 8, 128), jnp.float32),
        compiler_params=pltpu.CompilerParams(vmem_limit_bytes=24 << 20),
        name="merge_blocks",
    )(received, received)


def set_edges(field, plane, first, last):
    left_half = lanes() < 64
    lower_row = rows() % 2 == 0
    turned = pltpu.roll(last, 64, 1)
    below = jnp.where(lower_row, 0.0, pltpu.roll(turned, 1, 0))
    field[plane, 0] = jnp.where(left_half, below, turned)
    turned = pltpu.roll(first, 64, 1)
    above = jnp.where(lower_row, pltpu.roll(turned, 7, 0), 0.0)
    field[plane, STEPS + 1] = jnp.where(left_half, turned, above)


def smooth_kernel(bounds, coefs, lower, own, upper, out, image, other, blur, slope, along, total, final):
    column = lanes() % 64
    first_y = column == 0
    last_y = column == 63

    def after(f):
        return jnp.where(last_y, 0.0, pltpu.roll(f, 127, 1))

    def before(f):
        return jnp.where(first_y, 0.0, pltpu.roll(f, 1, 1))

    def blur_y(f):
        return (f + after(f)) + (f + before(f))

    zero = jnp.zeros((8, 128), jnp.float32)

    def clear(field, plane):
        for step in range(STEPS + 2):
            field[plane, step] = zero

    for plane in (HALO - 1, HALO + PLANES):
        clear(other, plane)

    def load(source, count, offset):
        @pl.loop(0, count)
        def _(plane):
            cells = [source[plane, step] for step in range(STEPS)]
            for step in range(STEPS):
                image[plane + offset, step + 1] = cells[step]
            set_edges(image, plane + offset, cells[0], cells[-1])

    load(lower, HALO, 0)
    load(own, PLANES, HALO)
    load(upper, HALO, HALO + PLANES)

    first_plane = bounds[0]
    end_plane = bounds[1]

    def along_y(source, plane):
        for step in range(STEPS + 2):
            cells = source[plane, step]
            up, down = after(cells), before(cells)
            blur[plane, step] = (cells + cells) + (up + down)
            slope[plane, step] = up - down

    def depth_blur(field, plane, step):
        deep = [field[plane - 1 + k, step] for k in range(GROUP + 2)]
        pairs = [deep[k] + deep[k + 1] for k in range(GROUP + 1)]
        return [pairs[k] + pairs[k + 1] for k in range(GROUP)], deep

    def depth_slope(deep):
        return [deep[k + 2] - deep[k] for k in range(GROUP)]

    for sweep in range(ITERS):
        source = image if sweep % 2 == 0 else other
        target = other if sweep % 2 == 0 else image
        margin = 2 * sweep + 1
        start = jnp.maximum(margin, first_plane - 1)
        stop = jnp.minimum(DEEP - margin, end_plane + 1)

        for k in range(GROUP + 1):
            along_y(source, start - 1 + k)

        @pl.loop(0, (stop - start) // GROUP)
        def _(group):
            plane = start + group * GROUP
            for k in range(GROUP):
                along_y(source, plane + GROUP + k)
            norm_z, norm_x, norm_y = coefs[0], coefs[1], coefs[2]

            flat, steep, wide = {}, {}, {}

            def prepare(step):
                flat[step], deep = depth_blur(blur, plane, step)
                steep[step] = depth_slope(deep)
                wide[step], _ = depth_blur(slope, plane, step)

            prepare(0)
            prepare(1)
            steep_pair = [steep[0][k] + steep[1][k] for k in range(GROUP)]
            wide_pair = [wide[0][k] + wide[1][k] for k in range(GROUP)]
            ends = {}
            for step in range(1, STEPS + 1):
                prepare(step + 1)
                for k in range(GROUP):
                    steep_next = steep[step][k] + steep[step + 1][k]
                    wide_next = wide[step][k] + wide[step + 1][k]
                    grad_z = steep_pair[k] + steep_next
                    grad_x = flat[step + 1][k] - flat[step - 1][k]
                    grad_y = wide_pair[k] + wide_next
                    steep_pair[k], wide_pair[k] = steep_next, wide_next
                    aligned = norm_z * grad_z + norm_x * grad_x + norm_y * grad_y
                    aligned = aligned * aligned
                    whole = grad_z * grad_z + grad_x * grad_x + grad_y * grad_y
                    along[plane + k, step] = aligned
                    total[plane + k, step] = whole
                    if step in (1, STEPS):
                        ends[step, k] = (aligned, whole)
            for k in range(GROUP):
                set_edges(along, plane + k, ends[1, k][0], ends[STEPS, k][0])
                set_edges(total, plane + k, ends[1, k][1], ends[STEPS, k][1])

        for outside, edge in ((first_plane == HALO, HALO - 1), (end_plane == HALO + PLANES, HALO + PLANES)):

            @pl.when(outside)
            def _():
                clear(along, edge)
                clear(total, edge)

        margin += 1
        begin = jnp.maximum(margin, first_plane)
        finish = jnp.minimum(DEEP - margin, end_plane)

        @pl.loop(0, (finish - begin) // GROUP)
        def _(group):
            plane = begin + group * GROUP
            c_mid, c_zz, c_xx, c_yy, c_zx, c_zy, c_xy = [coefs[3 + i] for i in range(7)]
            a_cells, t_cells, deep, tilted = {}, {}, {}, {}

            def prepare(step):
                a_cells[step], _ = depth_blur(along, plane, step)
                t_cells[step], _ = depth_blur(total, plane, step)
                deep[step] = [source[plane - 1 + k, step] for k in range(GROUP + 2)]
                steep = depth_slope(deep[step])
                tilted[step] = [c_zx * steep[k] + c_xy * slope[plane + k, step] for k in range(GROUP)]

            prepare(0)
            prepare(1)
            a_pair = [a_cells[0][k] + a_cells[1][k] for k in range(GROUP)]
            t_pair = [t_cells[0][k] + t_cells[1][k] for k in range(GROUP)]
            ends = {}
            for step in range(1, STEPS + 1):
                prepare(step + 1)
                lean = depth_slope([slope[plane - 1 + k, step] for k in range(GROUP + 2)])
                for k in range(GROUP):
                    a_new = a_cells[step][k] + a_cells[step + 1][k]
                    t_new = t_cells[step][k] + t_cells[step + 1][k]
                    aligned = blur_y(a_pair[k] + a_new)
                    whole = blur_y(t_pair[k] + t_new)
                    a_pair[k], t_pair[k] = a_new, t_new
                    weight = aligned / (whole + jnp.float32(TINY * 65536.0))
                    now = deep[step][k + 1]
                    change = (
                        (c_mid * now + c_zz * (deep[step][k] + deep[step][k + 2]))
                        + (c_xx * (deep[step - 1][k + 1] + deep[step + 1][k + 1]) + c_yy * blur[plane + k, step])
                        + ((tilted[step + 1][k] - tilted[step - 1][k]) + c_zy * lean[k])
                    )
                    new = now + weight * change
                    if sweep == ITERS - 1:
                        base = pl.multiple_of((plane + k - HALO) * 128, 128) + (step - 1) * 8
                        final[pl.ds(base, 8), :] = new
                    else:
                        target[plane + k, step] = new
                        if step in (1, STEPS):
                            ends[step, k] = new
            if sweep < ITERS - 1:
                for k in range(GROUP):
                    set_edges(target, plane + k, ends[1, k], ends[STEPS, k])

    low_half = lanes() < 64
    for b in range(4):
        for upper_half in range(2):
            for k in range(8):
                base = k * 16 + b * 2 + upper_half
                first = final[pl.ds(base, 8, stride=128), :]
                second = final[pl.ds(base + 8, 8, stride=128), :]
                tile = upper_half * 16 + k
                out[b, :, tile * 128 : tile * 128 + 128] = jnp.where(low_half, first, pltpu.roll(second, 64, 1))
                tile += 8
                out[b, :, tile * 128 : tile * 128 + 128] = jnp.where(low_half, pltpu.roll(first, 64, 1), second)


def smooth(bounds, coefs, lower, own, upper, interpret=False):
    field = pltpu.VMEM((DEEP + GROUP, STEPS + 2, 8, 128), jnp.float32)
    vmem = pl.BlockSpec(memory_space=pltpu.VMEM)
    return pl.pallas_call(
        smooth_kernel,
        in_specs=[pl.BlockSpec(memory_space=pltpu.SMEM), vmem, vmem, vmem, vmem],
        out_specs=vmem,
        out_shape=jax.ShapeDtypeStruct((4, PLANES, STEPS * 256), jnp.float32),
        scratch_shapes=[field] * 6 + [pltpu.VMEM((PLANES * STEPS * 8, 128), jnp.float32)],
        compiler_params=pltpu.CompilerParams(vmem_limit_bytes=32 << 20),
        name="smooth_image",
        interpret=interpret,
    )(bounds, coefs, lower, own, upper)


def coefficients(classes):
    tilt = 0.2 + 0.1 * (classes % 4).astype(jnp.float32)
    azimuth = 0.3 + math.pi / 2.0 * (classes // 4).astype(jnp.float32)
    norm_z = jnp.cos(tilt)
    norm_x = jnp.sin(tilt) * jnp.cos(azimuth)
    norm_y = jnp.sin(tilt) * jnp.sin(azimuth)
    c_zz = RATE * (1.0 - norm_z * norm_z)
    c_xx = RATE * (1.0 - norm_x * norm_x)
    c_yy = RATE * (1.0 - norm_y * norm_y)
    cross = -0.5 * RATE
    values = jnp.stack(
        [
            norm_z,
            norm_x,
            norm_y,
            -2.0 * (c_zz + c_xx + 2.0 * c_yy),
            c_zz,
            c_xx,
            c_yy,
            cross * norm_z * norm_x,
            cross * norm_z * norm_y,
            cross * norm_x * norm_y,
        ]
    )
    return jnp.broadcast_to(jnp.repeat(values, 2, axis=1)[:, :, None], (10, 8, 128))


def local(partials, aperture, owner_map, dip_class):
    senders = lax.axis_size("shots")
    owned = owner_map.shape[0] // senders
    sent = pack(aperture, owner_map, partials, senders)
    received = lax.all_to_all(sent, "shots", 0, 0, tiled=True)
    image = merge(received).reshape(PLANES, STEPS, 8, 128)
    depth_count = lax.axis_size("depth")
    lower = lax.ppermute(image[PLANES - HALO :], "depth", [(i, i + 1) for i in range(depth_count - 1)])
    upper = lax.ppermute(image[:HALO], "depth", [(i + 1, i) for i in range(depth_count - 1)])
    mine = lax.axis_index("shots") * owned + jnp.arange(owned)
    classes = jnp.sum(jnp.where(owner_map[None, :] == mine[:, None], dip_class[None, :], 0), axis=1)
    place = lax.axis_index("depth")
    bounds = jnp.stack([HALO - place * PLANES, HALO + (depth_count - place) * PLANES]).astype(jnp.int32)
    return smooth(bounds, coefficients(classes), lower, image, upper)


def solution(mesh):
    placed = (P("shots", "depth", None), P("shots"), P(), P())
    return jax.shard_map(
        local, mesh=mesh, in_specs=placed, out_specs=P("shots", "depth", None), check_vma=False
    )
```

```python
import math

import jax
import jax.numpy as jnp
from jax import lax
from jax.experimental import pallas as pl
from jax.experimental.pallas import tpu as pltpu
from jax.sharding import PartitionSpec as P

STEPS = 16
HALO = 6
PLANES = 8
DEEP = PLANES + 2 * HALO
ITERS = 3
RATE = 0.15
TINY = 1e-6
TILES = 32
GROUP = 2


def lanes():
    return lax.broadcasted_iota(jnp.int32, (8, 128), 1)


def rows():
    return lax.broadcasted_iota(jnp.int32, (8, 128), 0)


def pack_kernel(aperture_hbm, owner_map_hbm, partials, out, aperture, owner_map, places, table_sems, block_sems, place_sem):
    slots = partials.shape[0]
    columns = partials.shape[2]
    tables = [
        pltpu.make_async_copy(aperture_hbm, aperture, table_sems.at[0]),
        pltpu.make_async_copy(owner_map_hbm, owner_map, table_sems.at[1]),
    ]
    for copy in tables:
        copy.start()
    for owner in range(places.shape[0]):
        places[owner] = jnp.full((8, 128), -1.0, jnp.float32)
    for copy in tables:
        copy.wait()

    def block(slot, owner):
        return pltpu.make_async_copy(partials.at[slot], out.at[owner, :, 0:columns], block_sems.at[slot])

    for slot in range(slots):
        brick = aperture[slot]

        @pl.when(brick >= 0)
        def _():
            row = owner_map[brick]
            owner = row // 4
            block(slot, owner).start()
            places[owner] = jnp.full((8, 128), row % 4, jnp.int32).astype(jnp.float32)

    labels = pltpu.make_async_copy(places, out.at[:, :, columns : columns + 128], place_sem)
    labels.start()
    for slot in range(slots):

        @pl.when(aperture[slot] >= 0)
        def _():
            block(slot, 0).wait()

    labels.wait()


def pack(aperture, owner_map, partials, owners):
    slots, planes, columns = partials.shape
    hbm = pl.BlockSpec(memory_space=pltpu.HBM)
    return pl.pallas_call(
        pack_kernel,
        in_specs=[hbm, hbm, hbm],
        out_specs=hbm,
        out_shape=jax.ShapeDtypeStruct((owners, planes, columns + 128), jnp.float32),
        scratch_shapes=[
            pltpu.SMEM(aperture.shape, jnp.int32),
            pltpu.SMEM(owner_map.shape, jnp.int32),
            pltpu.VMEM((owners, planes, 128), jnp.float32),
            pltpu.SemaphoreType.DMA((2,)),
            pltpu.SemaphoreType.DMA((slots,)),
            pltpu.SemaphoreType.DMA,
        ],
        compiler_params=pltpu.CompilerParams(vmem_limit_bytes=60 << 20),
        name="pack_blocks",
    )(aperture, owner_map, partials)


def merge_kernel(received, out, places, blocks, sums, place_sem, block_sems):
    senders, planes, columns = blocks.shape
    labels = pltpu.make_async_copy(received.at[:, 0:1, columns : columns + 128], places, place_sem)
    labels.start()
    for brick in range(4):
        for tile in range(TILES):
            sums[brick, tile] = jnp.zeros((8, 128), jnp.float32)
    labels.wait()

    def block(sender):
        return pltpu.make_async_copy(
            received.at[sender, :, 0:columns], blocks.at[sender], block_sems.at[sender]
        )

    for sender in range(senders):

        @pl.when(places[sender, 0, 0] >= 0.0)
        def _():
            block(sender).start()

    for sender in range(senders):
        place = places[sender, 0, 0].astype(jnp.int32)

        @pl.when(place >= 0)
        def _():
            block(sender).wait()
            for tile in range(TILES):
                sums[place, tile] += blocks[sender, :, tile * 128 : tile * 128 + 128]

    low = lanes() < 64
    for b in range(4):
        for upper in range(2):
            for k in range(8):
                even = sums[b, upper * 16 + k]
                odd = sums[b, upper * 16 + 8 + k]
                base = k * 16 + b * 2 + upper
                out[pl.ds(base, 8, stride=128), :] = jnp.where(low, even, pltpu.roll(odd, 64, 1))
                out[pl.ds(base + 8, 8, stride=128), :] = jnp.where(low, pltpu.roll(even, 64, 1), odd)


def merge(received):
    senders, planes, columns = received.shape
    columns -= 128
    return pl.pallas_call(
        merge_kernel,
        in_specs=[pl.BlockSpec(memory_space=pltpu.HBM)],
        out_specs=pl.BlockSpec(memory_space=pltpu.VMEM),
        out_shape=jax.ShapeDtypeStruct((PLANES * STEPS * 8, 128), jnp.float32),
        scratch_shapes=[
            pltpu.SMEM((senders, 1, 128), jnp.float32),
            pltpu.VMEM((senders, planes, columns), jnp.float32),
            pltpu.VMEM((4, TILES, 8, 128), jnp.float32),
            pltpu.SemaphoreType.DMA,
            pltpu.SemaphoreType.DMA((senders,)),
        ],
        compiler_params=pltpu.CompilerParams(vmem_limit_bytes=48 << 20),
        name="merge_blocks",
    )(received)


def set_edges(field, plane, first, last):
    left_half = lanes() < 64
    lower_row = rows() % 2 == 0
    turned = pltpu.roll(last, 64, 1)
    below = jnp.where(lower_row, 0.0, pltpu.roll(turned, 1, 0))
    field[plane, 0] = jnp.where(left_half, below, turned)
    turned = pltpu.roll(first, 64, 1)
    above = jnp.where(lower_row, pltpu.roll(turned, 7, 0), 0.0)
    field[plane, STEPS + 1] = jnp.where(left_half, turned, above)


def smooth_kernel(bounds, coefs, lower, own, upper, out, image, other, blur, slope, along, total, final):
    column = lanes() % 64
    first_y = column == 0
    last_y = column == 63

    def after(f):
        return jnp.where(last_y, 0.0, pltpu.roll(f, 127, 1))

    def before(f):
        return jnp.where(first_y, 0.0, pltpu.roll(f, 1, 1))

    def blur_y(f):
        return (f + after(f)) + (f + before(f))

    zero = jnp.zeros((8, 128), jnp.float32)

    def clear(field, plane):
        for step in range(STEPS + 2):
            field[plane, step] = zero

    for plane in (HALO - 1, HALO + PLANES):
        clear(other, plane)

    def load(source, count, offset):
        @pl.loop(0, count)
        def _(plane):
            cells = [source[plane, step] for step in range(STEPS)]
            for step in range(STEPS):
                image[plane + offset, step + 1] = cells[step]
            set_edges(image, plane + offset, cells[0], cells[-1])

    load(lower, HALO, 0)
    load(own, PLANES, HALO)
    load(upper, HALO, HALO + PLANES)

    first_plane = bounds[0]
    end_plane = bounds[1]

    def along_y(source, plane):
        for step in range(STEPS + 2):
            cells = source[plane, step]
            up, down = after(cells), before(cells)
            blur[plane, step] = (cells + cells) + (up + down)
            slope[plane, step] = up - down

    def depth_blur(field, plane, step):
        deep = [field[plane - 1 + k, step] for k in range(GROUP + 2)]
        pairs = [deep[k] + deep[k + 1] for k in range(GROUP + 1)]
        return [pairs[k] + pairs[k + 1] for k in range(GROUP)], deep

    def depth_slope(deep):
        return [deep[k + 2] - deep[k] for k in range(GROUP)]

    for sweep in range(ITERS):
        source = image if sweep % 2 == 0 else other
        target = other if sweep % 2 == 0 else image
        margin = 2 * sweep + 1
        start = jnp.maximum(margin, first_plane - 1)
        stop = jnp.minimum(DEEP - margin, end_plane + 1)

        for k in range(GROUP + 1):
            along_y(source, start - 1 + k)

        @pl.loop(0, (stop - start) // GROUP)
        def _(group):
            plane = start + group * GROUP
            for k in range(GROUP):
                along_y(source, plane + GROUP + k)
            norm_z, norm_x, norm_y = coefs[0], coefs[1], coefs[2]

            flat, steep, wide = {}, {}, {}

            def prepare(step):
                flat[step], deep = depth_blur(blur, plane, step)
                steep[step] = depth_slope(deep)
                wide[step], _ = depth_blur(slope, plane, step)

            prepare(0)
            prepare(1)
            steep_pair = [steep[0][k] + steep[1][k] for k in range(GROUP)]
            wide_pair = [wide[0][k] + wide[1][k] for k in range(GROUP)]
            ends = {}
            for step in range(1, STEPS + 1):
                prepare(step + 1)
                for k in range(GROUP):
                    steep_next = steep[step][k] + steep[step + 1][k]
                    wide_next = wide[step][k] + wide[step + 1][k]
                    grad_z = steep_pair[k] + steep_next
                    grad_x = flat[step + 1][k] - flat[step - 1][k]
                    grad_y = wide_pair[k] + wide_next
                    steep_pair[k], wide_pair[k] = steep_next, wide_next
                    aligned = norm_z * grad_z + norm_x * grad_x + norm_y * grad_y
                    aligned = aligned * aligned
                    whole = grad_z * grad_z + grad_x * grad_x + grad_y * grad_y
                    along[plane + k, step] = aligned
                    total[plane + k, step] = whole
                    if step in (1, STEPS):
                        ends[step, k] = (aligned, whole)
            for k in range(GROUP):
                set_edges(along, plane + k, ends[1, k][0], ends[STEPS, k][0])
                set_edges(total, plane + k, ends[1, k][1], ends[STEPS, k][1])

        for outside, edge in ((first_plane == HALO, HALO - 1), (end_plane == HALO + PLANES, HALO + PLANES)):

            @pl.when(outside)
            def _():
                clear(along, edge)
                clear(total, edge)

        margin += 1
        begin = jnp.maximum(margin, first_plane)
        finish = jnp.minimum(DEEP - margin, end_plane)

        @pl.loop(0, (finish - begin) // GROUP)
        def _(group):
            plane = begin + group * GROUP
            c_mid, c_zz, c_xx, c_yy, c_zx, c_zy, c_xy = [coefs[3 + i] for i in range(7)]
            a_cells, t_cells, deep, tilted = {}, {}, {}, {}

            def prepare(step):
                a_cells[step], _ = depth_blur(along, plane, step)
                t_cells[step], _ = depth_blur(total, plane, step)
                deep[step] = [source[plane - 1 + k, step] for k in range(GROUP + 2)]
                steep = depth_slope(deep[step])
                tilted[step] = [c_zx * steep[k] + c_xy * slope[plane + k, step] for k in range(GROUP)]

            prepare(0)
            prepare(1)
            a_pair = [a_cells[0][k] + a_cells[1][k] for k in range(GROUP)]
            t_pair = [t_cells[0][k] + t_cells[1][k] for k in range(GROUP)]
            ends = {}
            for step in range(1, STEPS + 1):
                prepare(step + 1)
                lean = depth_slope([slope[plane - 1 + k, step] for k in range(GROUP + 2)])
                for k in range(GROUP):
                    a_new = a_cells[step][k] + a_cells[step + 1][k]
                    t_new = t_cells[step][k] + t_cells[step + 1][k]
                    aligned = blur_y(a_pair[k] + a_new)
                    whole = blur_y(t_pair[k] + t_new)
                    a_pair[k], t_pair[k] = a_new, t_new
                    weight = aligned / (whole + jnp.float32(TINY * 65536.0))
                    now = deep[step][k + 1]
                    change = (
                        (c_mid * now + c_zz * (deep[step][k] + deep[step][k + 2]))
                        + (c_xx * (deep[step - 1][k + 1] + deep[step + 1][k + 1]) + c_yy * blur[plane + k, step])
                        + ((tilted[step + 1][k] - tilted[step - 1][k]) + c_zy * lean[k])
                    )
                    new = now + weight * change
                    if sweep == ITERS - 1:
                        base = pl.multiple_of((plane + k - HALO) * 128, 128) + (step - 1) * 8
                        final[pl.ds(base, 8), :] = new
                    else:
                        target[plane + k, step] = new
                        if step in (1, STEPS):
                            ends[step, k] = new
            if sweep < ITERS - 1:
                for k in range(GROUP):
                    set_edges(target, plane + k, ends[1, k], ends[STEPS, k])

    low_half = lanes() < 64
    for b in range(4):
        for upper_half in range(2):
            for k in range(8):
                base = k * 16 + b * 2 + upper_half
                first = final[pl.ds(base, 8, stride=128), :]
                second = final[pl.ds(base + 8, 8, stride=128), :]
                tile = upper_half * 16 + k
                out[b, :, tile * 128 : tile * 128 + 128] = jnp.where(low_half, first, pltpu.roll(second, 64, 1))
                tile += 8
                out[b, :, tile * 128 : tile * 128 + 128] = jnp.where(low_half, pltpu.roll(first, 64, 1), second)


def smooth(bounds, coefs, lower, own, upper, interpret=False):
    field = pltpu.VMEM((DEEP + GROUP, STEPS + 2, 8, 128), jnp.float32)
    vmem = pl.BlockSpec(memory_space=pltpu.VMEM)
    return pl.pallas_call(
        smooth_kernel,
        in_specs=[pl.BlockSpec(memory_space=pltpu.SMEM), vmem, vmem, vmem, vmem],
        out_specs=vmem,
        out_shape=jax.ShapeDtypeStruct((4, PLANES, STEPS * 256), jnp.float32),
        scratch_shapes=[field] * 6 + [pltpu.VMEM((PLANES * STEPS * 8, 128), jnp.float32)],
        compiler_params=pltpu.CompilerParams(vmem_limit_bytes=32 << 20),
        name="smooth_image",
        interpret=interpret,
    )(bounds, coefs, lower, own, upper)


def coefficients(classes):
    tilt = 0.2 + 0.1 * (classes % 4).astype(jnp.float32)
    azimuth = 0.3 + math.pi / 2.0 * (classes // 4).astype(jnp.float32)
    norm_z = jnp.cos(tilt)
    norm_x = jnp.sin(tilt) * jnp.cos(azimuth)
    norm_y = jnp.sin(tilt) * jnp.sin(azimuth)
    c_zz = RATE * (1.0 - norm_z * norm_z)
    c_xx = RATE * (1.0 - norm_x * norm_x)
    c_yy = RATE * (1.0 - norm_y * norm_y)
    cross = -0.5 * RATE
    values = jnp.stack(
        [
            norm_z,
            norm_x,
            norm_y,
            -2.0 * (c_zz + c_xx + 2.0 * c_yy),
            c_zz,
            c_xx,
            c_yy,
            cross * norm_z * norm_x,
            cross * norm_z * norm_y,
            cross * norm_x * norm_y,
        ]
    )
    return jnp.broadcast_to(jnp.repeat(values, 2, axis=1)[:, :, None], (10, 8, 128))


def local(partials, aperture, owner_map, dip_class):
    senders = lax.axis_size("shots")
    owned = owner_map.shape[0] // senders
    sent = pack(aperture, owner_map, partials, senders)
    received = lax.all_to_all(sent, "shots", 0, 0, tiled=True)
    image = merge(received).reshape(PLANES, STEPS, 8, 128)
    depth_count = lax.axis_size("depth")
    lower = lax.ppermute(image[PLANES - HALO :], "depth", [(i, i + 1) for i in range(depth_count - 1)])
    upper = lax.ppermute(image[:HALO], "depth", [(i + 1, i) for i in range(depth_count - 1)])
    mine = lax.axis_index("shots") * owned + jnp.arange(owned)
    classes = jnp.sum(jnp.where(owner_map[None, :] == mine[:, None], dip_class[None, :], 0), axis=1)
    place = lax.axis_index("depth")
    bounds = jnp.stack([HALO - place * PLANES, HALO + (depth_count - place) * PLANES]).astype(jnp.int32)
    return smooth(bounds, coefficients(classes), lower, image, upper)


def solution(mesh):
    placed = (P("shots", "depth", None), P("shots"), P(), P())
    return jax.shard_map(
        local, mesh=mesh, in_specs=placed, out_specs=P("shots", "depth", None), check_vma=False
    )
```

```python
import math

import jax
import jax.numpy as jnp
from jax import lax
from jax.experimental import pallas as pl
from jax.experimental.pallas import tpu as pltpu
from jax.sharding import PartitionSpec as P

STEPS = 16
HALO = 6
PLANES = 8
DEEP = PLANES + 2 * HALO
ITERS = 3
RATE = 0.15
TINY = 1e-6
TILES = 32
GROUP = 2


def lanes():
    return lax.broadcasted_iota(jnp.int32, (8, 128), 1)


def rows():
    return lax.broadcasted_iota(jnp.int32, (8, 128), 0)


def pack_kernel(
    aperture_hbm, owner_map_hbm, partials, out, aperture, owner_map, blocks, places, table_sems, in_sems, out_sems, place_sem
):
    slots = partials.shape[0]
    columns = partials.shape[2]
    tables = [
        pltpu.make_async_copy(aperture_hbm, aperture, table_sems.at[0]),
        pltpu.make_async_copy(owner_map_hbm, owner_map, table_sems.at[1]),
    ]
    for copy in tables:
        copy.start()
    fetches = [pltpu.make_async_copy(partials.at[slot], blocks.at[slot], in_sems.at[slot]) for slot in range(slots)]
    for fetch in fetches:
        fetch.start()
    for owner in range(places.shape[0]):
        places[owner] = jnp.full((8, 128), -1.0, jnp.float32)
    for copy in tables:
        copy.wait()

    def block(slot, owner):
        return pltpu.make_async_copy(blocks.at[slot], out.at[owner, :, 0:columns], out_sems.at[slot])

    for slot in range(slots):
        fetches[slot].wait()
        brick = aperture[slot]

        @pl.when(brick >= 0)
        def _():
            row = owner_map[brick]
            owner = row // 4
            block(slot, owner).start()
            places[owner] = jnp.full((8, 128), row % 4, jnp.int32).astype(jnp.float32)

    labels = pltpu.make_async_copy(places, out.at[:, :, columns : columns + 128], place_sem)
    labels.start()
    for slot in range(slots):

        @pl.when(aperture[slot] >= 0)
        def _():
            block(slot, 0).wait()

    labels.wait()


def pack(aperture, owner_map, partials, owners):
    slots, planes, columns = partials.shape
    hbm = pl.BlockSpec(memory_space=pltpu.HBM)
    return pl.pallas_call(
        pack_kernel,
        in_specs=[hbm, hbm, hbm],
        out_specs=hbm,
        out_shape=jax.ShapeDtypeStruct((owners, planes, columns + 128), jnp.float32),
        scratch_shapes=[
            pltpu.SMEM(aperture.shape, jnp.int32),
            pltpu.SMEM(owner_map.shape, jnp.int32),
            pltpu.VMEM(partials.shape, jnp.float32),
            pltpu.VMEM((owners, planes, 128), jnp.float32),
            pltpu.SemaphoreType.DMA((2,)),
            pltpu.SemaphoreType.DMA((slots,)),
            pltpu.SemaphoreType.DMA((slots,)),
            pltpu.SemaphoreType.DMA,
        ],
        compiler_params=pltpu.CompilerParams(vmem_limit_bytes=60 << 20),
        name="pack_blocks",
    )(aperture, owner_map, partials)


def merge_kernel(received, out, places, blocks, sums, place_sem, block_sems):
    senders, planes, columns = blocks.shape
    labels = pltpu.make_async_copy(received.at[:, 0:1, columns : columns + 128], places, place_sem)
    labels.start()
    for brick in range(4):
        for tile in range(TILES):
            sums[brick, tile] = jnp.zeros((8, 128), jnp.float32)
    labels.wait()

    def block(sender):
        return pltpu.make_async_copy(
            received.at[sender, :, 0:columns], blocks.at[sender], block_sems.at[sender]
        )

    for sender in range(senders):

        @pl.when(places[sender, 0, 0] >= 0.0)
        def _():
            block(sender).start()

    for sender in range(senders):
        place = places[sender, 0, 0].astype(jnp.int32)

        @pl.when(place >= 0)
        def _():
            block(sender).wait()
            for tile in range(TILES):
                sums[place, tile] += blocks[sender, :, tile * 128 : tile * 128 + 128]

    low = lanes() < 64
    for b in range(4):
        for upper in range(2):
            for k in range(8):
                even = sums[b, upper * 16 + k]
                odd = sums[b, upper * 16 + 8 + k]
                base = k * 16 + b * 2 + upper
                out[pl.ds(base, 8, stride=128), :] = jnp.where(low, even, pltpu.roll(odd, 64, 1))
                out[pl.ds(base + 8, 8, stride=128), :] = jnp.where(low, pltpu.roll(even, 64, 1), odd)


def merge(received):
    senders, planes, columns = received.shape
    columns -= 128
    return pl.pallas_call(
        merge_kernel,
        in_specs=[pl.BlockSpec(memory_space=pltpu.HBM)],
        out_specs=pl.BlockSpec(memory_space=pltpu.VMEM),
        out_shape=jax.ShapeDtypeStruct((PLANES * STEPS * 8, 128), jnp.float32),
        scratch_shapes=[
            pltpu.SMEM((senders, 1, 128), jnp.float32),
            pltpu.VMEM((senders, planes, columns), jnp.float32),
            pltpu.VMEM((4, TILES, 8, 128), jnp.float32),
            pltpu.SemaphoreType.DMA,
            pltpu.SemaphoreType.DMA((senders,)),
        ],
        compiler_params=pltpu.CompilerParams(vmem_limit_bytes=48 << 20),
        name="merge_blocks",
    )(received)


def set_edges(field, plane, first, last):
    left_half = lanes() < 64
    lower_row = rows() % 2 == 0
    turned = pltpu.roll(last, 64, 1)
    below = jnp.where(lower_row, 0.0, pltpu.roll(turned, 1, 0))
    field[plane, 0] = jnp.where(left_half, below, turned)
    turned = pltpu.roll(first, 64, 1)
    above = jnp.where(lower_row, pltpu.roll(turned, 7, 0), 0.0)
    field[plane, STEPS + 1] = jnp.where(left_half, turned, above)


def smooth_kernel(bounds, coefs, lower, own, upper, out, image, other, blur, slope, along, total, final):
    column = lanes() % 64
    first_y = column == 0
    last_y = column == 63

    def after(f):
        return jnp.where(last_y, 0.0, pltpu.roll(f, 127, 1))

    def before(f):
        return jnp.where(first_y, 0.0, pltpu.roll(f, 1, 1))

    def blur_y(f):
        return (f + after(f)) + (f + before(f))

    zero = jnp.zeros((8, 128), jnp.float32)

    def clear(field, plane):
        for step in range(STEPS + 2):
            field[plane, step] = zero

    for plane in (HALO - 1, HALO + PLANES):
        clear(other, plane)

    def load(source, count, offset):
        @pl.loop(0, count)
        def _(plane):
            cells = [source[plane, step] for step in range(STEPS)]
            for step in range(STEPS):
                image[plane + offset, step + 1] = cells[step]
            set_edges(image, plane + offset, cells[0], cells[-1])

    load(lower, HALO, 0)
    load(own, PLANES, HALO)
    load(upper, HALO, HALO + PLANES)

    first_plane = bounds[0]
    end_plane = bounds[1]

    def along_y(source, plane):
        for step in range(STEPS + 2):
            cells = source[plane, step]
            up, down = after(cells), before(cells)
            blur[plane, step] = (cells + cells) + (up + down)
            slope[plane, step] = up - down

    def depth_blur(field, plane, step):
        deep = [field[plane - 1 + k, step] for k in range(GROUP + 2)]
        pairs = [deep[k] + deep[k + 1] for k in range(GROUP + 1)]
        return [pairs[k] + pairs[k + 1] for k in range(GROUP)], deep

    def depth_slope(deep):
        return [deep[k + 2] - deep[k] for k in range(GROUP)]

    for sweep in range(ITERS):
        source = image if sweep % 2 == 0 else other
        target = other if sweep % 2 == 0 else image
        margin = 2 * sweep + 1
        start = jnp.maximum(margin, first_plane - 1)
        stop = jnp.minimum(DEEP - margin, end_plane + 1)

        for k in range(GROUP + 1):
            along_y(source, start - 1 + k)

        @pl.loop(0, (stop - start) // GROUP)
        def _(group):
            plane = start + group * GROUP
            for k in range(GROUP):
                along_y(source, plane + GROUP + k)
            norm_z, norm_x, norm_y = coefs[0], coefs[1], coefs[2]

            flat, steep, wide = {}, {}, {}

            def prepare(step):
                flat[step], deep = depth_blur(blur, plane, step)
                steep[step] = depth_slope(deep)
                wide[step], _ = depth_blur(slope, plane, step)

            prepare(0)
            prepare(1)
            steep_pair = [steep[0][k] + steep[1][k] for k in range(GROUP)]
            wide_pair = [wide[0][k] + wide[1][k] for k in range(GROUP)]
            ends = {}
            for step in range(1, STEPS + 1):
                prepare(step + 1)
                for k in range(GROUP):
                    steep_next = steep[step][k] + steep[step + 1][k]
                    wide_next = wide[step][k] + wide[step + 1][k]
                    grad_z = steep_pair[k] + steep_next
                    grad_x = flat[step + 1][k] - flat[step - 1][k]
                    grad_y = wide_pair[k] + wide_next
                    steep_pair[k], wide_pair[k] = steep_next, wide_next
                    aligned = norm_z * grad_z + norm_x * grad_x + norm_y * grad_y
                    aligned = aligned * aligned
                    whole = grad_z * grad_z + grad_x * grad_x + grad_y * grad_y
                    along[plane + k, step] = aligned
                    total[plane + k, step] = whole
                    if step in (1, STEPS):
                        ends[step, k] = (aligned, whole)
            for k in range(GROUP):
                set_edges(along, plane + k, ends[1, k][0], ends[STEPS, k][0])
                set_edges(total, plane + k, ends[1, k][1], ends[STEPS, k][1])

        for outside, edge in ((first_plane == HALO, HALO - 1), (end_plane == HALO + PLANES, HALO + PLANES)):

            @pl.when(outside)
            def _():
                clear(along, edge)
                clear(total, edge)

        margin += 1
        begin = jnp.maximum(margin, first_plane)
        finish = jnp.minimum(DEEP - margin, end_plane)

        @pl.loop(0, (finish - begin) // GROUP)
        def _(group):
            plane = begin + group * GROUP
            c_mid, c_zz, c_xx, c_yy, c_zx, c_zy, c_xy = [coefs[3 + i] for i in range(7)]
            a_cells, t_cells, deep, tilted = {}, {}, {}, {}

            def prepare(step):
                a_cells[step], _ = depth_blur(along, plane, step)
                t_cells[step], _ = depth_blur(total, plane, step)
                deep[step] = [source[plane - 1 + k, step] for k in range(GROUP + 2)]
                steep = depth_slope(deep[step])
                tilted[step] = [c_zx * steep[k] + c_xy * slope[plane + k, step] for k in range(GROUP)]

            prepare(0)
            prepare(1)
            a_pair = [a_cells[0][k] + a_cells[1][k] for k in range(GROUP)]
            t_pair = [t_cells[0][k] + t_cells[1][k] for k in range(GROUP)]
            ends = {}
            for step in range(1, STEPS + 1):
                prepare(step + 1)
                lean = depth_slope([slope[plane - 1 + k, step] for k in range(GROUP + 2)])
                for k in range(GROUP):
                    a_new = a_cells[step][k] + a_cells[step + 1][k]
                    t_new = t_cells[step][k] + t_cells[step + 1][k]
                    aligned = blur_y(a_pair[k] + a_new)
                    whole = blur_y(t_pair[k] + t_new)
                    a_pair[k], t_pair[k] = a_new, t_new
                    weight = aligned / (whole + jnp.float32(TINY * 65536.0))
                    now = deep[step][k + 1]
                    change = (
                        (c_mid * now + c_zz * (deep[step][k] + deep[step][k + 2]))
                        + (c_xx * (deep[step - 1][k + 1] + deep[step + 1][k + 1]) + c_yy * blur[plane + k, step])
                        + ((tilted[step + 1][k] - tilted[step - 1][k]) + c_zy * lean[k])
                    )
                    new = now + weight * change
                    if sweep == ITERS - 1:
                        base = pl.multiple_of((plane + k - HALO) * 128, 128) + (step - 1) * 8
                        final[pl.ds(base, 8), :] = new
                    else:
                        target[plane + k, step] = new
                        if step in (1, STEPS):
                            ends[step, k] = new
            if sweep < ITERS - 1:
                for k in range(GROUP):
                    set_edges(target, plane + k, ends[1, k], ends[STEPS, k])

    low_half = lanes() < 64
    for b in range(4):
        for upper_half in range(2):
            for k in range(8):
                base = k * 16 + b * 2 + upper_half
                first = final[pl.ds(base, 8, stride=128), :]
                second = final[pl.ds(base + 8, 8, stride=128), :]
                tile = upper_half * 16 + k
                out[b, :, tile * 128 : tile * 128 + 128] = jnp.where(low_half, first, pltpu.roll(second, 64, 1))
                tile += 8
                out[b, :, tile * 128 : tile * 128 + 128] = jnp.where(low_half, pltpu.roll(first, 64, 1), second)


def smooth(bounds, coefs, lower, own, upper, interpret=False):
    field = pltpu.VMEM((DEEP + GROUP, STEPS + 2, 8, 128), jnp.float32)
    vmem = pl.BlockSpec(memory_space=pltpu.VMEM)
    return pl.pallas_call(
        smooth_kernel,
        in_specs=[pl.BlockSpec(memory_space=pltpu.SMEM), vmem, vmem, vmem, vmem],
        out_specs=vmem,
        out_shape=jax.ShapeDtypeStruct((4, PLANES, STEPS * 256), jnp.float32),
        scratch_shapes=[field] * 6 + [pltpu.VMEM((PLANES * STEPS * 8, 128), jnp.float32)],
        compiler_params=pltpu.CompilerParams(vmem_limit_bytes=32 << 20),
        name="smooth_image",
        interpret=interpret,
    )(bounds, coefs, lower, own, upper)


def coefficients(classes):
    tilt = 0.2 + 0.1 * (classes % 4).astype(jnp.float32)
    azimuth = 0.3 + math.pi / 2.0 * (classes // 4).astype(jnp.float32)
    norm_z = jnp.cos(tilt)
    norm_x = jnp.sin(tilt) * jnp.cos(azimuth)
    norm_y = jnp.sin(tilt) * jnp.sin(azimuth)
    c_zz = RATE * (1.0 - norm_z * norm_z)
    c_xx = RATE * (1.0 - norm_x * norm_x)
    c_yy = RATE * (1.0 - norm_y * norm_y)
    cross = -0.5 * RATE
    values = jnp.stack(
        [
            norm_z,
            norm_x,
            norm_y,
            -2.0 * (c_zz + c_xx + 2.0 * c_yy),
            c_zz,
            c_xx,
            c_yy,
            cross * norm_z * norm_x,
            cross * norm_z * norm_y,
            cross * norm_x * norm_y,
        ]
    )
    return jnp.broadcast_to(jnp.repeat(values, 2, axis=1)[:, :, None], (10, 8, 128))


def local(partials, aperture, owner_map, dip_class):
    senders = lax.axis_size("shots")
    owned = owner_map.shape[0] // senders
    sent = pack(aperture, owner_map, partials, senders)
    received = lax.all_to_all(sent, "shots", 0, 0, tiled=True)
    image = merge(received).reshape(PLANES, STEPS, 8, 128)
    depth_count = lax.axis_size("depth")
    lower = lax.ppermute(image[PLANES - HALO :], "depth", [(i, i + 1) for i in range(depth_count - 1)])
    upper = lax.ppermute(image[:HALO], "depth", [(i + 1, i) for i in range(depth_count - 1)])
    mine = lax.axis_index("shots") * owned + jnp.arange(owned)
    classes = jnp.sum(jnp.where(owner_map[None, :] == mine[:, None], dip_class[None, :], 0), axis=1)
    place = lax.axis_index("depth")
    bounds = jnp.stack([HALO - place * PLANES, HALO + (depth_count - place) * PLANES]).astype(jnp.int32)
    return smooth(bounds, coefficients(classes), lower, image, upper)


def solution(mesh):
    placed = (P("shots", "depth", None), P("shots"), P(), P())
    return jax.shard_map(
        local, mesh=mesh, in_specs=placed, out_specs=P("shots", "depth", None), check_vma=False
    )
```

```python
import math

import jax
import jax.numpy as jnp
from jax import lax
from jax.experimental import pallas as pl
from jax.experimental.pallas import tpu as pltpu
from jax.sharding import PartitionSpec as P

STEPS = 16
HALO = 6
PLANES = 8
DEEP = PLANES + 2 * HALO
ITERS = 3
RATE = 0.15
TINY = 1e-6
TILES = 32
GROUP = 2


def lanes():
    return lax.broadcasted_iota(jnp.int32, (8, 128), 1)


def rows():
    return lax.broadcasted_iota(jnp.int32, (8, 128), 0)


def pack_kernel(
    aperture_hbm, owner_map_hbm, partials, out, aperture, owner_map, blocks, places, table_sems, in_sems, out_sems, place_sem
):
    slots = partials.shape[0]
    columns = partials.shape[2]
    tables = [
        pltpu.make_async_copy(aperture_hbm, aperture, table_sems.at[0]),
        pltpu.make_async_copy(owner_map_hbm, owner_map, table_sems.at[1]),
    ]
    for copy in tables:
        copy.start()
    fetches = [pltpu.make_async_copy(partials.at[slot], blocks.at[slot], in_sems.at[slot]) for slot in range(slots)]
    for fetch in fetches:
        fetch.start()
    for owner in range(places.shape[0]):
        places[owner] = jnp.full((8, 128), -1.0, jnp.float32)
    for copy in tables:
        copy.wait()

    def block(slot, owner):
        return pltpu.make_async_copy(blocks.at[slot], out.at[owner, :, 0:columns], out_sems.at[slot])

    for slot in range(slots):
        fetches[slot].wait()
        brick = aperture[slot]

        @pl.when(brick >= 0)
        def _():
            row = owner_map[brick]
            owner = row // 4
            block(slot, owner).start()
            places[owner] = jnp.full((8, 128), row % 4, jnp.int32).astype(jnp.float32)

    labels = pltpu.make_async_copy(places, out.at[:, :, columns : columns + 128], place_sem)
    labels.start()
    for slot in range(slots):

        @pl.when(aperture[slot] >= 0)
        def _():
            block(slot, 0).wait()

    labels.wait()


def pack(aperture, owner_map, partials, owners):
    slots, planes, columns = partials.shape
    hbm = pl.BlockSpec(memory_space=pltpu.HBM)
    return pl.pallas_call(
        pack_kernel,
        in_specs=[hbm, hbm, hbm],
        out_specs=hbm,
        out_shape=jax.ShapeDtypeStruct((owners, planes, columns + 128), jnp.float32),
        scratch_shapes=[
            pltpu.SMEM(aperture.shape, jnp.int32),
            pltpu.SMEM(owner_map.shape, jnp.int32),
            pltpu.VMEM(partials.shape, jnp.float32),
            pltpu.VMEM((owners, planes, 128), jnp.float32),
            pltpu.SemaphoreType.DMA((2,)),
            pltpu.SemaphoreType.DMA((slots,)),
            pltpu.SemaphoreType.DMA((slots,)),
            pltpu.SemaphoreType.DMA,
        ],
        compiler_params=pltpu.CompilerParams(vmem_limit_bytes=60 << 20),
        name="pack_blocks",
    )(aperture, owner_map, partials)


def merge_kernel(received, out, places, blocks, sums, place_sem, block_sems):
    senders, planes, columns = blocks.shape
    labels = pltpu.make_async_copy(received.at[:, 0:1, columns : columns + 128], places, place_sem)
    labels.start()
    for brick in range(4):
        for tile in range(TILES):
            sums[brick, tile] = jnp.zeros((8, 128), jnp.float32)
    labels.wait()

    def block(sender):
        return pltpu.make_async_copy(
            received.at[sender, :, 0:columns], blocks.at[sender], block_sems.at[sender]
        )

    for sender in range(senders):

        @pl.when(places[sender, 0, 0] >= 0.0)
        def _():
            block(sender).start()

    for sender in range(senders):
        place = places[sender, 0, 0].astype(jnp.int32)

        @pl.when(place >= 0)
        def _():
            block(sender).wait()
            for tile in range(TILES):
                sums[place, tile] += blocks[sender, :, tile * 128 : tile * 128 + 128]

    low = lanes() < 64
    for b in range(4):
        for upper in range(2):
            for k in range(8):
                even = sums[b, upper * 16 + k]
                odd = sums[b, upper * 16 + 8 + k]
                base = k * 16 + b * 2 + upper
                out[pl.ds(base, 8, stride=128), :] = jnp.where(low, even, pltpu.roll(odd, 64, 1))
                out[pl.ds(base + 8, 8, stride=128), :] = jnp.where(low, pltpu.roll(even, 64, 1), odd)


def merge(received):
    senders, planes, columns = received.shape
    columns -= 128
    return pl.pallas_call(
        merge_kernel,
        in_specs=[pl.BlockSpec(memory_space=pltpu.HBM)],
        out_specs=pl.BlockSpec(memory_space=pltpu.VMEM),
        out_shape=jax.ShapeDtypeStruct((PLANES * STEPS * 8, 128), jnp.float32),
        scratch_shapes=[
            pltpu.SMEM((senders, 1, 128), jnp.float32),
            pltpu.VMEM((senders, planes, columns), jnp.float32),
            pltpu.VMEM((4, TILES, 8, 128), jnp.float32),
            pltpu.SemaphoreType.DMA,
            pltpu.SemaphoreType.DMA((senders,)),
        ],
        compiler_params=pltpu.CompilerParams(vmem_limit_bytes=48 << 20),
        name="merge_blocks",
    )(received)


def left_edge(last):
    turned = pltpu.roll(last, 64, 1)
    below = jnp.where(rows() % 2 == 0, 0.0, pltpu.roll(turned, 1, 0))
    return jnp.where(lanes() < 64, below, turned)


def right_edge(first):
    turned = pltpu.roll(first, 64, 1)
    above = jnp.where(rows() % 2 == 0, pltpu.roll(turned, 7, 0), 0.0)
    return jnp.where(lanes() < 64, turned, above)


def smooth_kernel(bounds, coefs, lower, own, upper, out, image, other, blur, slope, along, total, final):
    column = lanes() % 64
    first_y = column == 0
    last_y = column == 63

    def after(f):
        return jnp.where(last_y, 0.0, pltpu.roll(f, 127, 1))

    def before(f):
        return jnp.where(first_y, 0.0, pltpu.roll(f, 1, 1))

    def blur_y(f):
        return (f + after(f)) + (f + before(f))

    zero = jnp.zeros((8, 128), jnp.float32)

    def clear(field, plane):
        for step in range(1, STEPS + 1):
            field[plane, step] = zero

    for plane in (HALO - 1, HALO + PLANES):
        clear(other, plane)

    def load(source, count, offset):
        @pl.loop(0, count // 2)
        def _(pair):
            for plane in (2 * pair, 2 * pair + 1):
                for step in range(STEPS):
                    image[plane + offset, step + 1] = source[plane, step]

    load(lower, HALO, 0)
    load(own, PLANES, HALO)
    load(upper, HALO, HALO + PLANES)

    first_plane = bounds[0]
    end_plane = bounds[1]

    def along_y(source, plane, step):
        if step == 0:
            cells = left_edge(source[plane, STEPS])
        elif step == STEPS + 1:
            cells = right_edge(source[plane, 1])
        else:
            cells = source[plane, step]
        if step in (0, STEPS + 1):
            source[plane, step] = cells
        up, down = after(cells), before(cells)
        blur[plane, step] = (cells + cells) + (up + down)
        slope[plane, step] = up - down

    def depth_blur(field, plane, step):
        deep = [field[plane - 1 + k, step] for k in range(GROUP + 2)]
        pairs = [deep[k] + deep[k + 1] for k in range(GROUP + 1)]
        return [pairs[k] + pairs[k + 1] for k in range(GROUP)], deep

    def depth_slope(deep):
        return [deep[k + 2] - deep[k] for k in range(GROUP)]

    for sweep in range(ITERS):
        source = image if sweep % 2 == 0 else other
        target = other if sweep % 2 == 0 else image
        margin = 2 * sweep + 1
        start = jnp.maximum(margin, first_plane - 1)
        stop = jnp.minimum(DEEP - margin, end_plane + 1)

        for k in range(GROUP + 1):
            for step in range(STEPS + 2):
                along_y(source, start - 1 + k, step)

        @pl.loop(0, (stop - start) // GROUP)
        def _(group):
            plane = start + group * GROUP
            norm_z, norm_x, norm_y = coefs[0], coefs[1], coefs[2]

            flat, steep, wide = {}, {}, {}

            def prepare(step):
                for k in range(GROUP):
                    along_y(source, plane + GROUP + k, step)
                flat[step], deep = depth_blur(blur, plane, step)
                steep[step] = depth_slope(deep)
                wide[step], _ = depth_blur(slope, plane, step)

            prepare(0)
            prepare(1)
            steep_pair = [steep[0][k] + steep[1][k] for k in range(GROUP)]
            wide_pair = [wide[0][k] + wide[1][k] for k in range(GROUP)]
            for step in range(1, STEPS + 1):
                prepare(step + 1)
                for k in range(GROUP):
                    steep_next = steep[step][k] + steep[step + 1][k]
                    wide_next = wide[step][k] + wide[step + 1][k]
                    grad_z = steep_pair[k] + steep_next
                    grad_x = flat[step + 1][k] - flat[step - 1][k]
                    grad_y = wide_pair[k] + wide_next
                    steep_pair[k], wide_pair[k] = steep_next, wide_next
                    aligned = norm_z * grad_z + norm_x * grad_x + norm_y * grad_y
                    aligned = aligned * aligned
                    whole = grad_z * grad_z + grad_x * grad_x + grad_y * grad_y
                    along[plane + k, step] = aligned
                    total[plane + k, step] = whole

        for outside, edge in ((first_plane == HALO, HALO - 1), (end_plane == HALO + PLANES, HALO + PLANES)):

            @pl.when(outside)
            def _():
                clear(along, edge)
                clear(total, edge)

        margin += 1
        begin = jnp.maximum(margin, first_plane)
        finish = jnp.minimum(DEEP - margin, end_plane)

        @pl.loop(0, (finish - begin) // GROUP)
        def _(group):
            plane = begin + group * GROUP
            c_mid, c_zz, c_xx, c_yy, c_zx, c_zy, c_xy = [coefs[3 + i] for i in range(7)]
            a_cells, t_cells, deep, tilted = {}, {}, {}, {}

            def prepare(step):
                for field, cells in ((along, a_cells), (total, t_cells)):
                    if step == 0:
                        cells[0] = [left_edge(f) for f in depth_blur(field, plane, STEPS)[0]]
                        cells[STEPS + 1] = [right_edge(f) for f in depth_blur(field, plane, 1)[0]]
                    elif step <= STEPS:
                        cells[step], _ = depth_blur(field, plane, step)
                deep[step] = [source[plane - 1 + k, step] for k in range(GROUP + 2)]
                steep = depth_slope(deep[step])
                tilted[step] = [c_zx * steep[k] + c_xy * slope[plane + k, step] for k in range(GROUP)]

            prepare(0)
            prepare(1)
            a_pair = [a_cells[0][k] + a_cells[1][k] for k in range(GROUP)]
            t_pair = [t_cells[0][k] + t_cells[1][k] for k in range(GROUP)]
            for step in range(1, STEPS + 1):
                prepare(step + 1)
                lean = depth_slope([slope[plane - 1 + k, step] for k in range(GROUP + 2)])
                for k in range(GROUP):
                    a_new = a_cells[step][k] + a_cells[step + 1][k]
                    t_new = t_cells[step][k] + t_cells[step + 1][k]
                    aligned = blur_y(a_pair[k] + a_new)
                    whole = blur_y(t_pair[k] + t_new)
                    a_pair[k], t_pair[k] = a_new, t_new
                    weight = aligned / (whole + jnp.float32(TINY * 65536.0))
                    now = deep[step][k + 1]
                    change = (
                        (c_mid * now + c_zz * (deep[step][k] + deep[step][k + 2]))
                        + (c_xx * (deep[step - 1][k + 1] + deep[step + 1][k + 1]) + c_yy * blur[plane + k, step])
                        + ((tilted[step + 1][k] - tilted[step - 1][k]) + c_zy * lean[k])
                    )
                    new = now + weight * change
                    if sweep < ITERS - 1:
                        target[plane + k, step] = new
                    else:
                        base = pl.multiple_of((plane + k - HALO) * 128, 128) + (step - 1) * 8
                        final[pl.ds(base, 8), :] = new

    low_half = lanes() < 64
    for b in range(4):
        for half in range(2):
            for k in range(8):
                base = k * 16 + b * 2 + half
                first = final[pl.ds(base, 8, stride=128), :]
                second = final[pl.ds(base + 8, 8, stride=128), :]
                tile = half * 16 + k
                out[b, :, tile * 128 : tile * 128 + 128] = jnp.where(low_half, first, pltpu.roll(second, 64, 1))
                tile += 8
                out[b, :, tile * 128 : tile * 128 + 128] = jnp.where(low_half, pltpu.roll(first, 64, 1), second)


def smooth(bounds, coefs, lower, own, upper, interpret=False):
    field = pltpu.VMEM((DEEP + GROUP, STEPS + 2, 8, 128), jnp.float32)
    vmem = pl.BlockSpec(memory_space=pltpu.VMEM)
    return pl.pallas_call(
        smooth_kernel,
        in_specs=[pl.BlockSpec(memory_space=pltpu.SMEM), vmem, vmem, vmem, vmem],
        out_specs=vmem,
        out_shape=jax.ShapeDtypeStruct((4, PLANES, STEPS * 256), jnp.float32),
        scratch_shapes=[field] * 6 + [pltpu.VMEM((PLANES * STEPS * 8, 128), jnp.float32)],
        compiler_params=pltpu.CompilerParams(vmem_limit_bytes=32 << 20),
        name="smooth_image",
        interpret=interpret,
    )(bounds, coefs, lower, own, upper)


def coefficients(classes):
    tilt = 0.2 + 0.1 * (classes % 4).astype(jnp.float32)
    azimuth = 0.3 + math.pi / 2.0 * (classes // 4).astype(jnp.float32)
    norm_z = jnp.cos(tilt)
    norm_x = jnp.sin(tilt) * jnp.cos(azimuth)
    norm_y = jnp.sin(tilt) * jnp.sin(azimuth)
    c_zz = RATE * (1.0 - norm_z * norm_z)
    c_xx = RATE * (1.0 - norm_x * norm_x)
    c_yy = RATE * (1.0 - norm_y * norm_y)
    cross = -0.5 * RATE
    values = jnp.stack(
        [
            norm_z,
            norm_x,
            norm_y,
            -2.0 * (c_zz + c_xx + 2.0 * c_yy),
            c_zz,
            c_xx,
            c_yy,
            cross * norm_z * norm_x,
            cross * norm_z * norm_y,
            cross * norm_x * norm_y,
        ]
    )
    return jnp.broadcast_to(jnp.repeat(values, 2, axis=1)[:, :, None], (10, 8, 128))


def local(partials, aperture, owner_map, dip_class):
    senders = lax.axis_size("shots")
    owned = owner_map.shape[0] // senders
    sent = pack(aperture, owner_map, partials, senders)
    received = lax.all_to_all(sent, "shots", 0, 0, tiled=True)
    image = merge(received).reshape(PLANES, STEPS, 8, 128)
    depth_count = lax.axis_size("depth")
    lower = lax.ppermute(image[PLANES - HALO :], "depth", [(i, i + 1) for i in range(depth_count - 1)])
    upper = lax.ppermute(image[:HALO], "depth", [(i + 1, i) for i in range(depth_count - 1)])
    mine = lax.axis_index("shots") * owned + jnp.arange(owned)
    classes = jnp.sum(jnp.where(owner_map[None, :] == mine[:, None], dip_class[None, :], 0), axis=1)
    place = lax.axis_index("depth")
    bounds = jnp.stack([HALO - place * PLANES, HALO + (depth_count - place) * PLANES]).astype(jnp.int32)
    return smooth(bounds, coefficients(classes), lower, image, upper)


def solution(mesh):
    placed = (P("shots", "depth", None), P("shots"), P(), P())
    return jax.shard_map(
        local, mesh=mesh, in_specs=placed, out_specs=P("shots", "depth", None), check_vma=False
    )
```

```python
import math

import jax
import jax.numpy as jnp
from jax import lax
from jax.experimental import pallas as pl
from jax.experimental.pallas import tpu as pltpu
from jax.sharding import PartitionSpec as P

STEPS = 16
HALO = 6
PLANES = 8
DEEP = PLANES + 2 * HALO
ITERS = 3
RATE = 0.15
TINY = 1e-6
TILES = 32
GROUP = 2


def lanes():
    return lax.broadcasted_iota(jnp.int32, (8, 128), 1)


def rows():
    return lax.broadcasted_iota(jnp.int32, (8, 128), 0)


def pack_kernel(
    aperture_hbm, owner_map_hbm, partials, out, aperture, owner_map, blocks, places, table_sems, in_sems, out_sems, place_sem
):
    slots = partials.shape[0]
    columns = partials.shape[2]
    tables = [
        pltpu.make_async_copy(aperture_hbm, aperture, table_sems.at[0]),
        pltpu.make_async_copy(owner_map_hbm, owner_map, table_sems.at[1]),
    ]
    for copy in tables:
        copy.start()
    fetches = [pltpu.make_async_copy(partials.at[slot], blocks.at[slot], in_sems.at[slot]) for slot in range(slots)]
    for fetch in fetches:
        fetch.start()
    for owner in range(places.shape[0]):
        places[owner] = jnp.full((8, 128), -1.0, jnp.float32)
    for copy in tables:
        copy.wait()

    def block(slot, owner):
        return pltpu.make_async_copy(blocks.at[slot], out.at[owner, :, 0:columns], out_sems.at[slot])

    for slot in range(slots):
        fetches[slot].wait()
        brick = aperture[slot]

        @pl.when(brick >= 0)
        def _():
            row = owner_map[brick]
            owner = row // 4
            block(slot, owner).start()
            places[owner] = jnp.full((8, 128), row % 4, jnp.int32).astype(jnp.float32)

    labels = pltpu.make_async_copy(places, out.at[:, :, columns : columns + 128], place_sem)
    labels.start()
    for slot in range(slots):

        @pl.when(aperture[slot] >= 0)
        def _():
            block(slot, 0).wait()

    labels.wait()


def pack(aperture, owner_map, partials, owners):
    slots, planes, columns = partials.shape
    hbm = pl.BlockSpec(memory_space=pltpu.HBM)
    return pl.pallas_call(
        pack_kernel,
        in_specs=[hbm, hbm, hbm],
        out_specs=hbm,
        out_shape=jax.ShapeDtypeStruct((owners, planes, columns + 128), jnp.float32),
        scratch_shapes=[
            pltpu.SMEM(aperture.shape, jnp.int32),
            pltpu.SMEM(owner_map.shape, jnp.int32),
            pltpu.VMEM(partials.shape, jnp.float32),
            pltpu.VMEM((owners, planes, 128), jnp.float32),
            pltpu.SemaphoreType.DMA((2,)),
            pltpu.SemaphoreType.DMA((slots,)),
            pltpu.SemaphoreType.DMA((slots,)),
            pltpu.SemaphoreType.DMA,
        ],
        compiler_params=pltpu.CompilerParams(vmem_limit_bytes=60 << 20),
        name="pack_blocks",
    )(aperture, owner_map, partials)


def merge_kernel(received, out, places, blocks, sums, place_sem, block_sems):
    senders, planes, columns = blocks.shape
    labels = pltpu.make_async_copy(received.at[:, 0:1, columns : columns + 128], places, place_sem)
    labels.start()
    for brick in range(4):
        for tile in range(TILES):
            sums[brick, tile] = jnp.zeros((8, 128), jnp.float32)
    labels.wait()

    def block(sender):
        return pltpu.make_async_copy(
            received.at[sender, :, 0:columns], blocks.at[sender], block_sems.at[sender]
        )

    for sender in range(senders):

        @pl.when(places[sender, 0, 0] >= 0.0)
        def _():
            block(sender).start()

    for sender in range(senders):
        place = places[sender, 0, 0].astype(jnp.int32)

        @pl.when(place >= 0)
        def _():
            block(sender).wait()
            for tile in range(TILES):
                sums[place, tile] += blocks[sender, :, tile * 128 : tile * 128 + 128]

    low = lanes() < 64
    for b in range(4):
        for upper in range(2):
            for k in range(8):
                even = sums[b, upper * 16 + k]
                odd = sums[b, upper * 16 + 8 + k]
                base = k * 16 + b * 2 + upper
                out[pl.ds(base, 8, stride=128), :] = jnp.where(low, even, pltpu.roll(odd, 64, 1))
                out[pl.ds(base + 8, 8, stride=128), :] = jnp.where(low, pltpu.roll(even, 64, 1), odd)


def merge(received):
    senders, planes, columns = received.shape
    columns -= 128
    return pl.pallas_call(
        merge_kernel,
        in_specs=[pl.BlockSpec(memory_space=pltpu.HBM)],
        out_specs=pl.BlockSpec(memory_space=pltpu.VMEM),
        out_shape=jax.ShapeDtypeStruct((PLANES * STEPS * 8, 128), jnp.float32),
        scratch_shapes=[
            pltpu.SMEM((senders, 1, 128), jnp.float32),
            pltpu.VMEM((senders, planes, columns), jnp.float32),
            pltpu.VMEM((4, TILES, 8, 128), jnp.float32),
            pltpu.SemaphoreType.DMA,
            pltpu.SemaphoreType.DMA((senders,)),
        ],
        compiler_params=pltpu.CompilerParams(vmem_limit_bytes=48 << 20),
        name="merge_blocks",
    )(received)


def left_edge(last):
    turned = pltpu.roll(last, 64, 1)
    below = jnp.where(rows() % 2 == 0, 0.0, pltpu.roll(turned, 1, 0))
    return jnp.where(lanes() < 64, below, turned)


def right_edge(first):
    turned = pltpu.roll(first, 64, 1)
    above = jnp.where(rows() % 2 == 0, pltpu.roll(turned, 7, 0), 0.0)
    return jnp.where(lanes() < 64, turned, above)


def smooth_kernel(bounds, coefs, lower, own, upper, out, image, other, blur, slope, along, total, final):
    column = lanes() % 64
    first_y = column == 0
    last_y = column == 63

    def after(f):
        return jnp.where(last_y, 0.0, pltpu.roll(f, 127, 1))

    def before(f):
        return jnp.where(first_y, 0.0, pltpu.roll(f, 1, 1))

    def blur_y(f):
        return (f + after(f)) + (f + before(f))

    zero = jnp.zeros((8, 128), jnp.float32)

    def clear(field, plane):
        for step in range(1, STEPS + 1):
            field[plane, step] = zero

    for plane in (HALO - 1, HALO + PLANES):
        clear(other, plane)

    def load(source, count, offset):
        @pl.loop(0, count // 2)
        def _(pair):
            for plane in (2 * pair, 2 * pair + 1):
                for step in range(STEPS):
                    image[plane + offset, step + 1] = source[plane, step]

    first_plane = bounds[0]
    end_plane = bounds[1]

    def load_or_clear(source, offset, outside):
        @pl.when(jnp.logical_not(outside))
        def _():
            load(source, HALO, offset)

        @pl.when(outside)
        def _():
            for plane in range(HALO):
                clear(image, plane + offset)

    load_or_clear(lower, 0, first_plane == HALO)
    load(own, PLANES, HALO)
    load_or_clear(upper, HALO + PLANES, end_plane == HALO + PLANES)

    def along_y(source, plane, step):
        if step == 0:
            cells = left_edge(source[plane, STEPS])
        elif step == STEPS + 1:
            cells = right_edge(source[plane, 1])
        else:
            cells = source[plane, step]
        if step in (0, STEPS + 1):
            source[plane, step] = cells
        up, down = after(cells), before(cells)
        blur[plane, step] = (cells + cells) + (up + down)
        slope[plane, step] = up - down

    def depth_blur(field, plane, step):
        deep = [field[plane - 1 + k, step] for k in range(GROUP + 2)]
        pairs = [deep[k] + deep[k + 1] for k in range(GROUP + 1)]
        return [pairs[k] + pairs[k + 1] for k in range(GROUP)], deep

    def depth_slope(deep):
        return [deep[k + 2] - deep[k] for k in range(GROUP)]

    for sweep in range(ITERS):
        source = image if sweep % 2 == 0 else other
        target = other if sweep % 2 == 0 else image
        margin = 2 * sweep + 1
        start = jnp.maximum(margin, first_plane - 1)
        stop = jnp.minimum(DEEP - margin, end_plane + 1)

        for k in range(GROUP + 1):
            for step in range(STEPS + 2):
                along_y(source, start - 1 + k, step)

        @pl.loop(0, (stop - start) // GROUP)
        def _(group):
            plane = start + group * GROUP
            norm_z, norm_x, norm_y = coefs[0], coefs[1], coefs[2]

            flat, steep, wide = {}, {}, {}

            def prepare(step):
                for k in range(GROUP):
                    along_y(source, plane + GROUP + k, step)
                flat[step], deep = depth_blur(blur, plane, step)
                steep[step] = depth_slope(deep)
                wide[step], _ = depth_blur(slope, plane, step)

            prepare(0)
            prepare(1)
            steep_pair = [steep[0][k] + steep[1][k] for k in range(GROUP)]
            wide_pair = [wide[0][k] + wide[1][k] for k in range(GROUP)]
            for step in range(1, STEPS + 1):
                prepare(step + 1)
                for k in range(GROUP):
                    steep_next = steep[step][k] + steep[step + 1][k]
                    wide_next = wide[step][k] + wide[step + 1][k]
                    grad_z = steep_pair[k] + steep_next
                    grad_x = flat[step + 1][k] - flat[step - 1][k]
                    grad_y = wide_pair[k] + wide_next
                    steep_pair[k], wide_pair[k] = steep_next, wide_next
                    aligned = norm_z * grad_z + norm_x * grad_x + norm_y * grad_y
                    aligned = aligned * aligned
                    whole = grad_z * grad_z + grad_x * grad_x + grad_y * grad_y
                    along[plane + k, step] = aligned
                    total[plane + k, step] = whole

        for outside, edge in ((first_plane == HALO, HALO - 1), (end_plane == HALO + PLANES, HALO + PLANES)):

            @pl.when(outside)
            def _():
                clear(along, edge)
                clear(total, edge)

        margin += 1
        begin = jnp.maximum(margin, first_plane)
        finish = jnp.minimum(DEEP - margin, end_plane)

        @pl.loop(0, (finish - begin) // GROUP)
        def _(group):
            plane = begin + group * GROUP
            c_mid, c_zz, c_xx, c_yy, c_zx, c_zy, c_xy = [coefs[3 + i] for i in range(7)]
            a_cells, t_cells, deep, tilted = {}, {}, {}, {}

            def prepare(step):
                for field, cells in ((along, a_cells), (total, t_cells)):
                    if step == 0:
                        cells[0] = [left_edge(f) for f in depth_blur(field, plane, STEPS)[0]]
                        cells[STEPS + 1] = [right_edge(f) for f in depth_blur(field, plane, 1)[0]]
                    elif step <= STEPS:
                        cells[step], _ = depth_blur(field, plane, step)
                deep[step] = [source[plane - 1 + k, step] for k in range(GROUP + 2)]
                steep = depth_slope(deep[step])
                tilted[step] = [c_zx * steep[k] + c_xy * slope[plane + k, step] for k in range(GROUP)]

            prepare(0)
            prepare(1)
            a_pair = [a_cells[0][k] + a_cells[1][k] for k in range(GROUP)]
            t_pair = [t_cells[0][k] + t_cells[1][k] for k in range(GROUP)]
            for step in range(1, STEPS + 1):
                prepare(step + 1)
                lean = depth_slope([slope[plane - 1 + k, step] for k in range(GROUP + 2)])
                for k in range(GROUP):
                    a_new = a_cells[step][k] + a_cells[step + 1][k]
                    t_new = t_cells[step][k] + t_cells[step + 1][k]
                    aligned = blur_y(a_pair[k] + a_new)
                    whole = blur_y(t_pair[k] + t_new)
                    a_pair[k], t_pair[k] = a_new, t_new
                    weight = aligned / (whole + jnp.float32(TINY * 65536.0))
                    now = deep[step][k + 1]
                    change = (
                        (c_mid * now + c_zz * (deep[step][k] + deep[step][k + 2]))
                        + (c_xx * (deep[step - 1][k + 1] + deep[step + 1][k + 1]) + c_yy * blur[plane + k, step])
                        + ((tilted[step + 1][k] - tilted[step - 1][k]) + c_zy * lean[k])
                    )
                    new = now + weight * change
                    if sweep < ITERS - 1:
                        target[plane + k, step] = new
                    else:
                        base = pl.multiple_of((plane + k - HALO) * 128, 128) + (step - 1) * 8
                        final[pl.ds(base, 8), :] = new

    low_half = lanes() < 64
    for b in range(4):
        for half in range(2):
            for k in range(8):
                base = k * 16 + b * 2 + half
                first = final[pl.ds(base, 8, stride=128), :]
                second = final[pl.ds(base + 8, 8, stride=128), :]
                tile = half * 16 + k
                out[b, :, tile * 128 : tile * 128 + 128] = jnp.where(low_half, first, pltpu.roll(second, 64, 1))
                tile += 8
                out[b, :, tile * 128 : tile * 128 + 128] = jnp.where(low_half, pltpu.roll(first, 64, 1), second)


def smooth(bounds, coefs, lower, own, upper, interpret=False):
    field = pltpu.VMEM((DEEP + GROUP, STEPS + 2, 8, 128), jnp.float32)
    vmem = pl.BlockSpec(memory_space=pltpu.VMEM)
    return pl.pallas_call(
        smooth_kernel,
        in_specs=[pl.BlockSpec(memory_space=pltpu.SMEM), vmem, vmem, vmem, vmem],
        out_specs=vmem,
        out_shape=jax.ShapeDtypeStruct((4, PLANES, STEPS * 256), jnp.float32),
        scratch_shapes=[field] * 6 + [pltpu.VMEM((PLANES * STEPS * 8, 128), jnp.float32)],
        compiler_params=pltpu.CompilerParams(vmem_limit_bytes=32 << 20),
        name="smooth_image",
        interpret=interpret,
    )(bounds, coefs, lower, own, upper)


def coefficients(classes):
    tilt = 0.2 + 0.1 * (classes % 4).astype(jnp.float32)
    azimuth = 0.3 + math.pi / 2.0 * (classes // 4).astype(jnp.float32)
    norm_z = jnp.cos(tilt)
    norm_x = jnp.sin(tilt) * jnp.cos(azimuth)
    norm_y = jnp.sin(tilt) * jnp.sin(azimuth)
    c_zz = RATE * (1.0 - norm_z * norm_z)
    c_xx = RATE * (1.0 - norm_x * norm_x)
    c_yy = RATE * (1.0 - norm_y * norm_y)
    cross = -0.5 * RATE
    values = jnp.stack(
        [
            norm_z,
            norm_x,
            norm_y,
            -2.0 * (c_zz + c_xx + 2.0 * c_yy),
            c_zz,
            c_xx,
            c_yy,
            cross * norm_z * norm_x,
            cross * norm_z * norm_y,
            cross * norm_x * norm_y,
        ]
    )
    return jnp.broadcast_to(jnp.repeat(values, 2, axis=1)[:, :, None], (10, 8, 128))


def local(partials, aperture, owner_map, dip_class):
    senders = lax.axis_size("shots")
    owned = owner_map.shape[0] // senders
    sent = pack(aperture, owner_map, partials, senders)
    received = lax.all_to_all(sent, "shots", 0, 0, tiled=True)
    image = merge(received).reshape(PLANES, STEPS, 8, 128)
    depth_count = lax.axis_size("depth")
    lower = lax.ppermute(image[PLANES - HALO :], "depth", [(i, (i + 1) % depth_count) for i in range(depth_count)])
    upper = lax.ppermute(image[:HALO], "depth", [((i + 1) % depth_count, i) for i in range(depth_count)])
    mine = lax.axis_index("shots") * owned + jnp.arange(owned)
    classes = jnp.sum(jnp.where(owner_map[None, :] == mine[:, None], dip_class[None, :], 0), axis=1)
    place = lax.axis_index("depth")
    bounds = jnp.stack([HALO - place * PLANES, HALO + (depth_count - place) * PLANES]).astype(jnp.int32)
    return smooth(bounds, coefficients(classes), lower, image, upper)


def solution(mesh):
    placed = (P("shots", "depth", None), P("shots"), P(), P())
    return jax.shard_map(
        local, mesh=mesh, in_specs=placed, out_specs=P("shots", "depth", None), check_vma=False
    )
```

```python
import math

import jax
import jax.numpy as jnp
from jax import lax
from jax.experimental import pallas as pl
from jax.experimental.pallas import tpu as pltpu
from jax.sharding import PartitionSpec as P

STEPS = 16
HALO = 6
PLANES = 8
DEEP = PLANES + 2 * HALO
ITERS = 3
RATE = 0.15
TINY = 1e-6
TILES = 32
GROUP = 2


def lanes():
    return lax.broadcasted_iota(jnp.int32, (8, 128), 1)


def rows():
    return lax.broadcasted_iota(jnp.int32, (8, 128), 0)


def coefficients(classes):
    tilt = 0.2 + 0.1 * (classes & 3).astype(jnp.float32)
    azimuth = 0.3 + math.pi / 2.0 * (classes >> 2).astype(jnp.float32)
    norm_z = jnp.cos(tilt)
    norm_x = jnp.sin(tilt) * jnp.cos(azimuth)
    norm_y = jnp.sin(tilt) * jnp.sin(azimuth)
    c_zz = RATE * (1.0 - norm_z * norm_z)
    c_xx = RATE * (1.0 - norm_x * norm_x)
    c_yy = RATE * (1.0 - norm_y * norm_y)
    cross = -0.5 * RATE
    return [
        norm_z,
        norm_x,
        norm_y,
        -2.0 * (c_zz + c_xx + 2.0 * c_yy),
        c_zz,
        c_xx,
        c_yy,
        cross * norm_z * norm_x,
        cross * norm_z * norm_y,
        cross * norm_x * norm_y,
    ]


def pack_kernel(
    aperture_hbm, owner_map_hbm, dip_class_hbm, partials, out, coefs, aperture, owner_map, dip_class, owned,
    blocks, places, table_sems, in_sems, out_sems, place_sem
):
    slots = partials.shape[0]
    columns = partials.shape[2]
    tables = [
        pltpu.make_async_copy(aperture_hbm, aperture, table_sems.at[0]),
        pltpu.make_async_copy(owner_map_hbm, owner_map, table_sems.at[1]),
        pltpu.make_async_copy(dip_class_hbm, dip_class, table_sems.at[2]),
    ]
    for copy in tables:
        copy.start()
    fetches = [pltpu.make_async_copy(partials.at[slot], blocks.at[slot], in_sems.at[slot]) for slot in range(slots)]
    for fetch in fetches:
        fetch.start()
    for owner in range(places.shape[0]):
        places[owner] = jnp.full((8, 128), -1.0, jnp.float32)
    for copy in tables:
        copy.wait()

    def block(slot, owner):
        return pltpu.make_async_copy(blocks.at[slot], out.at[owner, :, 0:columns], out_sems.at[slot])

    for slot in range(slots):
        fetches[slot].wait()
        brick = aperture[slot]

        @pl.when(brick >= 0)
        def _():
            row = owner_map[brick]
            owner = row // 4
            block(slot, owner).start()
            places[owner] = jnp.full((8, 128), row % 4, jnp.int32).astype(jnp.float32)

    labels = pltpu.make_async_copy(places, out.at[:, :, columns : columns + 128], place_sem)
    labels.start()

    base = lax.axis_index("shots") * 4
    for place in range(4):
        owned[place] = 0

    @pl.loop(0, owner_map.shape[0] // 8)
    def _(group):
        for k in range(8):
            brick = group * 8 + k
            place = owner_map[brick] - base

            @pl.when(jnp.logical_and(place >= 0, place < 4))
            def _():
                owned[place] = dip_class[brick]

    brick_of_row = rows() // 2
    classes = jnp.full((8, 128), owned[3], jnp.int32)
    for place in range(3):
        classes = jnp.where(brick_of_row == place, owned[place], classes)
    for i, value in enumerate(coefficients(classes)):
        coefs[i] = value

    for slot in range(slots):

        @pl.when(aperture[slot] >= 0)
        def _():
            block(slot, 0).wait()

    labels.wait()


def pack(aperture, owner_map, dip_class, partials, owners):
    slots, planes, columns = partials.shape
    hbm = pl.BlockSpec(memory_space=pltpu.HBM)
    return pl.pallas_call(
        pack_kernel,
        in_specs=[hbm] * 4,
        out_specs=[hbm, pl.BlockSpec(memory_space=pltpu.VMEM)],
        out_shape=[
            jax.ShapeDtypeStruct((owners, planes, columns + 128), jnp.float32),
            jax.ShapeDtypeStruct((10, 8, 128), jnp.float32),
        ],
        scratch_shapes=[
            pltpu.SMEM(aperture.shape, jnp.int32),
            pltpu.SMEM(owner_map.shape, jnp.int32),
            pltpu.SMEM(dip_class.shape, jnp.int32),
            pltpu.SMEM((4,), jnp.int32),
            pltpu.VMEM(partials.shape, jnp.float32),
            pltpu.VMEM((owners, planes, 128), jnp.float32),
            pltpu.SemaphoreType.DMA((3,)),
            pltpu.SemaphoreType.DMA((slots,)),
            pltpu.SemaphoreType.DMA((slots,)),
            pltpu.SemaphoreType.DMA,
        ],
        compiler_params=pltpu.CompilerParams(vmem_limit_bytes=60 << 20),
        name="pack_blocks",
    )(aperture, owner_map, dip_class, partials)


def merge_kernel(received, out, places, sums, place_sem):
    senders = received.shape[0]
    columns = received.shape[2] - 128
    labels = pltpu.make_async_copy(received.at[:, 0:1, columns : columns + 128], places, place_sem)
    labels.start()
    for brick in range(4):
        for tile in range(TILES):
            sums[brick, tile] = jnp.zeros((8, 128), jnp.float32)
    labels.wait()

    @pl.loop(0, senders)
    def _(sender):
        place = places[sender, 0, 0].astype(jnp.int32)

        @pl.when(place >= 0)
        def _():
            for tile in range(TILES):
                sums[place, tile] += received[sender, :, tile * 128 : tile * 128 + 128]

    low = lanes() < 64
    for b in range(4):
        for upper in range(2):
            for k in range(8):
                even = sums[b, upper * 16 + k]
                odd = sums[b, upper * 16 + 8 + k]
                base = k * 16 + b * 2 + upper
                out[pl.ds(base, 8, stride=128), :] = jnp.where(low, even, pltpu.roll(odd, 64, 1))
                out[pl.ds(base + 8, 8, stride=128), :] = jnp.where(low, pltpu.roll(even, 64, 1), odd)


def merge(received):
    senders = received.shape[0]
    vmem = pl.BlockSpec(memory_space=pltpu.VMEM)
    return pl.pallas_call(
        merge_kernel,
        in_specs=[vmem],
        out_specs=vmem,
        out_shape=jax.ShapeDtypeStruct((PLANES * STEPS * 8, 128), jnp.float32),
        scratch_shapes=[
            pltpu.SMEM((senders, 1, 128), jnp.float32),
            pltpu.VMEM((4, TILES, 8, 128), jnp.float32),
            pltpu.SemaphoreType.DMA,
        ],
        compiler_params=pltpu.CompilerParams(vmem_limit_bytes=32 << 20),
        name="merge_blocks",
    )(received)


def left_edge(last):
    turned = pltpu.roll(last, 64, 1)
    below = jnp.where(rows() % 2 == 0, 0.0, pltpu.roll(turned, 1, 0))
    return jnp.where(lanes() < 64, below, turned)


def right_edge(first):
    turned = pltpu.roll(first, 64, 1)
    above = jnp.where(rows() % 2 == 0, pltpu.roll(turned, 7, 0), 0.0)
    return jnp.where(lanes() < 64, turned, above)


def smooth_kernel(coefs, lower, own, upper, out, image, other, blur, slope, along, total, final):
    column = lanes() % 64
    first_y = column == 0
    last_y = column == 63

    def after(f):
        return jnp.where(last_y, 0.0, pltpu.roll(f, 127, 1))

    def before(f):
        return jnp.where(first_y, 0.0, pltpu.roll(f, 1, 1))

    def blur_y(f):
        return (f + after(f)) + (f + before(f))

    zero = jnp.zeros((8, 128), jnp.float32)

    def clear(field, plane):
        for step in range(1, STEPS + 1):
            field[plane, step] = zero

    for plane in (HALO - 1, HALO + PLANES):
        clear(other, plane)

    def load(source, count, offset):
        @pl.loop(0, count // 2)
        def _(pair):
            for plane in (2 * pair, 2 * pair + 1):
                for step in range(STEPS):
                    image[plane + offset, step + 1] = source[plane, step]

    place = lax.axis_index("depth")
    first_plane = HALO - place * PLANES
    end_plane = HALO + (lax.axis_size("depth") - place) * PLANES

    def load_or_clear(source, offset, outside):
        @pl.when(jnp.logical_not(outside))
        def _():
            load(source, HALO, offset)

        @pl.when(outside)
        def _():
            for plane in range(HALO):
                clear(image, plane + offset)

    load_or_clear(lower, 0, first_plane == HALO)
    load(own, PLANES, HALO)
    load_or_clear(upper, HALO + PLANES, end_plane == HALO + PLANES)

    def along_y(source, plane, step):
        if step == 0:
            cells = left_edge(source[plane, STEPS])
        elif step == STEPS + 1:
            cells = right_edge(source[plane, 1])
        else:
            cells = source[plane, step]
        if step in (0, STEPS + 1):
            source[plane, step] = cells
        up, down = after(cells), before(cells)
        blur[plane, step] = (cells + cells) + (up + down)
        slope[plane, step] = up - down

    def depth_blur(field, plane, step):
        deep = [field[plane - 1 + k, step] for k in range(GROUP + 2)]
        pairs = [deep[k] + deep[k + 1] for k in range(GROUP + 1)]
        return [pairs[k] + pairs[k + 1] for k in range(GROUP)], deep

    def depth_slope(deep):
        return [deep[k + 2] - deep[k] for k in range(GROUP)]

    for sweep in range(ITERS):
        source = image if sweep % 2 == 0 else other
        target = other if sweep % 2 == 0 else image
        margin = 2 * sweep + 1
        start = jnp.maximum(margin, first_plane - 1)
        stop = jnp.minimum(DEEP - margin, end_plane + 1)

        for k in range(GROUP + 1):
            for step in range(STEPS + 2):
                along_y(source, start - 1 + k, step)

        @pl.loop(0, (stop - start) // GROUP)
        def _(group):
            plane = start + group * GROUP
            norm_z, norm_x, norm_y = coefs[0], coefs[1], coefs[2]

            flat, steep, wide = {}, {}, {}

            def prepare(step):
                for k in range(GROUP):
                    along_y(source, plane + GROUP + k, step)
                flat[step], deep = depth_blur(blur, plane, step)
                steep[step] = depth_slope(deep)
                wide[step], _ = depth_blur(slope, plane, step)

            prepare(0)
            prepare(1)
            steep_pair = [steep[0][k] + steep[1][k] for k in range(GROUP)]
            wide_pair = [wide[0][k] + wide[1][k] for k in range(GROUP)]
            for step in range(1, STEPS + 1):
                prepare(step + 1)
                for k in range(GROUP):
                    steep_next = steep[step][k] + steep[step + 1][k]
                    wide_next = wide[step][k] + wide[step + 1][k]
                    grad_z = steep_pair[k] + steep_next
                    grad_x = flat[step + 1][k] - flat[step - 1][k]
                    grad_y = wide_pair[k] + wide_next
                    steep_pair[k], wide_pair[k] = steep_next, wide_next
                    aligned = norm_z * grad_z + norm_x * grad_x + norm_y * grad_y
                    aligned = aligned * aligned
                    whole = grad_z * grad_z + grad_x * grad_x + grad_y * grad_y
                    along[plane + k, step] = aligned
                    total[plane + k, step] = whole

        for outside, edge in ((first_plane == HALO, HALO - 1), (end_plane == HALO + PLANES, HALO + PLANES)):

            @pl.when(outside)
            def _():
                clear(along, edge)
                clear(total, edge)

        margin += 1
        begin = jnp.maximum(margin, first_plane)
        finish = jnp.minimum(DEEP - margin, end_plane)

        @pl.loop(0, (finish - begin) // GROUP)
        def _(group):
            plane = begin + group * GROUP
            c_mid, c_zz, c_xx, c_yy, c_zx, c_zy, c_xy = [coefs[3 + i] for i in range(7)]
            a_cells, t_cells, deep, tilted = {}, {}, {}, {}

            def prepare(step):
                for field, cells in ((along, a_cells), (total, t_cells)):
                    if step == 0:
                        cells[0] = [left_edge(f) for f in depth_blur(field, plane, STEPS)[0]]
                        cells[STEPS + 1] = [right_edge(f) for f in depth_blur(field, plane, 1)[0]]
                    elif step <= STEPS:
                        cells[step], _ = depth_blur(field, plane, step)
                deep[step] = [source[plane - 1 + k, step] for k in range(GROUP + 2)]
                steep = depth_slope(deep[step])
                tilted[step] = [c_zx * steep[k] + c_xy * slope[plane + k, step] for k in range(GROUP)]

            prepare(0)
            prepare(1)
            a_pair = [a_cells[0][k] + a_cells[1][k] for k in range(GROUP)]
            t_pair = [t_cells[0][k] + t_cells[1][k] for k in range(GROUP)]
            for step in range(1, STEPS + 1):
                prepare(step + 1)
                lean = depth_slope([slope[plane - 1 + k, step] for k in range(GROUP + 2)])
                for k in range(GROUP):
                    a_new = a_cells[step][k] + a_cells[step + 1][k]
                    t_new = t_cells[step][k] + t_cells[step + 1][k]
                    aligned = blur_y(a_pair[k] + a_new)
                    whole = blur_y(t_pair[k] + t_new)
                    a_pair[k], t_pair[k] = a_new, t_new
                    weight = aligned / (whole + jnp.float32(TINY * 65536.0))
                    now = deep[step][k + 1]
                    change = (
                        (c_mid * now + c_zz * (deep[step][k] + deep[step][k + 2]))
                        + (c_xx * (deep[step - 1][k + 1] + deep[step + 1][k + 1]) + c_yy * blur[plane + k, step])
                        + ((tilted[step + 1][k] - tilted[step - 1][k]) + c_zy * lean[k])
                    )
                    new = now + weight * change
                    if sweep < ITERS - 1:
                        target[plane + k, step] = new
                    else:
                        base = pl.multiple_of((plane + k - HALO) * 128, 128) + (step - 1) * 8
                        final[pl.ds(base, 8), :] = new

    low_half = lanes() < 64
    for b in range(4):
        for half in range(2):
            for k in range(8):
                base = k * 16 + b * 2 + half
                first = final[pl.ds(base, 8, stride=128), :]
                second = final[pl.ds(base + 8, 8, stride=128), :]
                tile = half * 16 + k
                out[b, :, tile * 128 : tile * 128 + 128] = jnp.where(low_half, first, pltpu.roll(second, 64, 1))
                tile += 8
                out[b, :, tile * 128 : tile * 128 + 128] = jnp.where(low_half, pltpu.roll(first, 64, 1), second)


def smooth(coefs, lower, own, upper, interpret=False):
    field = pltpu.VMEM((DEEP + GROUP, STEPS + 2, 8, 128), jnp.float32)
    vmem = pl.BlockSpec(memory_space=pltpu.VMEM)
    return pl.pallas_call(
        smooth_kernel,
        in_specs=[vmem] * 4,
        out_specs=vmem,
        out_shape=jax.ShapeDtypeStruct((4, PLANES, STEPS * 256), jnp.float32),
        scratch_shapes=[field] * 6 + [pltpu.VMEM((PLANES * STEPS * 8, 128), jnp.float32)],
        compiler_params=pltpu.CompilerParams(vmem_limit_bytes=32 << 20),
        name="smooth_image",
        interpret=interpret,
    )(coefs, lower, own, upper)


def local(partials, aperture, owner_map, dip_class):
    sent, coefs = pack(aperture, owner_map, dip_class, partials, lax.axis_size("shots"))
    received = lax.all_to_all(sent, "shots", 0, 0, tiled=True)
    image = merge(received).reshape(PLANES, STEPS, 8, 128)
    depth_count = lax.axis_size("depth")
    lower = lax.ppermute(image[PLANES - HALO :], "depth", [(i, (i + 1) % depth_count) for i in range(depth_count)])
    upper = lax.ppermute(image[:HALO], "depth", [((i + 1) % depth_count, i) for i in range(depth_count)])
    return smooth(coefs, lower, image, upper)


def solution(mesh):
    placed = (P("shots", "depth", None), P("shots"), P(), P())
    return jax.shard_map(
        local, mesh=mesh, in_specs=placed, out_specs=P("shots", "depth", None), check_vma=False
    )
```

```python
import math

import jax
import jax.numpy as jnp
from jax import lax
from jax.experimental import pallas as pl
from jax.experimental.pallas import tpu as pltpu
from jax.sharding import PartitionSpec as P

STEPS = 16
HALO = 6
PLANES = 8
DEEP = PLANES + 2 * HALO
ITERS = 3
RATE = 0.15
TINY = 1e-6
TILES = 32
GROUP = 2
NEAR = 2
KEPT = (HALO - 1, HALO, HALO + PLANES - 1, HALO + PLANES)


def lanes():
    return lax.broadcasted_iota(jnp.int32, (8, 128), 1)


def rows():
    return lax.broadcasted_iota(jnp.int32, (8, 128), 0)


def coefficients(classes):
    tilt = 0.2 + 0.1 * (classes & 3).astype(jnp.float32)
    azimuth = 0.3 + math.pi / 2.0 * (classes >> 2).astype(jnp.float32)
    norm_z = jnp.cos(tilt)
    norm_x = jnp.sin(tilt) * jnp.cos(azimuth)
    norm_y = jnp.sin(tilt) * jnp.sin(azimuth)
    c_zz = RATE * (1.0 - norm_z * norm_z)
    c_xx = RATE * (1.0 - norm_x * norm_x)
    c_yy = RATE * (1.0 - norm_y * norm_y)
    cross = -0.5 * RATE
    return [
        norm_z,
        norm_x,
        norm_y,
        -2.0 * (c_zz + c_xx + 2.0 * c_yy),
        c_zz,
        c_xx,
        c_yy,
        cross * norm_z * norm_x,
        cross * norm_z * norm_y,
        cross * norm_x * norm_y,
    ]


def pack_kernel(
    aperture_hbm, owner_map_hbm, dip_class_hbm, partials, out, coefs, aperture, owner_map, dip_class, owned,
    blocks, places, table_sems, in_sems, out_sems, place_sem
):
    slots = partials.shape[0]
    columns = partials.shape[2]
    tables = [
        pltpu.make_async_copy(aperture_hbm, aperture, table_sems.at[0]),
        pltpu.make_async_copy(owner_map_hbm, owner_map, table_sems.at[1]),
        pltpu.make_async_copy(dip_class_hbm, dip_class, table_sems.at[2]),
    ]
    for copy in tables:
        copy.start()
    fetches = [pltpu.make_async_copy(partials.at[slot], blocks.at[slot], in_sems.at[slot]) for slot in range(slots)]
    for fetch in fetches:
        fetch.start()
    for owner in range(places.shape[0]):
        places[owner] = jnp.full((8, 128), -1.0, jnp.float32)
    for copy in tables:
        copy.wait()

    def block(slot, owner):
        return pltpu.make_async_copy(blocks.at[slot], out.at[owner, :, 0:columns], out_sems.at[slot])

    for slot in range(slots):
        fetches[slot].wait()
        brick = aperture[slot]

        @pl.when(brick >= 0)
        def _():
            row = owner_map[brick]
            owner = row // 4
            block(slot, owner).start()
            places[owner] = jnp.full((8, 128), row % 4, jnp.int32).astype(jnp.float32)

    labels = pltpu.make_async_copy(places, out.at[:, :, columns : columns + 128], place_sem)
    labels.start()

    base = lax.axis_index("shots") * 4
    for place in range(4):
        owned[place] = 0

    @pl.loop(0, owner_map.shape[0] // 8)
    def _(group):
        for k in range(8):
            brick = group * 8 + k
            place = owner_map[brick] - base

            @pl.when(jnp.logical_and(place >= 0, place < 4))
            def _():
                owned[place] = dip_class[brick]

    brick_of_row = rows() // 2
    classes = jnp.full((8, 128), owned[3], jnp.int32)
    for place in range(3):
        classes = jnp.where(brick_of_row == place, owned[place], classes)
    for i, value in enumerate(coefficients(classes)):
        coefs[i] = value

    for slot in range(slots):

        @pl.when(aperture[slot] >= 0)
        def _():
            block(slot, 0).wait()

    labels.wait()


def pack(aperture, owner_map, dip_class, partials, owners):
    slots, planes, columns = partials.shape
    hbm = pl.BlockSpec(memory_space=pltpu.HBM)
    return pl.pallas_call(
        pack_kernel,
        in_specs=[hbm] * 4,
        out_specs=[hbm, pl.BlockSpec(memory_space=pltpu.VMEM)],
        out_shape=[
            jax.ShapeDtypeStruct((owners, planes, columns + 128), jnp.float32),
            jax.ShapeDtypeStruct((10, 8, 128), jnp.float32),
        ],
        scratch_shapes=[
            pltpu.SMEM(aperture.shape, jnp.int32),
            pltpu.SMEM(owner_map.shape, jnp.int32),
            pltpu.SMEM(dip_class.shape, jnp.int32),
            pltpu.SMEM((4,), jnp.int32),
            pltpu.VMEM(partials.shape, jnp.float32),
            pltpu.VMEM((owners, planes, 128), jnp.float32),
            pltpu.SemaphoreType.DMA((3,)),
            pltpu.SemaphoreType.DMA((slots,)),
            pltpu.SemaphoreType.DMA((slots,)),
            pltpu.SemaphoreType.DMA,
        ],
        compiler_params=pltpu.CompilerParams(vmem_limit_bytes=60 << 20),
        name="pack_blocks",
    )(aperture, owner_map, dip_class, partials)


def merge_kernel(received, out, places, sums, place_sem):
    senders = received.shape[0]
    columns = received.shape[2] - 128
    labels = pltpu.make_async_copy(received.at[:, 0:1, columns : columns + 128], places, place_sem)
    labels.start()
    for brick in range(4):
        for tile in range(TILES):
            sums[brick, tile] = jnp.zeros((8, 128), jnp.float32)
    labels.wait()

    @pl.loop(0, senders)
    def _(sender):
        place = places[sender, 0, 0].astype(jnp.int32)

        @pl.when(place >= 0)
        def _():
            for tile in range(TILES):
                sums[place, tile] += received[sender, :, tile * 128 : tile * 128 + 128]

    low = lanes() < 64
    for b in range(4):
        for upper in range(2):
            for k in range(8):
                even = sums[b, upper * 16 + k]
                odd = sums[b, upper * 16 + 8 + k]
                base = k * 16 + b * 2 + upper
                out[pl.ds(base, 8, stride=128), :] = jnp.where(low, even, pltpu.roll(odd, 64, 1))
                out[pl.ds(base + 8, 8, stride=128), :] = jnp.where(low, pltpu.roll(even, 64, 1), odd)


def merge(received):
    senders = received.shape[0]
    vmem = pl.BlockSpec(memory_space=pltpu.VMEM)
    return pl.pallas_call(
        merge_kernel,
        in_specs=[vmem],
        out_specs=vmem,
        out_shape=jax.ShapeDtypeStruct((PLANES * STEPS * 8, 128), jnp.float32),
        scratch_shapes=[
            pltpu.SMEM((senders, 1, 128), jnp.float32),
            pltpu.VMEM((4, TILES, 8, 128), jnp.float32),
            pltpu.SemaphoreType.DMA,
        ],
        compiler_params=pltpu.CompilerParams(vmem_limit_bytes=32 << 20),
        name="merge_blocks",
    )(received)


def left_edge(last):
    turned = pltpu.roll(last, 64, 1)
    below = jnp.where(rows() % 2 == 0, 0.0, pltpu.roll(turned, 1, 0))
    return jnp.where(lanes() < 64, below, turned)


def right_edge(first):
    turned = pltpu.roll(first, 64, 1)
    above = jnp.where(rows() % 2 == 0, pltpu.roll(turned, 7, 0), 0.0)
    return jnp.where(lanes() < 64, turned, above)


def depth_range():
    place = lax.axis_index("depth")
    return HALO - place * PLANES, HALO + (lax.axis_size("depth") - place) * PLANES


def clear(field, plane):
    for step in range(1, STEPS + 1):
        field[plane, step] = jnp.zeros((8, 128), jnp.float32)


def load(field, offset, source, first, count):
    @pl.loop(0, count // 2)
    def _(pair):
        for plane in (2 * pair, 2 * pair + 1):
            for step in range(STEPS):
                field[plane + offset, step + 1] = source[plane + first, step]


def load_or_clear(outside, field, offset, source):
    @pl.when(jnp.logical_not(outside))
    def _():
        load(field, offset, source, 0, source.shape[0])

    @pl.when(outside)
    def _():
        for plane in range(source.shape[0]):
            clear(field, plane + offset)


def sweep_parts(coefs, blur, slope, along, total):
    column = lanes() % 64
    first_y = column == 0
    last_y = column == 63

    def after(f):
        return jnp.where(last_y, 0.0, pltpu.roll(f, 127, 1))

    def before(f):
        return jnp.where(first_y, 0.0, pltpu.roll(f, 1, 1))

    def blur_y(f):
        return (f + after(f)) + (f + before(f))

    def along_y(source, plane, step):
        if step == 0:
            cells = left_edge(source[plane, STEPS])
        elif step == STEPS + 1:
            cells = right_edge(source[plane, 1])
        else:
            cells = source[plane, step]
        if step in (0, STEPS + 1):
            source[plane, step] = cells
        up, down = after(cells), before(cells)
        blur[plane, step] = (cells + cells) + (up + down)
        slope[plane, step] = up - down

    def depth_blur(field, plane, step):
        deep = [field[plane - 1 + k, step] for k in range(GROUP + 2)]
        pairs = [deep[k] + deep[k + 1] for k in range(GROUP + 1)]
        return [pairs[k] + pairs[k + 1] for k in range(GROUP)], deep

    def depth_slope(deep):
        return [deep[k + 2] - deep[k] for k in range(GROUP)]

    def y_pass(source, plane):
        for step in range(STEPS + 2):
            along_y(source, plane, step)

    def products(source, start, stop):
        for k in range(GROUP + 1):
            y_pass(source, start - 1 + k)

        @pl.loop(0, (stop - start) // GROUP)
        def _(group):
            plane = start + group * GROUP
            norm_z, norm_x, norm_y = coefs[0], coefs[1], coefs[2]

            flat, steep, wide = {}, {}, {}

            def prepare(step):
                for k in range(GROUP):
                    along_y(source, plane + GROUP + k, step)
                flat[step], deep = depth_blur(blur, plane, step)
                steep[step] = depth_slope(deep)
                wide[step], _ = depth_blur(slope, plane, step)

            prepare(0)
            prepare(1)
            steep_pair = [steep[0][k] + steep[1][k] for k in range(GROUP)]
            wide_pair = [wide[0][k] + wide[1][k] for k in range(GROUP)]
            for step in range(1, STEPS + 1):
                prepare(step + 1)
                for k in range(GROUP):
                    steep_next = steep[step][k] + steep[step + 1][k]
                    wide_next = wide[step][k] + wide[step + 1][k]
                    grad_z = steep_pair[k] + steep_next
                    grad_x = flat[step + 1][k] - flat[step - 1][k]
                    grad_y = wide_pair[k] + wide_next
                    steep_pair[k], wide_pair[k] = steep_next, wide_next
                    aligned = norm_z * grad_z + norm_x * grad_x + norm_y * grad_y
                    aligned = aligned * aligned
                    whole = grad_z * grad_z + grad_x * grad_x + grad_y * grad_y
                    along[plane + k, step] = aligned
                    total[plane + k, step] = whole

    def update(source, begin, finish, store):
        @pl.loop(0, (finish - begin) // GROUP)
        def _(group):
            plane = begin + group * GROUP
            c_mid, c_zz, c_xx, c_yy, c_zx, c_zy, c_xy = [coefs[3 + i] for i in range(7)]
            a_cells, t_cells, deep, tilted = {}, {}, {}, {}

            def prepare(step):
                for field, cells in ((along, a_cells), (total, t_cells)):
                    if step == 0:
                        cells[0] = [left_edge(f) for f in depth_blur(field, plane, STEPS)[0]]
                        cells[STEPS + 1] = [right_edge(f) for f in depth_blur(field, plane, 1)[0]]
                    elif step <= STEPS:
                        cells[step], _ = depth_blur(field, plane, step)
                deep[step] = [source[plane - 1 + k, step] for k in range(GROUP + 2)]
                steep = depth_slope(deep[step])
                tilted[step] = [c_zx * steep[k] + c_xy * slope[plane + k, step] for k in range(GROUP)]

            prepare(0)
            prepare(1)
            a_pair = [a_cells[0][k] + a_cells[1][k] for k in range(GROUP)]
            t_pair = [t_cells[0][k] + t_cells[1][k] for k in range(GROUP)]
            for step in range(1, STEPS + 1):
                prepare(step + 1)
                lean = depth_slope([slope[plane - 1 + k, step] for k in range(GROUP + 2)])
                for k in range(GROUP):
                    a_new = a_cells[step][k] + a_cells[step + 1][k]
                    t_new = t_cells[step][k] + t_cells[step + 1][k]
                    aligned = blur_y(a_pair[k] + a_new)
                    whole = blur_y(t_pair[k] + t_new)
                    a_pair[k], t_pair[k] = a_new, t_new
                    weight = aligned / (whole + jnp.float32(TINY * 65536.0))
                    now = deep[step][k + 1]
                    change = (
                        (c_mid * now + c_zz * (deep[step][k] + deep[step][k + 2]))
                        + (c_xx * (deep[step - 1][k + 1] + deep[step + 1][k + 1]) + c_yy * blur[plane + k, step])
                        + ((tilted[step + 1][k] - tilted[step - 1][k]) + c_zy * lean[k])
                    )
                    new = now + weight * change
                    store(plane + k, step, new)

    return y_pass, products, update


def first_kernel(coefs, lower, own, upper, out, tensors, image, blur, slope, along, total):
    first_plane, end_plane = depth_range()
    low_end, high_end = first_plane == HALO, end_plane == HALO + PLANES
    _, products, update = sweep_parts(coefs, blur, slope, along, total)
    load_or_clear(low_end, image, HALO - NEAR, lower)
    load(image, HALO, own, 0, PLANES)
    load_or_clear(high_end, image, HALO + PLANES, upper)
    products(image, HALO - 1, HALO + PLANES + 1)
    clear_outside(low_end, high_end, along, total)

    def store(plane, step, new):
        out[plane - HALO, step - 1] = new

    update(image, HALO, HALO + PLANES, store)
    for which, field in enumerate((along, total)):
        for k, plane in enumerate(KEPT):
            for step in range(STEPS):
                tensors[which, k, step] = field[plane, step + 1]


def clear_outside(low_end, high_end, along, total):
    for outside, edge in ((low_end, HALO - 1), (high_end, HALO + PLANES)):

        @pl.when(outside)
        def _():
            clear(along, edge)
            clear(total, edge)


def rest_kernel(
    coefs, far_lower, near_lower, own, near_upper, far_upper, swept, tensors, out, image, other, blur, slope, along, total, final
):
    first_plane, end_plane = depth_range()
    low_end, high_end = first_plane == HALO, end_plane == HALO + PLANES
    y_pass, products, update = sweep_parts(coefs, blur, slope, along, total)
    load(other, HALO, swept, 0, PLANES)
    clear(other, HALO - 1)
    clear(other, HALO + PLANES)
    for which, field in enumerate((along, total)):
        for k, plane in enumerate(KEPT):
            for step in range(STEPS):
                field[plane, step + 1] = tensors[which, k, step]

    def keep(plane, step, new):
        other[plane, step] = new

    @pl.when(jnp.logical_not(low_end))
    def _():
        load(image, 0, far_lower, 0, HALO - NEAR)
        load(image, HALO - NEAR, near_lower, 0, NEAR)
        load(image, HALO, own, 0, NEAR)
        products(image, 1, HALO - 1)
        update(image, 2, HALO, keep)

    @pl.when(jnp.logical_not(high_end))
    def _():
        top = HALO + PLANES
        load(image, top - NEAR, own, PLANES - NEAR, NEAR)
        load(image, top, near_upper, 0, NEAR)
        load(image, top + NEAR, far_upper, 0, HALO - NEAR)
        y_pass(image, top - 1)
        products(image, top + 1, DEEP - 1)
        update(image, top, DEEP - 2, keep)

    @pl.when(low_end)
    def _():
        clear(image, HALO - 1)

    @pl.when(high_end)
    def _():
        clear(image, HALO + PLANES)

    for sweep in range(1, ITERS):
        source, target = (other, image) if sweep % 2 == 1 else (image, other)
        margin = 2 * sweep + 1
        products(source, jnp.maximum(margin, first_plane - 1), jnp.minimum(DEEP - margin, end_plane + 1))
        clear_outside(low_end, high_end, along, total)

        def store(plane, step, new):
            if sweep < ITERS - 1:
                target[plane, step] = new
            else:
                base = pl.multiple_of((plane - HALO) * 128, 128) + (step - 1) * 8
                final[pl.ds(base, 8), :] = new

        margin += 1
        update(source, jnp.maximum(margin, first_plane), jnp.minimum(DEEP - margin, end_plane), store)

    low_half = lanes() < 64
    for b in range(4):
        for half in range(2):
            for k in range(8):
                base = k * 16 + b * 2 + half
                first = final[pl.ds(base, 8, stride=128), :]
                second = final[pl.ds(base + 8, 8, stride=128), :]
                tile = half * 16 + k
                out[b, :, tile * 128 : tile * 128 + 128] = jnp.where(low_half, first, pltpu.roll(second, 64, 1))
                tile += 8
                out[b, :, tile * 128 : tile * 128 + 128] = jnp.where(low_half, pltpu.roll(first, 64, 1), second)


def smooth(coefs, image, depth_ring, interpret=False):
    field = pltpu.VMEM((DEEP + GROUP, STEPS + 2, 8, 128), jnp.float32)
    vmem = pl.BlockSpec(memory_space=pltpu.VMEM)
    near_lower = depth_ring(image[PLANES - NEAR :], 1)
    near_upper = depth_ring(image[:NEAR], -1)
    middle = image[NEAR : PLANES - NEAR]
    far_lower = depth_ring(middle, 1)
    far_upper = depth_ring(middle, -1)
    params = pltpu.CompilerParams(vmem_limit_bytes=32 << 20)
    swept, tensors = pl.pallas_call(
        first_kernel,
        in_specs=[vmem] * 4,
        out_specs=[vmem] * 2,
        out_shape=[
            jax.ShapeDtypeStruct((PLANES, STEPS, 8, 128), jnp.float32),
            jax.ShapeDtypeStruct((2, len(KEPT), STEPS, 8, 128), jnp.float32),
        ],
        scratch_shapes=[field] * 5,
        compiler_params=params,
        cost_estimate=pl.CostEstimate(flops=20_000_000, bytes_accessed=12_000_000, transcendentals=0),
        name="smooth_own",
        interpret=interpret,
    )(coefs, near_lower, image, near_upper)
    return pl.pallas_call(
        rest_kernel,
        in_specs=[vmem] * 8,
        out_specs=vmem,
        out_shape=jax.ShapeDtypeStruct((4, PLANES, STEPS * 256), jnp.float32),
        scratch_shapes=[field] * 6 + [pltpu.VMEM((PLANES * STEPS * 8, 128), jnp.float32)],
        compiler_params=params,
        name="smooth_image",
        interpret=interpret,
    )(coefs, far_lower, near_lower, image, near_upper, far_upper, swept, tensors)


def local(partials, aperture, owner_map, dip_class):
    sent, coefs = pack(aperture, owner_map, dip_class, partials, lax.axis_size("shots"))
    received = lax.all_to_all(sent, "shots", 0, 0, tiled=True)
    image = merge(received).reshape(PLANES, STEPS, 8, 128)
    count = lax.axis_size("depth")

    def depth_ring(planes, way):
        return lax.ppermute(planes, "depth", [(i, (i + way) % count) for i in range(count)])

    return smooth(coefs, image, depth_ring)


def solution(mesh):
    placed = (P("shots", "depth", None), P("shots"), P(), P())
    return jax.shard_map(
        local, mesh=mesh, in_specs=placed, out_specs=P("shots", "depth", None), check_vma=False
    )
```

```python
import math

import jax
import jax.numpy as jnp
from jax import lax
from jax.experimental import pallas as pl
from jax.experimental.pallas import tpu as pltpu
from jax.sharding import PartitionSpec as P

STEPS = 16
HALO = 6
PLANES = 8
DEEP = PLANES + 2 * HALO
ITERS = 3
RATE = 0.15
TINY = 1e-6
TILES = 32
GROUP = 2


def lanes():
    return lax.broadcasted_iota(jnp.int32, (8, 128), 1)


def rows():
    return lax.broadcasted_iota(jnp.int32, (8, 128), 0)


def coefficients(classes):
    tilt = 0.2 + 0.1 * (classes & 3).astype(jnp.float32)
    azimuth = 0.3 + math.pi / 2.0 * (classes >> 2).astype(jnp.float32)
    norm_z = jnp.cos(tilt)
    norm_x = jnp.sin(tilt) * jnp.cos(azimuth)
    norm_y = jnp.sin(tilt) * jnp.sin(azimuth)
    c_zz = RATE * (1.0 - norm_z * norm_z)
    c_xx = RATE * (1.0 - norm_x * norm_x)
    c_yy = RATE * (1.0 - norm_y * norm_y)
    cross = -0.5 * RATE
    return [
        norm_z,
        norm_x,
        norm_y,
        -2.0 * (c_zz + c_xx + 2.0 * c_yy),
        c_zz,
        c_xx,
        c_yy,
        cross * norm_z * norm_x,
        cross * norm_z * norm_y,
        cross * norm_x * norm_y,
    ]


def pack_kernel(
    aperture_hbm, owner_map_hbm, dip_class_hbm, partials, out, coefs, aperture, owner_map, dip_class, owned,
    blocks, places, table_sems, in_sems, out_sems, place_sem
):
    slots = partials.shape[0]
    columns = partials.shape[2]
    tables = [
        pltpu.make_async_copy(aperture_hbm, aperture, table_sems.at[0]),
        pltpu.make_async_copy(owner_map_hbm, owner_map, table_sems.at[1]),
        pltpu.make_async_copy(dip_class_hbm, dip_class, table_sems.at[2]),
    ]
    for copy in tables:
        copy.start()
    fetches = [pltpu.make_async_copy(partials.at[slot], blocks.at[slot], in_sems.at[slot]) for slot in range(slots)]
    for fetch in fetches:
        fetch.start()
    for owner in range(places.shape[0]):
        places[owner] = jnp.full((8, 128), -1.0, jnp.float32)
    for copy in tables:
        copy.wait()

    def block(slot, owner):
        return pltpu.make_async_copy(blocks.at[slot], out.at[owner, :, 0:columns], out_sems.at[slot])

    for slot in range(slots):
        fetches[slot].wait()
        brick = aperture[slot]

        @pl.when(brick >= 0)
        def _():
            row = owner_map[brick]
            owner = row // 4
            block(slot, owner).start()
            places[owner] = jnp.full((8, 128), row % 4, jnp.int32).astype(jnp.float32)

    labels = pltpu.make_async_copy(places, out.at[:, :, columns : columns + 128], place_sem)
    labels.start()

    base = lax.axis_index("shots") * 4
    for place in range(4):
        owned[place] = 0

    @pl.loop(0, owner_map.shape[0] // 8)
    def _(group):
        for k in range(8):
            brick = group * 8 + k
            place = owner_map[brick] - base
            owned[jnp.where(jnp.logical_and(place >= 0, place < 4), place, 4)] = dip_class[brick]

    brick_of_row = rows() // 2
    classes = jnp.full((8, 128), owned[3], jnp.int32)
    for place in range(3):
        classes = jnp.where(brick_of_row == place, owned[place], classes)
    for i, value in enumerate(coefficients(classes)):
        coefs[i] = value

    for slot in range(slots):

        @pl.when(aperture[slot] >= 0)
        def _():
            block(slot, 0).wait()

    labels.wait()


def pack(aperture, owner_map, dip_class, partials, owners):
    slots, planes, columns = partials.shape
    hbm = pl.BlockSpec(memory_space=pltpu.HBM)
    return pl.pallas_call(
        pack_kernel,
        in_specs=[hbm] * 4,
        out_specs=[hbm, pl.BlockSpec(memory_space=pltpu.VMEM)],
        out_shape=[
            jax.ShapeDtypeStruct((owners, planes, columns + 128), jnp.float32),
            jax.ShapeDtypeStruct((10, 8, 128), jnp.float32),
        ],
        scratch_shapes=[
            pltpu.SMEM(aperture.shape, jnp.int32),
            pltpu.SMEM(owner_map.shape, jnp.int32),
            pltpu.SMEM(dip_class.shape, jnp.int32),
            pltpu.SMEM((8,), jnp.int32),
            pltpu.VMEM(partials.shape, jnp.float32),
            pltpu.VMEM((owners, planes, 128), jnp.float32),
            pltpu.SemaphoreType.DMA((3,)),
            pltpu.SemaphoreType.DMA((slots,)),
            pltpu.SemaphoreType.DMA((slots,)),
            pltpu.SemaphoreType.DMA,
        ],
        compiler_params=pltpu.CompilerParams(vmem_limit_bytes=60 << 20),
        name="pack_blocks",
    )(aperture, owner_map, dip_class, partials)


def merge_kernel(received, out, places, sums, place_sem):
    senders = received.shape[0]
    columns = received.shape[2] - 128
    labels = pltpu.make_async_copy(received.at[:, 0:1, columns : columns + 128], places, place_sem)
    labels.start()

    @pl.loop(0, 4)
    def _(brick):
        for tile in range(TILES):
            sums[brick, tile] = jnp.zeros((8, 128), jnp.float32)

    labels.wait()

    @pl.loop(0, senders)
    def _(sender):
        place = places[sender, 0, 0].astype(jnp.int32)

        @pl.when(place >= 0)
        def _():
            for tile in range(TILES):
                sums[place, tile] += received[sender, :, tile * 128 : tile * 128 + 128]

    low = lanes() < 64

    @pl.loop(0, 4)
    def _(b):
        for upper in range(2):
            for k in range(8):
                even = sums[b, upper * 16 + k]
                odd = sums[b, upper * 16 + 8 + k]
                base = k * 16 + b * 2 + upper
                out[pl.ds(base, 8, stride=128), :] = jnp.where(low, even, pltpu.roll(odd, 64, 1))
                out[pl.ds(base + 8, 8, stride=128), :] = jnp.where(low, pltpu.roll(even, 64, 1), odd)


def merge(received):
    senders = received.shape[0]
    vmem = pl.BlockSpec(memory_space=pltpu.VMEM)
    return pl.pallas_call(
        merge_kernel,
        in_specs=[vmem],
        out_specs=vmem,
        out_shape=jax.ShapeDtypeStruct((PLANES * STEPS * 8, 128), jnp.float32),
        scratch_shapes=[
            pltpu.SMEM((senders, 1, 128), jnp.float32),
            pltpu.VMEM((4, TILES, 8, 128), jnp.float32),
            pltpu.SemaphoreType.DMA,
        ],
        compiler_params=pltpu.CompilerParams(vmem_limit_bytes=32 << 20),
        name="merge_blocks",
    )(received)


def left_edge(last):
    turned = pltpu.roll(last, 64, 1)
    below = jnp.where(rows() % 2 == 0, 0.0, pltpu.roll(turned, 1, 0))
    return jnp.where(lanes() < 64, below, turned)


def right_edge(first):
    turned = pltpu.roll(first, 64, 1)
    above = jnp.where(rows() % 2 == 0, pltpu.roll(turned, 7, 0), 0.0)
    return jnp.where(lanes() < 64, turned, above)


def smooth_kernel(coefs, lower, own, upper, out, fresh, image, blur, slope, along, total, final):
    column = lanes() % 64
    first_y = column == 0
    last_y = column == 63

    def after(f):
        return jnp.where(last_y, 0.0, pltpu.roll(f, 127, 1))

    def before(f):
        return jnp.where(first_y, 0.0, pltpu.roll(f, 1, 1))

    def blur_y(f):
        return (f + after(f)) + (f + before(f))

    zero = jnp.zeros((8, 128), jnp.float32)

    def clear(field, plane):
        for step in range(1, STEPS + 1):
            field[plane, step] = zero

    def load(source, count, offset):
        @pl.loop(0, count // 2)
        def _(pair):
            for plane in (2 * pair, 2 * pair + 1):
                for step in range(STEPS):
                    fresh[plane + offset, step + 1] = source[plane, step]

    place = lax.axis_index("depth")
    first_plane = HALO - place * PLANES
    end_plane = HALO + (lax.axis_size("depth") - place) * PLANES

    def load_or_clear(source, offset, outside):
        @pl.when(jnp.logical_not(outside))
        def _():
            load(source, HALO, offset)

        @pl.when(outside)
        def _():
            @pl.loop(0, HALO)
            def _(plane):
                clear(fresh, plane + offset)

    load_or_clear(lower, 0, first_plane == HALO)
    load(own, PLANES, HALO)
    load_or_clear(upper, HALO + PLANES, end_plane == HALO + PLANES)

    def along_y(plane, step):
        if step == 0:
            cells = left_edge(fresh[plane, STEPS])
        elif step == STEPS + 1:
            cells = right_edge(fresh[plane, 1])
        else:
            cells = fresh[plane, step]
        image[plane, step] = cells
        up, down = after(cells), before(cells)
        blur[plane, step] = (cells + cells) + (up + down)
        slope[plane, step] = up - down

    def depth_blur(field, plane, step):
        deep = [field[plane - 1 + k, step] for k in range(GROUP + 2)]
        pairs = [deep[k] + deep[k + 1] for k in range(GROUP + 1)]
        return [pairs[k] + pairs[k + 1] for k in range(GROUP)], deep

    def depth_slope(deep):
        return [deep[k + 2] - deep[k] for k in range(GROUP)]

    @pl.loop(0, ITERS)
    def _(sweep):
        margin = 2 * sweep + 1
        start = jnp.maximum(margin, first_plane - 1)
        stop = jnp.minimum(DEEP - margin, end_plane + 1)

        @pl.loop(0, GROUP + 1)
        def _(k):
            for step in range(STEPS + 2):
                along_y(start - 1 + k, step)

        @pl.loop(0, (stop - start) // GROUP)
        def _(group):
            plane = start + group * GROUP
            norm_z, norm_x, norm_y = coefs[0], coefs[1], coefs[2]

            flat, steep, wide = {}, {}, {}

            def prepare(step):
                for k in range(GROUP):
                    along_y(plane + GROUP + k, step)
                flat[step], deep = depth_blur(blur, plane, step)
                steep[step] = depth_slope(deep)
                wide[step], _ = depth_blur(slope, plane, step)

            prepare(0)
            prepare(1)
            steep_pair = [steep[0][k] + steep[1][k] for k in range(GROUP)]
            wide_pair = [wide[0][k] + wide[1][k] for k in range(GROUP)]
            for step in range(1, STEPS + 1):
                prepare(step + 1)
                for k in range(GROUP):
                    steep_next = steep[step][k] + steep[step + 1][k]
                    wide_next = wide[step][k] + wide[step + 1][k]
                    grad_z = steep_pair[k] + steep_next
                    grad_x = flat[step + 1][k] - flat[step - 1][k]
                    grad_y = wide_pair[k] + wide_next
                    steep_pair[k], wide_pair[k] = steep_next, wide_next
                    aligned = norm_z * grad_z + norm_x * grad_x + norm_y * grad_y
                    aligned = aligned * aligned
                    whole = grad_z * grad_z + grad_x * grad_x + grad_y * grad_y
                    along[plane + k, step] = aligned
                    total[plane + k, step] = whole

        for outside, edge in ((first_plane == HALO, HALO - 1), (end_plane == HALO + PLANES, HALO + PLANES)):

            @pl.when(outside)
            def _():
                clear(along, edge)
                clear(total, edge)

        margin = margin + 1
        begin = jnp.maximum(margin, first_plane)
        finish = jnp.minimum(DEEP - margin, end_plane)

        @pl.loop(0, (finish - begin) // GROUP)
        def _(group):
            plane = begin + group * GROUP
            c_mid, c_zz, c_xx, c_yy, c_zx, c_zy, c_xy = [coefs[3 + i] for i in range(7)]
            a_cells, t_cells, deep, tilted = {}, {}, {}, {}

            def prepare(step):
                for field, cells in ((along, a_cells), (total, t_cells)):
                    if step == 0:
                        cells[0] = [left_edge(f) for f in depth_blur(field, plane, STEPS)[0]]
                        cells[STEPS + 1] = [right_edge(f) for f in depth_blur(field, plane, 1)[0]]
                    elif step <= STEPS:
                        cells[step], _ = depth_blur(field, plane, step)
                deep[step] = [image[plane - 1 + k, step] for k in range(GROUP + 2)]
                steep = depth_slope(deep[step])
                tilted[step] = [c_zx * steep[k] + c_xy * slope[plane + k, step] for k in range(GROUP)]

            prepare(0)
            prepare(1)
            a_pair = [a_cells[0][k] + a_cells[1][k] for k in range(GROUP)]
            t_pair = [t_cells[0][k] + t_cells[1][k] for k in range(GROUP)]
            for step in range(1, STEPS + 1):
                prepare(step + 1)
                lean = depth_slope([slope[plane - 1 + k, step] for k in range(GROUP + 2)])
                for k in range(GROUP):
                    a_new = a_cells[step][k] + a_cells[step + 1][k]
                    t_new = t_cells[step][k] + t_cells[step + 1][k]
                    aligned = blur_y(a_pair[k] + a_new)
                    whole = blur_y(t_pair[k] + t_new)
                    a_pair[k], t_pair[k] = a_new, t_new
                    weight = aligned / (whole + jnp.float32(TINY * 65536.0))
                    now = deep[step][k + 1]
                    change = (
                        (c_mid * now + c_zz * (deep[step][k] + deep[step][k + 2]))
                        + (c_xx * (deep[step - 1][k + 1] + deep[step + 1][k + 1]) + c_yy * blur[plane + k, step])
                        + ((tilted[step + 1][k] - tilted[step - 1][k]) + c_zy * lean[k])
                    )
                    new = now + weight * change
                    fresh[plane + k, step] = new

    @pl.loop(0, PLANES)
    def _(plane):
        for step in range(STEPS):
            final[pl.ds(pl.multiple_of(plane * 128, 128) + step * 8, 8), :] = fresh[plane + HALO, step + 1]

    low_half = lanes() < 64

    @pl.loop(0, 4)
    def _(b):
        for half in range(2):
            for k in range(8):
                base = k * 16 + b * 2 + half
                first = final[pl.ds(base, 8, stride=128), :]
                second = final[pl.ds(base + 8, 8, stride=128), :]
                tile = half * 16 + k
                out[b, :, tile * 128 : tile * 128 + 128] = jnp.where(low_half, first, pltpu.roll(second, 64, 1))
                tile += 8
                out[b, :, tile * 128 : tile * 128 + 128] = jnp.where(low_half, pltpu.roll(first, 64, 1), second)


def smooth(coefs, lower, own, upper, interpret=False):
    field = pltpu.VMEM((DEEP + GROUP, STEPS + 2, 8, 128), jnp.float32)
    vmem = pl.BlockSpec(memory_space=pltpu.VMEM)
    return pl.pallas_call(
        smooth_kernel,
        in_specs=[vmem] * 4,
        out_specs=vmem,
        out_shape=jax.ShapeDtypeStruct((4, PLANES, STEPS * 256), jnp.float32),
        scratch_shapes=[field] * 6 + [pltpu.VMEM((PLANES * STEPS * 8, 128), jnp.float32)],
        compiler_params=pltpu.CompilerParams(vmem_limit_bytes=32 << 20),
        name="smooth_image",
        interpret=interpret,
    )(coefs, lower, own, upper)


def local(partials, aperture, owner_map, dip_class):
    sent, coefs = pack(aperture, owner_map, dip_class, partials, lax.axis_size("shots"))
    received = lax.all_to_all(sent, "shots", 0, 0, tiled=True)
    image = merge(received).reshape(PLANES, STEPS, 8, 128)
    depth_count = lax.axis_size("depth")
    lower = lax.ppermute(image[PLANES - HALO :], "depth", [(i, (i + 1) % depth_count) for i in range(depth_count)])
    upper = lax.ppermute(image[:HALO], "depth", [((i + 1) % depth_count, i) for i in range(depth_count)])
    return smooth(coefs, lower, image, upper)


def solution(mesh):
    placed = (P("shots", "depth", None), P("shots"), P(), P())
    return jax.shard_map(
        local, mesh=mesh, in_specs=placed, out_specs=P("shots", "depth", None), check_vma=False
    )
```

```python
import math

import jax
import jax.numpy as jnp
from jax import lax
from jax.experimental import pallas as pl
from jax.experimental.pallas import tpu as pltpu
from jax.sharding import PartitionSpec as P

STEPS = 16
HALO = 6
PLANES = 8
DEEP = PLANES + 2 * HALO
ITERS = 3
RATE = 0.15
TINY = 1e-6
TILES = 32
GROUP = 2
PITCH = STEPS * 8 + 8


def lanes():
    return lax.broadcasted_iota(jnp.int32, (8, 128), 1)


def rows():
    return lax.broadcasted_iota(jnp.int32, (8, 128), 0)


def coefficients(classes):
    tilt = 0.2 + 0.1 * (classes & 3).astype(jnp.float32)
    azimuth = 0.3 + math.pi / 2.0 * (classes >> 2).astype(jnp.float32)
    norm_z = jnp.cos(tilt)
    norm_x = jnp.sin(tilt) * jnp.cos(azimuth)
    norm_y = jnp.sin(tilt) * jnp.sin(azimuth)
    c_zz = RATE * (1.0 - norm_z * norm_z)
    c_xx = RATE * (1.0 - norm_x * norm_x)
    c_yy = RATE * (1.0 - norm_y * norm_y)
    cross = -0.5 * RATE
    return [
        norm_z,
        norm_x,
        norm_y,
        -2.0 * (c_zz + c_xx + 2.0 * c_yy),
        c_zz,
        c_xx,
        c_yy,
        cross * norm_z * norm_x,
        cross * norm_z * norm_y,
        cross * norm_x * norm_y,
    ]


def pack_kernel(
    aperture_hbm, owner_map_hbm, dip_class_hbm, partials, out, coefs, aperture, owner_map, dip_class, owned,
    blocks, places, table_sems, in_sems, out_sems, place_sem
):
    slots = partials.shape[0]
    columns = partials.shape[2]
    tables = [
        pltpu.make_async_copy(aperture_hbm, aperture, table_sems.at[0]),
        pltpu.make_async_copy(owner_map_hbm, owner_map, table_sems.at[1]),
        pltpu.make_async_copy(dip_class_hbm, dip_class, table_sems.at[2]),
    ]
    for copy in tables:
        copy.start()
    fetches = [pltpu.make_async_copy(partials.at[slot], blocks.at[slot], in_sems.at[slot]) for slot in range(slots)]
    for fetch in fetches:
        fetch.start()
    for owner in range(places.shape[0]):
        places[owner] = jnp.full((8, 128), -1.0, jnp.float32)
    for copy in tables:
        copy.wait()

    def block(slot, owner):
        return pltpu.make_async_copy(blocks.at[slot], out.at[owner, :, 0:columns], out_sems.at[slot])

    for slot in range(slots):
        fetches[slot].wait()
        brick = aperture[slot]

        @pl.when(brick >= 0)
        def _():
            row = owner_map[brick]
            owner = row // 4
            block(slot, owner).start()
            places[owner] = jnp.full((8, 128), row % 4, jnp.int32).astype(jnp.float32)

    labels = pltpu.make_async_copy(places, out.at[:, :, columns : columns + 128], place_sem)
    labels.start()

    base = lax.axis_index("shots") * 4
    for place in range(4):
        owned[place] = 0

    @pl.loop(0, owner_map.shape[0] // 8)
    def _(group):
        for k in range(8):
            brick = group * 8 + k
            place = owner_map[brick] - base

            @pl.when(jnp.logical_and(place >= 0, place < 4))
            def _():
                owned[place] = dip_class[brick]

    brick_of_row = rows() // 2
    classes = jnp.full((8, 128), owned[3], jnp.int32)
    for place in range(3):
        classes = jnp.where(brick_of_row == place, owned[place], classes)
    for i, value in enumerate(coefficients(classes)):
        coefs[i] = value

    for slot in range(slots):

        @pl.when(aperture[slot] >= 0)
        def _():
            block(slot, 0).wait()

    labels.wait()


def pack(aperture, owner_map, dip_class, partials, owners):
    slots, planes, columns = partials.shape
    hbm = pl.BlockSpec(memory_space=pltpu.HBM)
    return pl.pallas_call(
        pack_kernel,
        in_specs=[hbm] * 4,
        out_specs=[hbm, pl.BlockSpec(memory_space=pltpu.VMEM)],
        out_shape=[
            jax.ShapeDtypeStruct((owners, planes, columns + 128), jnp.float32),
            jax.ShapeDtypeStruct((10, 8, 128), jnp.float32),
        ],
        scratch_shapes=[
            pltpu.SMEM(aperture.shape, jnp.int32),
            pltpu.SMEM(owner_map.shape, jnp.int32),
            pltpu.SMEM(dip_class.shape, jnp.int32),
            pltpu.SMEM((4,), jnp.int32),
            pltpu.VMEM(partials.shape, jnp.float32),
            pltpu.VMEM((owners, planes, 128), jnp.float32),
            pltpu.SemaphoreType.DMA((3,)),
            pltpu.SemaphoreType.DMA((slots,)),
            pltpu.SemaphoreType.DMA((slots,)),
            pltpu.SemaphoreType.DMA,
        ],
        compiler_params=pltpu.CompilerParams(vmem_limit_bytes=60 << 20),
        name="pack_blocks",
    )(aperture, owner_map, dip_class, partials)


def merge_kernel(received, out, places, sums, spread, place_sem):
    senders = received.shape[0]
    columns = received.shape[2] - 128
    labels = pltpu.make_async_copy(received.at[:, 0:1, columns : columns + 128], places, place_sem)
    labels.start()
    for brick in range(4):
        for tile in range(TILES):
            sums[brick, tile] = jnp.zeros((8, 128), jnp.float32)
    labels.wait()

    @pl.loop(0, senders)
    def _(sender):
        place = places[sender, 0, 0].astype(jnp.int32)

        @pl.when(place >= 0)
        def _():
            for tile in range(TILES):
                sums[place, tile] += received[sender, :, tile * 128 : tile * 128 + 128]

    low = lanes() < 64
    for b in range(4):
        for upper in range(2):
            for k in range(8):
                even = sums[b, upper * 16 + k]
                odd = sums[b, upper * 16 + 8 + k]
                base = k * 16 + b * 2 + upper
                spread[pl.ds(base, 8, stride=PITCH), :] = jnp.where(low, even, pltpu.roll(odd, 64, 1))
                spread[pl.ds(base + 8, 8, stride=PITCH), :] = jnp.where(low, pltpu.roll(even, 64, 1), odd)

    for plane in range(PLANES):
        out[plane * STEPS * 8 : (plane + 1) * STEPS * 8, :] = spread[plane * PITCH : plane * PITCH + STEPS * 8, :]


def merge(received):
    senders = received.shape[0]
    vmem = pl.BlockSpec(memory_space=pltpu.VMEM)
    return pl.pallas_call(
        merge_kernel,
        in_specs=[vmem],
        out_specs=vmem,
        out_shape=jax.ShapeDtypeStruct((PLANES * STEPS * 8, 128), jnp.float32),
        scratch_shapes=[
            pltpu.SMEM((senders, 1, 128), jnp.float32),
            pltpu.VMEM((4, TILES, 8, 128), jnp.float32),
            pltpu.VMEM((PLANES * PITCH, 128), jnp.float32),
            pltpu.SemaphoreType.DMA,
        ],
        compiler_params=pltpu.CompilerParams(vmem_limit_bytes=32 << 20),
        name="merge_blocks",
    )(received)


def left_edge(last):
    turned = pltpu.roll(last, 64, 1)
    below = jnp.where(rows() % 2 == 0, 0.0, pltpu.roll(turned, 1, 0))
    return jnp.where(lanes() < 64, below, turned)


def right_edge(first):
    turned = pltpu.roll(first, 64, 1)
    above = jnp.where(rows() % 2 == 0, pltpu.roll(turned, 7, 0), 0.0)
    return jnp.where(lanes() < 64, turned, above)


def smooth_kernel(coefs, lower, own, upper, out, image, other, blur, slope, along, total, final):
    column = lanes() % 64
    first_y = column == 0
    last_y = column == 63

    def after(f):
        return jnp.where(last_y, 0.0, pltpu.roll(f, 127, 1))

    def before(f):
        return jnp.where(first_y, 0.0, pltpu.roll(f, 1, 1))

    def blur_y(f):
        return (f + after(f)) + (f + before(f))

    zero = jnp.zeros((8, 128), jnp.float32)

    def clear(field, plane):
        for step in range(1, STEPS + 1):
            field[plane, step] = zero

    for plane in (HALO - 1, HALO + PLANES):
        clear(other, plane)

    def load(source, count, offset):
        @pl.loop(0, count // 2)
        def _(pair):
            for plane in (2 * pair, 2 * pair + 1):
                for step in range(STEPS):
                    image[plane + offset, step + 1] = source[plane, step]

    place = lax.axis_index("depth")
    first_plane = HALO - place * PLANES
    end_plane = HALO + (lax.axis_size("depth") - place) * PLANES

    def load_or_clear(source, offset, outside):
        @pl.when(jnp.logical_not(outside))
        def _():
            load(source, HALO, offset)

        @pl.when(outside)
        def _():
            for plane in range(HALO):
                clear(image, plane + offset)

    load_or_clear(lower, 0, first_plane == HALO)
    load(own, PLANES, HALO)
    load_or_clear(upper, HALO + PLANES, end_plane == HALO + PLANES)

    def along_y(source, plane, step):
        if step == 0:
            cells = left_edge(source[plane, STEPS])
        elif step == STEPS + 1:
            cells = right_edge(source[plane, 1])
        else:
            cells = source[plane, step]
        if step in (0, STEPS + 1):
            source[plane, step] = cells
        up, down = after(cells), before(cells)
        blur[plane, step] = (cells + cells) + (up + down)
        slope[plane, step] = up - down

    def depth_blur(field, plane, step):
        deep = [field[plane - 1 + k, step] for k in range(GROUP + 2)]
        pairs = [deep[k] + deep[k + 1] for k in range(GROUP + 1)]
        return [pairs[k] + pairs[k + 1] for k in range(GROUP)], deep

    def depth_slope(deep):
        return [deep[k + 2] - deep[k] for k in range(GROUP)]

    for sweep in range(ITERS):
        source = image if sweep % 2 == 0 else other
        target = other if sweep % 2 == 0 else image
        margin = 2 * sweep + 1
        start = jnp.maximum(margin, first_plane - 1)
        stop = jnp.minimum(DEEP - margin, end_plane + 1)

        for k in range(GROUP + 1):
            for step in range(STEPS + 2):
                along_y(source, start - 1 + k, step)

        @pl.loop(0, (stop - start) // GROUP)
        def _(group):
            plane = start + group * GROUP
            norm_z, norm_x, norm_y = coefs[0], coefs[1], coefs[2]

            flat, steep, wide = {}, {}, {}

            def prepare(step):
                for k in range(GROUP):
                    along_y(source, plane + GROUP + k, step)
                flat[step], deep = depth_blur(blur, plane, step)
                steep[step] = depth_slope(deep)
                wide[step], _ = depth_blur(slope, plane, step)

            prepare(0)
            prepare(1)
            steep_pair = [steep[0][k] + steep[1][k] for k in range(GROUP)]
            wide_pair = [wide[0][k] + wide[1][k] for k in range(GROUP)]
            for step in range(1, STEPS + 1):
                prepare(step + 1)
                for k in range(GROUP):
                    steep_next = steep[step][k] + steep[step + 1][k]
                    wide_next = wide[step][k] + wide[step + 1][k]
                    grad_z = steep_pair[k] + steep_next
                    grad_x = flat[step + 1][k] - flat[step - 1][k]
                    grad_y = wide_pair[k] + wide_next
                    steep_pair[k], wide_pair[k] = steep_next, wide_next
                    aligned = norm_z * grad_z + norm_x * grad_x + norm_y * grad_y
                    aligned = aligned * aligned
                    whole = grad_z * grad_z + grad_x * grad_x + grad_y * grad_y
                    along[plane + k, step] = aligned
                    total[plane + k, step] = whole

        for outside, edge in ((first_plane == HALO, HALO - 1), (end_plane == HALO + PLANES, HALO + PLANES)):

            @pl.when(outside)
            def _():
                clear(along, edge)
                clear(total, edge)

        margin += 1
        begin = jnp.maximum(margin, first_plane)
        finish = jnp.minimum(DEEP - margin, end_plane)

        @pl.loop(0, (finish - begin) // GROUP)
        def _(group):
            plane = begin + group * GROUP
            c_mid, c_zz, c_xx, c_yy, c_zx, c_zy, c_xy = [coefs[3 + i] for i in range(7)]
            a_cells, t_cells, deep, tilted = {}, {}, {}, {}

            def prepare(step):
                for field, cells in ((along, a_cells), (total, t_cells)):
                    if step == 0:
                        cells[0] = [left_edge(f) for f in depth_blur(field, plane, STEPS)[0]]
                        cells[STEPS + 1] = [right_edge(f) for f in depth_blur(field, plane, 1)[0]]
                    elif step <= STEPS:
                        cells[step], _ = depth_blur(field, plane, step)
                deep[step] = [source[plane - 1 + k, step] for k in range(GROUP + 2)]
                steep = depth_slope(deep[step])
                tilted[step] = [c_zx * steep[k] + c_xy * slope[plane + k, step] for k in range(GROUP)]

            prepare(0)
            prepare(1)
            a_pair = [a_cells[0][k] + a_cells[1][k] for k in range(GROUP)]
            t_pair = [t_cells[0][k] + t_cells[1][k] for k in range(GROUP)]
            for step in range(1, STEPS + 1):
                prepare(step + 1)
                lean = depth_slope([slope[plane - 1 + k, step] for k in range(GROUP + 2)])
                for k in range(GROUP):
                    a_new = a_cells[step][k] + a_cells[step + 1][k]
                    t_new = t_cells[step][k] + t_cells[step + 1][k]
                    aligned = blur_y(a_pair[k] + a_new)
                    whole = blur_y(t_pair[k] + t_new)
                    a_pair[k], t_pair[k] = a_new, t_new
                    weight = aligned / (whole + jnp.float32(TINY * 65536.0))
                    now = deep[step][k + 1]
                    change = (
                        (c_mid * now + c_zz * (deep[step][k] + deep[step][k + 2]))
                        + (c_xx * (deep[step - 1][k + 1] + deep[step + 1][k + 1]) + c_yy * blur[plane + k, step])
                        + ((tilted[step + 1][k] - tilted[step - 1][k]) + c_zy * lean[k])
                    )
                    new = now + weight * change
                    if sweep < ITERS - 1:
                        target[plane + k, step] = new
                    else:
                        base = pl.multiple_of((plane + k - HALO) * PITCH, 8) + (step - 1) * 8
                        final[pl.ds(base, 8), :] = new

    low_half = lanes() < 64
    for b in range(4):
        for half in range(2):
            for k in range(8):
                base = k * 16 + b * 2 + half
                first = final[pl.ds(base, 8, stride=PITCH), :]
                second = final[pl.ds(base + 8, 8, stride=PITCH), :]
                tile = half * 16 + k
                out[b, :, tile * 128 : tile * 128 + 128] = jnp.where(low_half, first, pltpu.roll(second, 64, 1))
                tile += 8
                out[b, :, tile * 128 : tile * 128 + 128] = jnp.where(low_half, pltpu.roll(first, 64, 1), second)


def smooth(coefs, lower, own, upper, interpret=False):
    field = pltpu.VMEM((DEEP + GROUP, STEPS + 2, 8, 128), jnp.float32)
    vmem = pl.BlockSpec(memory_space=pltpu.VMEM)
    return pl.pallas_call(
        smooth_kernel,
        in_specs=[vmem] * 4,
        out_specs=vmem,
        out_shape=jax.ShapeDtypeStruct((4, PLANES, STEPS * 256), jnp.float32),
        scratch_shapes=[field] * 6 + [pltpu.VMEM((PLANES * PITCH, 128), jnp.float32)],
        compiler_params=pltpu.CompilerParams(vmem_limit_bytes=32 << 20),
        name="smooth_image",
        interpret=interpret,
    )(coefs, lower, own, upper)


def local(partials, aperture, owner_map, dip_class):
    sent, coefs = pack(aperture, owner_map, dip_class, partials, lax.axis_size("shots"))
    received = lax.all_to_all(sent, "shots", 0, 0, tiled=True)
    image = merge(received).reshape(PLANES, STEPS, 8, 128)
    depth_count = lax.axis_size("depth")
    lower = lax.ppermute(image[PLANES - HALO :], "depth", [(i, (i + 1) % depth_count) for i in range(depth_count)])
    upper = lax.ppermute(image[:HALO], "depth", [((i + 1) % depth_count, i) for i in range(depth_count)])
    return smooth(coefs, lower, image, upper)


def solution(mesh):
    placed = (P("shots", "depth", None), P("shots"), P(), P())
    return jax.shard_map(
        local, mesh=mesh, in_specs=placed, out_specs=P("shots", "depth", None), check_vma=False
    )
```

```python
import math

import jax
import jax.numpy as jnp
from jax import lax
from jax.experimental import pallas as pl
from jax.experimental.pallas import tpu as pltpu
from jax.sharding import PartitionSpec as P

STEPS = 16
HALO = 6
PLANES = 8
DEEP = PLANES + 2 * HALO
ITERS = 3
RATE = 0.15
TINY = 1e-6
TILES = 32
GROUP = 2
PITCH = STEPS * 8 + 8


def lanes():
    return lax.broadcasted_iota(jnp.int32, (8, 128), 1)


def rows():
    return lax.broadcasted_iota(jnp.int32, (8, 128), 0)


def coefficients(classes):
    tilt = 0.2 + 0.1 * (classes & 3).astype(jnp.float32)
    azimuth = 0.3 + math.pi / 2.0 * (classes >> 2).astype(jnp.float32)
    norm_z = jnp.cos(tilt)
    norm_x = jnp.sin(tilt) * jnp.cos(azimuth)
    norm_y = jnp.sin(tilt) * jnp.sin(azimuth)
    c_zz = RATE * (1.0 - norm_z * norm_z)
    c_xx = RATE * (1.0 - norm_x * norm_x)
    c_yy = RATE * (1.0 - norm_y * norm_y)
    cross = -0.5 * RATE
    return [
        norm_z,
        norm_x,
        norm_y,
        -2.0 * (c_zz + c_xx + 2.0 * c_yy),
        c_zz,
        c_xx,
        c_yy,
        cross * norm_z * norm_x,
        cross * norm_z * norm_y,
        cross * norm_x * norm_y,
    ]


def pack_kernel(
    aperture_hbm, owner_map_hbm, dip_class_hbm, partials, out, coefs, aperture, owner_map, dip_class, owned,
    blocks, places, table_sems, in_sems, out_sems, place_sem
):
    slots = partials.shape[0]
    columns = partials.shape[2]
    tables = [
        pltpu.make_async_copy(aperture_hbm, aperture, table_sems.at[0]),
        pltpu.make_async_copy(owner_map_hbm, owner_map, table_sems.at[1]),
        pltpu.make_async_copy(dip_class_hbm, dip_class, table_sems.at[2]),
    ]
    for copy in tables:
        copy.start()
    fetches = [pltpu.make_async_copy(partials.at[slot], blocks.at[slot], in_sems.at[slot]) for slot in range(slots)]
    for fetch in fetches:
        fetch.start()
    for owner in range(places.shape[0]):
        places[owner] = jnp.full((8, 128), -1.0, jnp.float32)
    for copy in tables:
        copy.wait()

    def block(slot, owner):
        return pltpu.make_async_copy(blocks.at[slot], out.at[owner, :, 0:columns], out_sems.at[slot])

    for slot in range(slots):
        fetches[slot].wait()
        brick = aperture[slot]

        @pl.when(brick >= 0)
        def _():
            row = owner_map[brick]
            owner = row // 4
            block(slot, owner).start()
            places[owner] = jnp.full((8, 128), row % 4, jnp.int32).astype(jnp.float32)

    labels = pltpu.make_async_copy(places, out.at[:, :, columns : columns + 128], place_sem)
    labels.start()

    base = lax.axis_index("shots") * 4
    for place in range(4):
        owned[place] = 0

    @pl.loop(0, owner_map.shape[0] // 8)
    def _(group):
        for k in range(8):
            brick = group * 8 + k
            place = owner_map[brick] - base

            @pl.when(jnp.logical_and(place >= 0, place < 4))
            def _():
                owned[place] = dip_class[brick]

    brick_of_row = rows() // 2
    classes = jnp.full((8, 128), owned[3], jnp.int32)
    for place in range(3):
        classes = jnp.where(brick_of_row == place, owned[place], classes)
    for i, value in enumerate(coefficients(classes)):
        coefs[i] = value

    for slot in range(slots):

        @pl.when(aperture[slot] >= 0)
        def _():
            block(slot, 0).wait()

    labels.wait()


def pack(aperture, owner_map, dip_class, partials, owners):
    slots, planes, columns = partials.shape
    hbm = pl.BlockSpec(memory_space=pltpu.HBM)
    return pl.pallas_call(
        pack_kernel,
        in_specs=[hbm] * 4,
        out_specs=[hbm, pl.BlockSpec(memory_space=pltpu.VMEM)],
        out_shape=[
            jax.ShapeDtypeStruct((owners, planes, columns + 128), jnp.float32),
            jax.ShapeDtypeStruct((10, 8, 128), jnp.float32),
        ],
        scratch_shapes=[
            pltpu.SMEM(aperture.shape, jnp.int32),
            pltpu.SMEM(owner_map.shape, jnp.int32),
            pltpu.SMEM(dip_class.shape, jnp.int32),
            pltpu.SMEM((4,), jnp.int32),
            pltpu.VMEM(partials.shape, jnp.float32),
            pltpu.VMEM((owners, planes, 128), jnp.float32),
            pltpu.SemaphoreType.DMA((3,)),
            pltpu.SemaphoreType.DMA((slots,)),
            pltpu.SemaphoreType.DMA((slots,)),
            pltpu.SemaphoreType.DMA,
        ],
        compiler_params=pltpu.CompilerParams(vmem_limit_bytes=60 << 20),
        name="pack_blocks",
    )(aperture, owner_map, dip_class, partials)


def merge_kernel(received, out, places, sums, spread, place_sem):
    senders = received.shape[0]
    columns = received.shape[2] - 128
    labels = pltpu.make_async_copy(received.at[:, 0:1, columns : columns + 128], places, place_sem)
    labels.start()
    for brick in range(4):
        for tile in range(TILES):
            sums[brick, tile] = jnp.zeros((8, 128), jnp.float32)
    labels.wait()

    @pl.loop(0, senders)
    def _(sender):
        place = places[sender, 0, 0].astype(jnp.int32)

        @pl.when(place >= 0)
        def _():
            for tile in range(TILES):
                sums[place, tile] += received[sender, :, tile * 128 : tile * 128 + 128]

    low = lanes() < 64
    for b in range(4):
        for upper in range(2):
            for k in range(8):
                even = sums[b, upper * 16 + k]
                odd = sums[b, upper * 16 + 8 + k]
                base = k * 16 + b * 2 + upper
                spread[pl.ds(base, 8, stride=PITCH), :] = jnp.where(low, even, pltpu.roll(odd, 64, 1))
                spread[pl.ds(base + 8, 8, stride=PITCH), :] = jnp.where(low, pltpu.roll(even, 64, 1), odd)

    for plane in range(PLANES):
        out[plane * STEPS * 8 : (plane + 1) * STEPS * 8, :] = spread[plane * PITCH : plane * PITCH + STEPS * 8, :]


def merge(received):
    senders = received.shape[0]
    vmem = pl.BlockSpec(memory_space=pltpu.VMEM)
    return pl.pallas_call(
        merge_kernel,
        in_specs=[vmem],
        out_specs=vmem,
        out_shape=jax.ShapeDtypeStruct((PLANES * STEPS * 8, 128), jnp.float32),
        scratch_shapes=[
            pltpu.SMEM((senders, 1, 128), jnp.float32),
            pltpu.VMEM((4, TILES, 8, 128), jnp.float32),
            pltpu.VMEM((PLANES * PITCH, 128), jnp.float32),
            pltpu.SemaphoreType.DMA,
        ],
        compiler_params=pltpu.CompilerParams(vmem_limit_bytes=32 << 20),
        name="merge_blocks",
    )(received)


def left_edge(last):
    turned = pltpu.roll(last, 64, 1)
    below = jnp.where(rows() % 2 == 0, 0.0, pltpu.roll(turned, 1, 0))
    return jnp.where(lanes() < 64, below, turned)


def right_edge(first):
    turned = pltpu.roll(first, 64, 1)
    above = jnp.where(rows() % 2 == 0, pltpu.roll(turned, 7, 0), 0.0)
    return jnp.where(lanes() < 64, turned, above)


def smooth_kernel(coefs, lower, own, upper, out, image, other, blur, slope, along, total, final):
    column = lanes() % 64
    first_y = column == 0
    last_y = column == 63

    def after(f):
        return jnp.where(last_y, 0.0, pltpu.roll(f, 127, 1))

    def before(f):
        return jnp.where(first_y, 0.0, pltpu.roll(f, 1, 1))

    def blur_y(f):
        return (f + after(f)) + (f + before(f))

    zero = jnp.zeros((8, 128), jnp.float32)

    def clear(field, plane):
        for step in range(1, STEPS + 1):
            field[plane, step] = zero

    def load(source, count, offset):
        @pl.loop(0, count // 2)
        def _(pair):
            for plane in (2 * pair, 2 * pair + 1):
                for step in range(STEPS):
                    image[plane + offset, step + 1] = source[plane, step]

    place = lax.axis_index("depth")
    low_end = place == 0
    high_end = place == lax.axis_size("depth") - 1

    def load_or_clear(source, offset, outside):
        @pl.when(jnp.logical_not(outside))
        def _():
            load(source, HALO, offset)

        @pl.when(outside)
        def _():
            for plane in range(HALO):
                clear(image, plane + offset)

    load_or_clear(lower, 0, low_end)
    load(own, PLANES, HALO)
    load_or_clear(upper, HALO + PLANES, high_end)

    def along_y(source, plane, step):
        if step == 0:
            cells = left_edge(source[plane, STEPS])
        elif step == STEPS + 1:
            cells = right_edge(source[plane, 1])
        else:
            cells = source[plane, step]
        if step in (0, STEPS + 1):
            source[plane, step] = cells
        up, down = after(cells), before(cells)
        blur[plane, step] = (cells + cells) + (up + down)
        slope[plane, step] = up - down

    def depth_blur(field, plane, step):
        deep = [field[plane - 1 + k, step] for k in range(GROUP + 2)]
        pairs = [deep[k] + deep[k + 1] for k in range(GROUP + 1)]
        return [pairs[k] + pairs[k + 1] for k in range(GROUP)], deep

    def depth_slope(deep):
        return [deep[k + 2] - deep[k] for k in range(GROUP)]

    def clear_outside(*fields):
        for outside, edge in ((low_end, HALO - 1), (high_end, HALO + PLANES)):

            @pl.when(outside)
            def _():
                for field in fields:
                    clear(field, edge)

    for sweep in range(ITERS):
        source = image if sweep % 2 == 0 else other
        target = other if sweep % 2 == 0 else image
        margin = 2 * sweep + 1
        start, stop = margin, DEEP - margin

        for k in range(GROUP + 1):
            for step in range(STEPS + 2):
                along_y(source, start - 1 + k, step)

        @pl.loop(0, (stop - start) // GROUP)
        def _(group):
            plane = start + group * GROUP
            norm_z, norm_x, norm_y = coefs[0], coefs[1], coefs[2]

            flat, steep, wide = {}, {}, {}

            def prepare(step):
                for k in range(GROUP):
                    along_y(source, plane + GROUP + k, step)
                flat[step], deep = depth_blur(blur, plane, step)
                steep[step] = depth_slope(deep)
                wide[step], _ = depth_blur(slope, plane, step)

            prepare(0)
            prepare(1)
            steep_pair = [steep[0][k] + steep[1][k] for k in range(GROUP)]
            wide_pair = [wide[0][k] + wide[1][k] for k in range(GROUP)]
            for step in range(1, STEPS + 1):
                prepare(step + 1)
                for k in range(GROUP):
                    steep_next = steep[step][k] + steep[step + 1][k]
                    wide_next = wide[step][k] + wide[step + 1][k]
                    grad_z = steep_pair[k] + steep_next
                    grad_x = flat[step + 1][k] - flat[step - 1][k]
                    grad_y = wide_pair[k] + wide_next
                    steep_pair[k], wide_pair[k] = steep_next, wide_next
                    aligned = norm_z * grad_z + norm_x * grad_x + norm_y * grad_y
                    aligned = aligned * aligned
                    whole = grad_z * grad_z + grad_x * grad_x + grad_y * grad_y
                    along[plane + k, step] = aligned
                    total[plane + k, step] = whole

        clear_outside(along, total)

        margin += 1
        begin, finish = margin, DEEP - margin

        @pl.loop(0, (finish - begin) // GROUP)
        def _(group):
            plane = begin + group * GROUP
            c_mid, c_zz, c_xx, c_yy, c_zx, c_zy, c_xy = [coefs[3 + i] for i in range(7)]
            a_cells, t_cells, deep, tilted = {}, {}, {}, {}

            def prepare(step):
                for field, cells in ((along, a_cells), (total, t_cells)):
                    if step == 0:
                        cells[0] = [left_edge(f) for f in depth_blur(field, plane, STEPS)[0]]
                        cells[STEPS + 1] = [right_edge(f) for f in depth_blur(field, plane, 1)[0]]
                    elif step <= STEPS:
                        cells[step], _ = depth_blur(field, plane, step)
                deep[step] = [source[plane - 1 + k, step] for k in range(GROUP + 2)]
                steep = depth_slope(deep[step])
                tilted[step] = [c_zx * steep[k] + c_xy * slope[plane + k, step] for k in range(GROUP)]

            prepare(0)
            prepare(1)
            a_pair = [a_cells[0][k] + a_cells[1][k] for k in range(GROUP)]
            t_pair = [t_cells[0][k] + t_cells[1][k] for k in range(GROUP)]
            for step in range(1, STEPS + 1):
                prepare(step + 1)
                lean = depth_slope([slope[plane - 1 + k, step] for k in range(GROUP + 2)])
                for k in range(GROUP):
                    a_new = a_cells[step][k] + a_cells[step + 1][k]
                    t_new = t_cells[step][k] + t_cells[step + 1][k]
                    aligned = blur_y(a_pair[k] + a_new)
                    whole = blur_y(t_pair[k] + t_new)
                    a_pair[k], t_pair[k] = a_new, t_new
                    weight = aligned / (whole + jnp.float32(TINY * 65536.0))
                    now = deep[step][k + 1]
                    change = (
                        (c_mid * now + c_zz * (deep[step][k] + deep[step][k + 2]))
                        + (c_xx * (deep[step - 1][k + 1] + deep[step + 1][k + 1]) + c_yy * blur[plane + k, step])
                        + ((tilted[step + 1][k] - tilted[step - 1][k]) + c_zy * lean[k])
                    )
                    new = now + weight * change
                    if sweep < ITERS - 1:
                        target[plane + k, step] = new
                    else:
                        base = pl.multiple_of((plane + k - HALO) * PITCH, 8) + (step - 1) * 8
                        final[pl.ds(base, 8), :] = new

        if sweep < ITERS - 1:
            clear_outside(target)

    low_half = lanes() < 64
    for b in range(4):
        for half in range(2):
            for k in range(8):
                base = k * 16 + b * 2 + half
                first = final[pl.ds(base, 8, stride=PITCH), :]
                second = final[pl.ds(base + 8, 8, stride=PITCH), :]
                tile = half * 16 + k
                out[b, :, tile * 128 : tile * 128 + 128] = jnp.where(low_half, first, pltpu.roll(second, 64, 1))
                tile += 8
                out[b, :, tile * 128 : tile * 128 + 128] = jnp.where(low_half, pltpu.roll(first, 64, 1), second)


def smooth(coefs, lower, own, upper, interpret=False):
    field = pltpu.VMEM((DEEP + GROUP, STEPS + 2, 8, 128), jnp.float32)
    vmem = pl.BlockSpec(memory_space=pltpu.VMEM)
    return pl.pallas_call(
        smooth_kernel,
        in_specs=[vmem] * 4,
        out_specs=vmem,
        out_shape=jax.ShapeDtypeStruct((4, PLANES, STEPS * 256), jnp.float32),
        scratch_shapes=[field] * 6 + [pltpu.VMEM((PLANES * PITCH, 128), jnp.float32)],
        compiler_params=pltpu.CompilerParams(vmem_limit_bytes=32 << 20),
        name="smooth_image",
        interpret=interpret,
    )(coefs, lower, own, upper)


def local(partials, aperture, owner_map, dip_class):
    sent, coefs = pack(aperture, owner_map, dip_class, partials, lax.axis_size("shots"))
    received = lax.all_to_all(sent, "shots", 0, 0, tiled=True)
    image = merge(received).reshape(PLANES, STEPS, 8, 128)
    depth_count = lax.axis_size("depth")
    lower = lax.ppermute(image[PLANES - HALO :], "depth", [(i, (i + 1) % depth_count) for i in range(depth_count)])
    upper = lax.ppermute(image[:HALO], "depth", [((i + 1) % depth_count, i) for i in range(depth_count)])
    return smooth(coefs, lower, image, upper)


def solution(mesh):
    placed = (P("shots", "depth", None), P("shots"), P(), P())
    return jax.shard_map(
        local, mesh=mesh, in_specs=placed, out_specs=P("shots", "depth", None), check_vma=False
    )
```

```python
import math

import jax
import jax.numpy as jnp
from jax import lax
from jax.experimental import pallas as pl
from jax.experimental.pallas import tpu as pltpu
from jax.sharding import PartitionSpec as P

STEPS = 16
HALO = 6
PLANES = 8
DEEP = PLANES + 2 * HALO
ITERS = 3
RATE = 0.15
TINY = 1e-6
TILES = 32
GROUP = 2
PITCH = STEPS * 8 + 8


def lanes():
    return lax.broadcasted_iota(jnp.int32, (8, 128), 1)


def rows():
    return lax.broadcasted_iota(jnp.int32, (8, 128), 0)


def coefficients(classes):
    tilt = 0.2 + 0.1 * (classes & 3).astype(jnp.float32)
    azimuth = 0.3 + math.pi / 2.0 * (classes >> 2).astype(jnp.float32)
    norm_z = jnp.cos(tilt)
    norm_x = jnp.sin(tilt) * jnp.cos(azimuth)
    norm_y = jnp.sin(tilt) * jnp.sin(azimuth)
    c_zz = RATE * (1.0 - norm_z * norm_z)
    c_xx = RATE * (1.0 - norm_x * norm_x)
    c_yy = RATE * (1.0 - norm_y * norm_y)
    cross = -0.5 * RATE
    return [
        norm_z,
        norm_x,
        norm_y,
        -2.0 * (c_zz + c_xx + 2.0 * c_yy),
        c_zz,
        c_xx,
        c_yy,
        cross * norm_z * norm_x,
        cross * norm_z * norm_y,
        cross * norm_x * norm_y,
    ]


def pack_kernel(
    aperture_hbm, owner_map_hbm, dip_class_hbm, partials, out, coefs, aperture, owner_map, dip_class, owned,
    blocks, places, table_sems, in_sems, out_sems, place_sem
):
    slots = partials.shape[0]
    columns = partials.shape[2]
    tables = [
        pltpu.make_async_copy(aperture_hbm, aperture, table_sems.at[0]),
        pltpu.make_async_copy(owner_map_hbm, owner_map, table_sems.at[1]),
        pltpu.make_async_copy(dip_class_hbm, dip_class, table_sems.at[2]),
    ]
    for copy in tables:
        copy.start()
    fetches = [pltpu.make_async_copy(partials.at[slot], blocks.at[slot], in_sems.at[slot]) for slot in range(slots)]
    for fetch in fetches:
        fetch.start()
    for owner in range(places.shape[0]):
        places[owner] = jnp.full((8, 128), -1.0, jnp.float32)
    for copy in tables:
        copy.wait()

    def block(slot, owner):
        return pltpu.make_async_copy(blocks.at[slot], out.at[owner, :, 0:columns], out_sems.at[slot])

    base = lax.axis_index("shots") * 4
    for place in range(4):
        owned[place] = 0

    @pl.loop(0, owner_map.shape[0] // 8)
    def _(group):
        for k in range(8):
            brick = group * 8 + k
            place = owner_map[brick] - base
            owned[jnp.where(jnp.logical_and(place >= 0, place < 4), place, 4)] = dip_class[brick]

    for slot in range(slots):
        fetches[slot].wait()
        brick = aperture[slot]

        @pl.when(brick >= 0)
        def _():
            row = owner_map[brick]
            owner = row // 4
            block(slot, owner).start()
            places[owner] = jnp.full((8, 128), row % 4, jnp.int32).astype(jnp.float32)

    labels = pltpu.make_async_copy(places, out.at[:, :, columns : columns + 128], place_sem)
    labels.start()

    brick_of_row = rows() // 2
    classes = jnp.full((8, 128), owned[3], jnp.int32)
    for place in range(3):
        classes = jnp.where(brick_of_row == place, owned[place], classes)
    for i, value in enumerate(coefficients(classes)):
        coefs[i] = value

    for slot in range(slots):

        @pl.when(aperture[slot] >= 0)
        def _():
            block(slot, 0).wait()

    labels.wait()


def pack(aperture, owner_map, dip_class, partials, owners):
    slots, planes, columns = partials.shape
    hbm = pl.BlockSpec(memory_space=pltpu.HBM)
    return pl.pallas_call(
        pack_kernel,
        in_specs=[hbm] * 4,
        out_specs=[hbm, pl.BlockSpec(memory_space=pltpu.VMEM)],
        out_shape=[
            jax.ShapeDtypeStruct((owners, planes, columns + 128), jnp.float32),
            jax.ShapeDtypeStruct((10, 8, 128), jnp.float32),
        ],
        scratch_shapes=[
            pltpu.SMEM(aperture.shape, jnp.int32),
            pltpu.SMEM(owner_map.shape, jnp.int32),
            pltpu.SMEM(dip_class.shape, jnp.int32),
            pltpu.SMEM((8,), jnp.int32),
            pltpu.VMEM(partials.shape, jnp.float32),
            pltpu.VMEM((owners, planes, 128), jnp.float32),
            pltpu.SemaphoreType.DMA((3,)),
            pltpu.SemaphoreType.DMA((slots,)),
            pltpu.SemaphoreType.DMA((slots,)),
            pltpu.SemaphoreType.DMA,
        ],
        compiler_params=pltpu.CompilerParams(vmem_limit_bytes=60 << 20),
        name="pack_blocks",
    )(aperture, owner_map, dip_class, partials)


def merge_kernel(received, out, places, sums, spread, place_sem):
    senders = received.shape[0]
    columns = received.shape[2] - 128
    labels = pltpu.make_async_copy(received.at[:, 0:1, columns : columns + 128], places, place_sem)
    labels.start()
    for brick in range(4):
        for tile in range(TILES):
            sums[brick, tile] = jnp.zeros((8, 128), jnp.float32)
    labels.wait()

    @pl.loop(0, senders)
    def _(sender):
        place = places[sender, 0, 0].astype(jnp.int32)

        @pl.when(place >= 0)
        def _():
            for tile in range(TILES):
                sums[place, tile] += received[sender, :, tile * 128 : tile * 128 + 128]

    low = lanes() < 64
    for b in range(4):
        for upper in range(2):
            for k in range(8):
                even = sums[b, upper * 16 + k]
                odd = sums[b, upper * 16 + 8 + k]
                base = k * 16 + b * 2 + upper
                spread[pl.ds(base, 8, stride=PITCH), :] = jnp.where(low, even, pltpu.roll(odd, 64, 1))
                spread[pl.ds(base + 8, 8, stride=PITCH), :] = jnp.where(low, pltpu.roll(even, 64, 1), odd)

    for plane in range(PLANES):
        out[plane * STEPS * 8 : (plane + 1) * STEPS * 8, :] = spread[plane * PITCH : plane * PITCH + STEPS * 8, :]


def merge(received):
    senders = received.shape[0]
    vmem = pl.BlockSpec(memory_space=pltpu.VMEM)
    return pl.pallas_call(
        merge_kernel,
        in_specs=[vmem],
        out_specs=vmem,
        out_shape=jax.ShapeDtypeStruct((PLANES * STEPS * 8, 128), jnp.float32),
        scratch_shapes=[
            pltpu.SMEM((senders, 1, 128), jnp.float32),
            pltpu.VMEM((4, TILES, 8, 128), jnp.float32),
            pltpu.VMEM((PLANES * PITCH, 128), jnp.float32),
            pltpu.SemaphoreType.DMA,
        ],
        compiler_params=pltpu.CompilerParams(vmem_limit_bytes=32 << 20),
        name="merge_blocks",
    )(received)


def left_edge(last):
    turned = pltpu.roll(last, 64, 1)
    below = jnp.where(rows() % 2 == 0, 0.0, pltpu.roll(turned, 1, 0))
    return jnp.where(lanes() < 64, below, turned)


def right_edge(first):
    turned = pltpu.roll(first, 64, 1)
    above = jnp.where(rows() % 2 == 0, pltpu.roll(turned, 7, 0), 0.0)
    return jnp.where(lanes() < 64, turned, above)


def smooth_kernel(coefs, lower, own, upper, out, image, other, blur, slope, along, total, final, bricks, out_sems):
    column = lanes() % 64
    first_y = column == 0
    last_y = column == 63

    def after(f):
        return jnp.where(last_y, 0.0, pltpu.roll(f, 127, 1))

    def before(f):
        return jnp.where(first_y, 0.0, pltpu.roll(f, 1, 1))

    def blur_y(f):
        return (f + after(f)) + (f + before(f))

    zero = jnp.zeros((8, 128), jnp.float32)

    def clear(field, plane):
        for step in range(1, STEPS + 1):
            field[plane, step] = zero

    def load(source, count, offset):
        @pl.loop(0, count // 2)
        def _(pair):
            for plane in (2 * pair, 2 * pair + 1):
                for step in range(STEPS):
                    image[plane + offset, step + 1] = source[plane, step]

    place = lax.axis_index("depth")
    low_end = place == 0
    high_end = place == lax.axis_size("depth") - 1

    def load_or_clear(source, offset, outside):
        @pl.when(jnp.logical_not(outside))
        def _():
            load(source, HALO, offset)

        @pl.when(outside)
        def _():
            for plane in range(HALO):
                clear(image, plane + offset)

    load_or_clear(lower, 0, low_end)
    load(own, PLANES, HALO)
    load_or_clear(upper, HALO + PLANES, high_end)

    def along_y(source, plane, step):
        if step == 0:
            cells = left_edge(source[plane, STEPS])
        elif step == STEPS + 1:
            cells = right_edge(source[plane, 1])
        else:
            cells = source[plane, step]
        if step in (0, STEPS + 1):
            source[plane, step] = cells
        up, down = after(cells), before(cells)
        blur[plane, step] = (cells + cells) + (up + down)
        slope[plane, step] = up - down

    def depth_blur(field, plane, step):
        deep = [field[plane - 1 + k, step] for k in range(GROUP + 2)]
        pairs = [deep[k] + deep[k + 1] for k in range(GROUP + 1)]
        return [pairs[k] + pairs[k + 1] for k in range(GROUP)], deep

    def depth_slope(deep):
        return [deep[k + 2] - deep[k] for k in range(GROUP)]

    def clear_outside(*fields):
        for outside, edge in ((low_end, HALO - 1), (high_end, HALO + PLANES)):

            @pl.when(outside)
            def _():
                for field in fields:
                    clear(field, edge)

    for sweep in range(ITERS):
        source = image if sweep % 2 == 0 else other
        target = other if sweep % 2 == 0 else image
        margin = 2 * sweep + 1
        start, stop = margin, DEEP - margin

        for k in range(GROUP + 1):
            for step in range(STEPS + 2):
                along_y(source, start - 1 + k, step)

        @pl.loop(0, (stop - start) // GROUP)
        def _(group):
            plane = start + group * GROUP
            norm_z, norm_x, norm_y = coefs[0], coefs[1], coefs[2]

            flat, steep, wide = {}, {}, {}

            def prepare(step):
                for k in range(GROUP):
                    along_y(source, plane + GROUP + k, step)
                flat[step], deep = depth_blur(blur, plane, step)
                steep[step] = depth_slope(deep)
                wide[step], _ = depth_blur(slope, plane, step)

            prepare(0)
            prepare(1)
            steep_pair = [steep[0][k] + steep[1][k] for k in range(GROUP)]
            wide_pair = [wide[0][k] + wide[1][k] for k in range(GROUP)]
            for step in range(1, STEPS + 1):
                prepare(step + 1)
                for k in range(GROUP):
                    steep_next = steep[step][k] + steep[step + 1][k]
                    wide_next = wide[step][k] + wide[step + 1][k]
                    grad_z = steep_pair[k] + steep_next
                    grad_x = flat[step + 1][k] - flat[step - 1][k]
                    grad_y = wide_pair[k] + wide_next
                    steep_pair[k], wide_pair[k] = steep_next, wide_next
                    aligned = norm_z * grad_z + norm_x * grad_x + norm_y * grad_y
                    aligned = aligned * aligned
                    whole = grad_z * grad_z + grad_x * grad_x + grad_y * grad_y
                    along[plane + k, step] = aligned
                    total[plane + k, step] = whole

        clear_outside(along, total)

        margin += 1
        begin, finish = margin, DEEP - margin

        @pl.loop(0, (finish - begin) // GROUP)
        def _(group):
            plane = begin + group * GROUP
            c_mid, c_zz, c_xx, c_yy, c_zx, c_zy, c_xy = [coefs[3 + i] for i in range(7)]
            a_cells, t_cells, deep, tilted = {}, {}, {}, {}

            def prepare(step):
                for field, cells in ((along, a_cells), (total, t_cells)):
                    if step == 0:
                        cells[0] = [left_edge(f) for f in depth_blur(field, plane, STEPS)[0]]
                        cells[STEPS + 1] = [right_edge(f) for f in depth_blur(field, plane, 1)[0]]
                    elif step <= STEPS:
                        cells[step], _ = depth_blur(field, plane, step)
                deep[step] = [source[plane - 1 + k, step] for k in range(GROUP + 2)]
                steep = depth_slope(deep[step])
                tilted[step] = [c_zx * steep[k] + c_xy * slope[plane + k, step] for k in range(GROUP)]

            prepare(0)
            prepare(1)
            a_pair = [a_cells[0][k] + a_cells[1][k] for k in range(GROUP)]
            t_pair = [t_cells[0][k] + t_cells[1][k] for k in range(GROUP)]
            for step in range(1, STEPS + 1):
                prepare(step + 1)
                lean = depth_slope([slope[plane - 1 + k, step] for k in range(GROUP + 2)])
                for k in range(GROUP):
                    a_new = a_cells[step][k] + a_cells[step + 1][k]
                    t_new = t_cells[step][k] + t_cells[step + 1][k]
                    aligned = blur_y(a_pair[k] + a_new)
                    whole = blur_y(t_pair[k] + t_new)
                    a_pair[k], t_pair[k] = a_new, t_new
                    weight = aligned / (whole + jnp.float32(TINY * 65536.0))
                    now = deep[step][k + 1]
                    change = (
                        (c_mid * now + c_zz * (deep[step][k] + deep[step][k + 2]))
                        + (c_xx * (deep[step - 1][k + 1] + deep[step + 1][k + 1]) + c_yy * blur[plane + k, step])
                        + ((tilted[step + 1][k] - tilted[step - 1][k]) + c_zy * lean[k])
                    )
                    new = now + weight * change
                    if sweep < ITERS - 1:
                        target[plane + k, step] = new
                    else:
                        base = pl.multiple_of((plane + k - HALO) * PITCH, 8) + (step - 1) * 8
                        final[pl.ds(base, 8), :] = new

        if sweep < ITERS - 1:
            clear_outside(target)

    low_half = lanes() < 64
    copies = [pltpu.make_async_copy(bricks.at[b], out.at[b], out_sems.at[b]) for b in range(4)]
    for b in range(4):
        for half in range(2):
            for k in range(8):
                base = k * 16 + b * 2 + half
                first = final[pl.ds(base, 8, stride=PITCH), :]
                second = final[pl.ds(base + 8, 8, stride=PITCH), :]
                tile = half * 16 + k
                bricks[b, :, tile * 128 : tile * 128 + 128] = jnp.where(low_half, first, pltpu.roll(second, 64, 1))
                tile += 8
                bricks[b, :, tile * 128 : tile * 128 + 128] = jnp.where(low_half, pltpu.roll(first, 64, 1), second)
        copies[b].start()
    for copy in copies:
        copy.wait()


def smooth(coefs, lower, own, upper, interpret=False):
    field = pltpu.VMEM((DEEP + GROUP, STEPS + 2, 8, 128), jnp.float32)
    vmem = pl.BlockSpec(memory_space=pltpu.VMEM)
    return pl.pallas_call(
        smooth_kernel,
        in_specs=[vmem] * 4,
        out_specs=pl.BlockSpec(memory_space=pltpu.HBM),
        out_shape=jax.ShapeDtypeStruct((4, PLANES, STEPS * 256), jnp.float32),
        scratch_shapes=[field] * 6
        + [
            pltpu.VMEM((PLANES * PITCH, 128), jnp.float32),
            pltpu.VMEM((4, PLANES, STEPS * 256), jnp.float32),
            pltpu.SemaphoreType.DMA((4,)),
        ],
        compiler_params=pltpu.CompilerParams(vmem_limit_bytes=32 << 20),
        name="smooth_image",
        interpret=interpret,
    )(coefs, lower, own, upper)


def local(partials, aperture, owner_map, dip_class):
    sent, coefs = pack(aperture, owner_map, dip_class, partials, lax.axis_size("shots"))
    received = lax.all_to_all(sent, "shots", 0, 0, tiled=True)
    image = merge(received).reshape(PLANES, STEPS, 8, 128)
    depth_count = lax.axis_size("depth")
    lower = lax.ppermute(image[PLANES - HALO :], "depth", [(i, (i + 1) % depth_count) for i in range(depth_count)])
    upper = lax.ppermute(image[:HALO], "depth", [((i + 1) % depth_count, i) for i in range(depth_count)])
    return smooth(coefs, lower, image, upper)


def solution(mesh):
    placed = (P("shots", "depth", None), P("shots"), P(), P())
    return jax.shard_map(
        local, mesh=mesh, in_specs=placed, out_specs=P("shots", "depth", None), check_vma=False
    )
```

```python
import math

import jax
import jax.numpy as jnp
from jax import lax
from jax.experimental import pallas as pl
from jax.experimental.pallas import tpu as pltpu
from jax.sharding import PartitionSpec as P

STEPS = 16
HALO = 6
PLANES = 8
DEEP = PLANES + 2 * HALO
ITERS = 3
RATE = 0.15
TINY = 1e-6
TILES = 32
GROUP = 2
PITCH = STEPS * 8 + 8


def lanes():
    return lax.broadcasted_iota(jnp.int32, (8, 128), 1)


def rows():
    return lax.broadcasted_iota(jnp.int32, (8, 128), 0)


def coefficients(classes):
    tilts = [0.2 + 0.1 * i for i in range(4)]
    azimuths = [0.3 + math.pi / 2.0 * i for i in range(2)]

    def pick(index, values):
        chosen = jnp.full(index.shape, values[-1], jnp.float32)
        for i, value in enumerate(values[:-1]):
            chosen = jnp.where(index == i, jnp.float32(value), chosen)
        return chosen

    tilt, azimuth = classes & 3, classes >> 2
    lean = pick(tilt, [math.sin(angle) for angle in tilts])
    norm_z = pick(tilt, [math.cos(angle) for angle in tilts])
    norm_x = lean * pick(azimuth, [math.cos(angle) for angle in azimuths])
    norm_y = lean * pick(azimuth, [math.sin(angle) for angle in azimuths])
    c_zz = RATE * (1.0 - norm_z * norm_z)
    c_xx = RATE * (1.0 - norm_x * norm_x)
    c_yy = RATE * (1.0 - norm_y * norm_y)
    cross = -0.5 * RATE
    return [
        norm_z,
        norm_x,
        norm_y,
        -2.0 * (c_zz + c_xx + 2.0 * c_yy),
        c_zz,
        c_xx,
        c_yy,
        cross * norm_z * norm_x,
        cross * norm_z * norm_y,
        cross * norm_x * norm_y,
    ]


def pack_kernel(
    aperture_hbm, owner_map_hbm, dip_class_hbm, partials, out, coefs, aperture, owner_map, dip_class, owned,
    blocks, places, table_sems, in_sems, out_sems, place_sem
):
    slots = partials.shape[0]
    columns = partials.shape[2]
    tables = [
        pltpu.make_async_copy(aperture_hbm, aperture, table_sems.at[0]),
        pltpu.make_async_copy(owner_map_hbm, owner_map, table_sems.at[1]),
        pltpu.make_async_copy(dip_class_hbm, dip_class, table_sems.at[2]),
    ]
    for copy in tables:
        copy.start()
    fetches = [pltpu.make_async_copy(partials.at[slot], blocks.at[slot], in_sems.at[slot]) for slot in range(slots)]
    for fetch in fetches:
        fetch.start()
    for owner in range(places.shape[0]):
        places[owner] = jnp.full((8, 128), -1.0, jnp.float32)
    for copy in tables:
        copy.wait()

    def block(slot, owner):
        return pltpu.make_async_copy(blocks.at[slot], out.at[owner, :, 0:columns], out_sems.at[slot])

    base = lax.axis_index("shots") * 4
    for place in range(4):
        owned[place] = 0

    @pl.loop(0, owner_map.shape[0] // 8)
    def _(group):
        for k in range(8):
            brick = group * 8 + k
            place = owner_map[brick] - base
            owned[jnp.where(jnp.logical_and(place >= 0, place < 4), place, 4)] = dip_class[brick]

    for slot in range(slots):
        fetches[slot].wait()
        brick = aperture[slot]

        @pl.when(brick >= 0)
        def _():
            row = owner_map[brick]
            owner = row // 4
            block(slot, owner).start()
            places[owner] = jnp.full((8, 128), row % 4, jnp.int32).astype(jnp.float32)

    labels = pltpu.make_async_copy(places, out.at[:, :, columns : columns + 128], place_sem)
    labels.start()

    brick_of_row = rows() // 2
    classes = jnp.full((8, 128), owned[3], jnp.int32)
    for place in range(3):
        classes = jnp.where(brick_of_row == place, owned[place], classes)
    for i, value in enumerate(coefficients(classes)):
        coefs[i] = value

    for slot in range(slots):

        @pl.when(aperture[slot] >= 0)
        def _():
            block(slot, 0).wait()

    labels.wait()


def pack(aperture, owner_map, dip_class, partials, owners):
    slots, planes, columns = partials.shape
    hbm = pl.BlockSpec(memory_space=pltpu.HBM)
    return pl.pallas_call(
        pack_kernel,
        in_specs=[hbm] * 4,
        out_specs=[hbm, pl.BlockSpec(memory_space=pltpu.VMEM)],
        out_shape=[
            jax.ShapeDtypeStruct((owners, planes, columns + 128), jnp.float32),
            jax.ShapeDtypeStruct((10, 8, 128), jnp.float32),
        ],
        scratch_shapes=[
            pltpu.SMEM(aperture.shape, jnp.int32),
            pltpu.SMEM(owner_map.shape, jnp.int32),
            pltpu.SMEM(dip_class.shape, jnp.int32),
            pltpu.SMEM((8,), jnp.int32),
            pltpu.VMEM(partials.shape, jnp.float32),
            pltpu.VMEM((owners, planes, 128), jnp.float32),
            pltpu.SemaphoreType.DMA((3,)),
            pltpu.SemaphoreType.DMA((slots,)),
            pltpu.SemaphoreType.DMA((slots,)),
            pltpu.SemaphoreType.DMA,
        ],
        compiler_params=pltpu.CompilerParams(vmem_limit_bytes=60 << 20),
        name="pack_blocks",
    )(aperture, owner_map, dip_class, partials)


def merge_kernel(received, out, places, sums, spread, place_sem):
    senders = received.shape[0]
    columns = received.shape[2] - 128
    labels = pltpu.make_async_copy(received.at[:, 0:1, columns : columns + 128], places, place_sem)
    labels.start()
    for brick in range(4):
        for tile in range(TILES):
            sums[brick, tile] = jnp.zeros((8, 128), jnp.float32)
    labels.wait()

    @pl.loop(0, senders)
    def _(sender):
        place = places[sender, 0, 0].astype(jnp.int32)

        @pl.when(place >= 0)
        def _():
            for tile in range(TILES):
                sums[place, tile] += received[sender, :, tile * 128 : tile * 128 + 128]

    low = lanes() < 64
    for b in range(4):
        for upper in range(2):
            for k in range(8):
                even = sums[b, upper * 16 + k]
                odd = sums[b, upper * 16 + 8 + k]
                base = k * 16 + b * 2 + upper
                spread[pl.ds(base, 8, stride=PITCH), :] = jnp.where(low, even, pltpu.roll(odd, 64, 1))
                spread[pl.ds(base + 8, 8, stride=PITCH), :] = jnp.where(low, pltpu.roll(even, 64, 1), odd)

    for plane in range(PLANES):
        out[plane * STEPS * 8 : (plane + 1) * STEPS * 8, :] = spread[plane * PITCH : plane * PITCH + STEPS * 8, :]


def merge(received):
    senders = received.shape[0]
    vmem = pl.BlockSpec(memory_space=pltpu.VMEM)
    return pl.pallas_call(
        merge_kernel,
        in_specs=[vmem],
        out_specs=vmem,
        out_shape=jax.ShapeDtypeStruct((PLANES * STEPS * 8, 128), jnp.float32),
        scratch_shapes=[
            pltpu.SMEM((senders, 1, 128), jnp.float32),
            pltpu.VMEM((4, TILES, 8, 128), jnp.float32),
            pltpu.VMEM((PLANES * PITCH, 128), jnp.float32),
            pltpu.SemaphoreType.DMA,
        ],
        compiler_params=pltpu.CompilerParams(vmem_limit_bytes=32 << 20),
        name="merge_blocks",
    )(received)


def left_edge(last):
    turned = pltpu.roll(last, 64, 1)
    below = jnp.where(rows() % 2 == 0, 0.0, pltpu.roll(turned, 1, 0))
    return jnp.where(lanes() < 64, below, turned)


def right_edge(first):
    turned = pltpu.roll(first, 64, 1)
    above = jnp.where(rows() % 2 == 0, pltpu.roll(turned, 7, 0), 0.0)
    return jnp.where(lanes() < 64, turned, above)


def smooth_kernel(coefs, lower, own, upper, out, image, other, blur, slope, along, total, final, bricks, out_sems):
    column = lanes() % 64
    first_y = column == 0
    last_y = column == 63

    def after(f):
        return jnp.where(last_y, 0.0, pltpu.roll(f, 127, 1))

    def before(f):
        return jnp.where(first_y, 0.0, pltpu.roll(f, 1, 1))

    def blur_y(f):
        return (f + after(f)) + (f + before(f))

    zero = jnp.zeros((8, 128), jnp.float32)

    def clear(field, plane):
        for step in range(1, STEPS + 1):
            field[plane, step] = zero

    def load(source, count, offset):
        @pl.loop(0, count // 2)
        def _(pair):
            for plane in (2 * pair, 2 * pair + 1):
                for step in range(STEPS):
                    image[plane + offset, step + 1] = source[plane, step]

    place = lax.axis_index("depth")
    low_end = place == 0
    high_end = place == lax.axis_size("depth") - 1

    def load_or_clear(source, offset, outside):
        @pl.when(jnp.logical_not(outside))
        def _():
            load(source, HALO, offset)

        @pl.when(outside)
        def _():
            for plane in range(HALO):
                clear(image, plane + offset)

    load_or_clear(lower, 0, low_end)
    load(own, PLANES, HALO)
    load_or_clear(upper, HALO + PLANES, high_end)

    def along_y(source, plane, step):
        if step == 0:
            cells = left_edge(source[plane, STEPS])
        elif step == STEPS + 1:
            cells = right_edge(source[plane, 1])
        else:
            cells = source[plane, step]
        if step in (0, STEPS + 1):
            source[plane, step] = cells
        up, down = after(cells), before(cells)
        blur[plane, step] = (cells + cells) + (up + down)
        slope[plane, step] = up - down

    def depth_blur(field, plane, step):
        deep = [field[plane - 1 + k, step] for k in range(GROUP + 2)]
        pairs = [deep[k] + deep[k + 1] for k in range(GROUP + 1)]
        return [pairs[k] + pairs[k + 1] for k in range(GROUP)], deep

    def depth_slope(deep):
        return [deep[k + 2] - deep[k] for k in range(GROUP)]

    def clear_outside(*fields):
        for outside, edge in ((low_end, HALO - 1), (high_end, HALO + PLANES)):

            @pl.when(outside)
            def _():
                for field in fields:
                    clear(field, edge)

    for sweep in range(ITERS):
        source = image if sweep % 2 == 0 else other
        target = other if sweep % 2 == 0 else image
        margin = 2 * sweep + 1
        start, stop = margin, DEEP - margin

        for k in range(GROUP + 1):
            for step in range(STEPS + 2):
                along_y(source, start - 1 + k, step)

        @pl.loop(0, (stop - start) // GROUP)
        def _(group):
            plane = start + group * GROUP
            norm_z, norm_x, norm_y = coefs[0], coefs[1], coefs[2]

            flat, steep, wide = {}, {}, {}

            def prepare(step):
                for k in range(GROUP):
                    along_y(source, plane + GROUP + k, step)
                flat[step], deep = depth_blur(blur, plane, step)
                steep[step] = depth_slope(deep)
                wide[step], _ = depth_blur(slope, plane, step)

            prepare(0)
            prepare(1)
            steep_pair = [steep[0][k] + steep[1][k] for k in range(GROUP)]
            wide_pair = [wide[0][k] + wide[1][k] for k in range(GROUP)]
            for step in range(1, STEPS + 1):
                prepare(step + 1)
                for k in range(GROUP):
                    steep_next = steep[step][k] + steep[step + 1][k]
                    wide_next = wide[step][k] + wide[step + 1][k]
                    grad_z = steep_pair[k] + steep_next
                    grad_x = flat[step + 1][k] - flat[step - 1][k]
                    grad_y = wide_pair[k] + wide_next
                    steep_pair[k], wide_pair[k] = steep_next, wide_next
                    aligned = norm_z * grad_z + norm_x * grad_x + norm_y * grad_y
                    aligned = aligned * aligned
                    whole = grad_z * grad_z + grad_x * grad_x + grad_y * grad_y
                    along[plane + k, step] = aligned
                    total[plane + k, step] = whole

        clear_outside(along, total)

        margin += 1
        begin, finish = margin, DEEP - margin

        @pl.loop(0, (finish - begin) // GROUP)
        def _(group):
            plane = begin + group * GROUP
            c_mid, c_zz, c_xx, c_yy, c_zx, c_zy, c_xy = [coefs[3 + i] for i in range(7)]
            a_cells, t_cells, deep, tilted = {}, {}, {}, {}

            def prepare(step):
                for field, cells in ((along, a_cells), (total, t_cells)):
                    if step == 0:
                        cells[0] = [left_edge(f) for f in depth_blur(field, plane, STEPS)[0]]
                        cells[STEPS + 1] = [right_edge(f) for f in depth_blur(field, plane, 1)[0]]
                    elif step <= STEPS:
                        cells[step], _ = depth_blur(field, plane, step)
                deep[step] = [source[plane - 1 + k, step] for k in range(GROUP + 2)]
                steep = depth_slope(deep[step])
                tilted[step] = [c_zx * steep[k] + c_xy * slope[plane + k, step] for k in range(GROUP)]

            prepare(0)
            prepare(1)
            a_pair = [a_cells[0][k] + a_cells[1][k] for k in range(GROUP)]
            t_pair = [t_cells[0][k] + t_cells[1][k] for k in range(GROUP)]
            for step in range(1, STEPS + 1):
                prepare(step + 1)
                lean = depth_slope([slope[plane - 1 + k, step] for k in range(GROUP + 2)])
                for k in range(GROUP):
                    a_new = a_cells[step][k] + a_cells[step + 1][k]
                    t_new = t_cells[step][k] + t_cells[step + 1][k]
                    aligned = blur_y(a_pair[k] + a_new)
                    whole = blur_y(t_pair[k] + t_new)
                    a_pair[k], t_pair[k] = a_new, t_new
                    weight = aligned / (whole + jnp.float32(TINY * 65536.0))
                    now = deep[step][k + 1]
                    change = (
                        (c_mid * now + c_zz * (deep[step][k] + deep[step][k + 2]))
                        + (c_xx * (deep[step - 1][k + 1] + deep[step + 1][k + 1]) + c_yy * blur[plane + k, step])
                        + ((tilted[step + 1][k] - tilted[step - 1][k]) + c_zy * lean[k])
                    )
                    new = now + weight * change
                    if sweep < ITERS - 1:
                        target[plane + k, step] = new
                    else:
                        base = pl.multiple_of((plane + k - HALO) * PITCH, 8) + (step - 1) * 8
                        final[pl.ds(base, 8), :] = new

        if sweep < ITERS - 1:
            clear_outside(target)

    low_half = lanes() < 64
    copies = [pltpu.make_async_copy(bricks.at[b], out.at[b], out_sems.at[b]) for b in range(4)]
    for b in range(4):
        for half in range(2):
            for k in range(8):
                base = k * 16 + b * 2 + half
                first = final[pl.ds(base, 8, stride=PITCH), :]
                second = final[pl.ds(base + 8, 8, stride=PITCH), :]
                tile = half * 16 + k
                bricks[b, :, tile * 128 : tile * 128 + 128] = jnp.where(low_half, first, pltpu.roll(second, 64, 1))
                tile += 8
                bricks[b, :, tile * 128 : tile * 128 + 128] = jnp.where(low_half, pltpu.roll(first, 64, 1), second)
        copies[b].start()
    for copy in copies:
        copy.wait()


def smooth(coefs, lower, own, upper, interpret=False):
    field = pltpu.VMEM((DEEP + GROUP, STEPS + 2, 8, 128), jnp.float32)
    vmem = pl.BlockSpec(memory_space=pltpu.VMEM)
    return pl.pallas_call(
        smooth_kernel,
        in_specs=[vmem] * 4,
        out_specs=pl.BlockSpec(memory_space=pltpu.HBM),
        out_shape=jax.ShapeDtypeStruct((4, PLANES, STEPS * 256), jnp.float32),
        scratch_shapes=[field] * 6
        + [
            pltpu.VMEM((PLANES * PITCH, 128), jnp.float32),
            pltpu.VMEM((4, PLANES, STEPS * 256), jnp.float32),
            pltpu.SemaphoreType.DMA((4,)),
        ],
        compiler_params=pltpu.CompilerParams(vmem_limit_bytes=32 << 20),
        name="smooth_image",
        interpret=interpret,
    )(coefs, lower, own, upper)


def local(partials, aperture, owner_map, dip_class):
    sent, coefs = pack(aperture, owner_map, dip_class, partials, lax.axis_size("shots"))
    received = lax.all_to_all(sent, "shots", 0, 0, tiled=True)
    image = merge(received).reshape(PLANES, STEPS, 8, 128)
    depth_count = lax.axis_size("depth")
    lower = lax.ppermute(image[PLANES - HALO :], "depth", [(i, (i + 1) % depth_count) for i in range(depth_count)])
    upper = lax.ppermute(image[:HALO], "depth", [((i + 1) % depth_count, i) for i in range(depth_count)])
    return smooth(coefs, lower, image, upper)


def solution(mesh):
    placed = (P("shots", "depth", None), P("shots"), P(), P())
    return jax.shard_map(
        local, mesh=mesh, in_specs=placed, out_specs=P("shots", "depth", None), check_vma=False
    )
```

```python
import math

import jax
import jax.numpy as jnp
from jax import lax
from jax.experimental import pallas as pl
from jax.experimental.pallas import tpu as pltpu
from jax.sharding import PartitionSpec as P

STEPS = 16
HALO = 6
PLANES = 8
DEEP = PLANES + 2 * HALO
ITERS = 3
RATE = 0.15
TINY = 1e-6
TILES = 32
GROUP = 2
PITCH = STEPS * 8 + 8


def lanes():
    return lax.broadcasted_iota(jnp.int32, (8, 128), 1)


def rows():
    return lax.broadcasted_iota(jnp.int32, (8, 128), 0)


def coefficients(classes):
    tilt = 0.2 + 0.1 * (classes & 3).astype(jnp.float32)
    azimuth = 0.3 + math.pi / 2.0 * (classes >> 2).astype(jnp.float32)
    norm_z = jnp.cos(tilt)
    norm_x = jnp.sin(tilt) * jnp.cos(azimuth)
    norm_y = jnp.sin(tilt) * jnp.sin(azimuth)
    c_zz = RATE * (1.0 - norm_z * norm_z)
    c_xx = RATE * (1.0 - norm_x * norm_x)
    c_yy = RATE * (1.0 - norm_y * norm_y)
    cross = -0.5 * RATE
    return [
        norm_z,
        norm_x,
        norm_y,
        -2.0 * (c_zz + c_xx + 2.0 * c_yy),
        c_zz,
        c_xx,
        c_yy,
        cross * norm_z * norm_x,
        cross * norm_z * norm_y,
        cross * norm_x * norm_y,
    ]


def pack_kernel(
    aperture_hbm, owner_map_hbm, partials, out, aperture, owner_map,
    blocks, places, table_sems, in_sems, out_sems, place_sem
):
    slots = partials.shape[0]
    columns = partials.shape[2]
    tables = [
        pltpu.make_async_copy(aperture_hbm, aperture, table_sems.at[0]),
        pltpu.make_async_copy(owner_map_hbm, owner_map, table_sems.at[1]),
    ]
    for copy in tables:
        copy.start()
    fetches = [pltpu.make_async_copy(partials.at[slot], blocks.at[slot], in_sems.at[slot]) for slot in range(slots)]
    for fetch in fetches:
        fetch.start()
    for owner in range(places.shape[0]):
        places[owner] = jnp.full((8, 128), -1.0, jnp.float32)
    for copy in tables:
        copy.wait()

    def block(slot, owner):
        return pltpu.make_async_copy(blocks.at[slot], out.at[owner, :, 0:columns], out_sems.at[slot])

    for slot in range(slots):
        fetches[slot].wait()
        brick = aperture[slot]

        @pl.when(brick >= 0)
        def _():
            row = owner_map[brick]
            owner = row // 4
            block(slot, owner).start()
            places[owner] = jnp.full((8, 128), row % 4, jnp.int32).astype(jnp.float32)

    labels = pltpu.make_async_copy(places, out.at[:, :, columns : columns + 128], place_sem)
    labels.start()

    for slot in range(slots):

        @pl.when(aperture[slot] >= 0)
        def _():
            block(slot, 0).wait()

    labels.wait()


def pack(aperture, owner_map, partials, owners):
    slots, planes, columns = partials.shape
    hbm = pl.BlockSpec(memory_space=pltpu.HBM)
    return pl.pallas_call(
        pack_kernel,
        in_specs=[hbm] * 3,
        out_specs=hbm,
        out_shape=jax.ShapeDtypeStruct((owners, planes, columns + 128), jnp.float32),
        scratch_shapes=[
            pltpu.SMEM(aperture.shape, jnp.int32),
            pltpu.SMEM(owner_map.shape, jnp.int32),
            pltpu.VMEM(partials.shape, jnp.float32),
            pltpu.VMEM((owners, planes, 128), jnp.float32),
            pltpu.SemaphoreType.DMA((2,)),
            pltpu.SemaphoreType.DMA((slots,)),
            pltpu.SemaphoreType.DMA((slots,)),
            pltpu.SemaphoreType.DMA,
        ],
        compiler_params=pltpu.CompilerParams(vmem_limit_bytes=60 << 20),
        name="pack_blocks",
    )(aperture, owner_map, partials)


def factors_kernel(owner_map_hbm, dip_class_hbm, merged, coefs, owner_map, dip_class, owned, table_sems):
    tables = [
        pltpu.make_async_copy(owner_map_hbm, owner_map, table_sems.at[0]),
        pltpu.make_async_copy(dip_class_hbm, dip_class, table_sems.at[1]),
    ]
    for copy in tables:
        copy.start()
    for copy in tables:
        copy.wait()
    base = lax.axis_index("shots") * 4
    for place in range(4):
        owned[place] = 0

    @pl.loop(0, owner_map.shape[0] // 8)
    def _(group):
        for k in range(8):
            brick = group * 8 + k
            place = owner_map[brick] - base
            owned[jnp.where(jnp.logical_and(place >= 0, place < 4), place, 4)] = dip_class[brick]

    brick_of_row = rows() // 2
    classes = jnp.full((8, 128), owned[3], jnp.int32)
    for place in range(3):
        classes = jnp.where(brick_of_row == place, owned[place], classes)
    for i, value in enumerate(coefficients(classes)):
        coefs[i] = value


def factors(owner_map, dip_class, merged):
    hbm = pl.BlockSpec(memory_space=pltpu.HBM)
    vmem = pl.BlockSpec(memory_space=pltpu.VMEM)
    return pl.pallas_call(
        factors_kernel,
        in_specs=[hbm, hbm, vmem],
        out_specs=vmem,
        out_shape=jax.ShapeDtypeStruct((10, 8, 128), jnp.float32),
        scratch_shapes=[
            pltpu.SMEM(owner_map.shape, jnp.int32),
            pltpu.SMEM(dip_class.shape, jnp.int32),
            pltpu.SMEM((8,), jnp.int32),
            pltpu.SemaphoreType.DMA((2,)),
        ],
        compiler_params=pltpu.CompilerParams(vmem_limit_bytes=56 << 20),
        name="update_factors",
    )(owner_map, dip_class, merged)


def merge_kernel(received, out, places, sums, spread, place_sem):
    senders = received.shape[0]
    columns = received.shape[2] - 128
    labels = pltpu.make_async_copy(received.at[:, 0:1, columns : columns + 128], places, place_sem)
    labels.start()
    for brick in range(4):
        for tile in range(TILES):
            sums[brick, tile] = jnp.zeros((8, 128), jnp.float32)
    labels.wait()

    @pl.loop(0, senders)
    def _(sender):
        place = places[sender, 0, 0].astype(jnp.int32)

        @pl.when(place >= 0)
        def _():
            for tile in range(TILES):
                sums[place, tile] += received[sender, :, tile * 128 : tile * 128 + 128]

    low = lanes() < 64
    for b in range(4):
        for upper in range(2):
            for k in range(8):
                even = sums[b, upper * 16 + k]
                odd = sums[b, upper * 16 + 8 + k]
                base = k * 16 + b * 2 + upper
                spread[pl.ds(base, 8, stride=PITCH), :] = jnp.where(low, even, pltpu.roll(odd, 64, 1))
                spread[pl.ds(base + 8, 8, stride=PITCH), :] = jnp.where(low, pltpu.roll(even, 64, 1), odd)

    for plane in range(PLANES):
        out[plane * STEPS * 8 : (plane + 1) * STEPS * 8, :] = spread[plane * PITCH : plane * PITCH + STEPS * 8, :]


def merge(received):
    senders = received.shape[0]
    vmem = pl.BlockSpec(memory_space=pltpu.VMEM)
    return pl.pallas_call(
        merge_kernel,
        in_specs=[vmem],
        out_specs=vmem,
        out_shape=jax.ShapeDtypeStruct((PLANES * STEPS * 8, 128), jnp.float32),
        scratch_shapes=[
            pltpu.SMEM((senders, 1, 128), jnp.float32),
            pltpu.VMEM((4, TILES, 8, 128), jnp.float32),
            pltpu.VMEM((PLANES * PITCH, 128), jnp.float32),
            pltpu.SemaphoreType.DMA,
        ],
        compiler_params=pltpu.CompilerParams(vmem_limit_bytes=32 << 20),
        name="merge_blocks",
    )(received)


def left_edge(last):
    turned = pltpu.roll(last, 64, 1)
    below = jnp.where(rows() % 2 == 0, 0.0, pltpu.roll(turned, 1, 0))
    return jnp.where(lanes() < 64, below, turned)


def right_edge(first):
    turned = pltpu.roll(first, 64, 1)
    above = jnp.where(rows() % 2 == 0, pltpu.roll(turned, 7, 0), 0.0)
    return jnp.where(lanes() < 64, turned, above)


def smooth_kernel(coefs, lower, own, upper, out, image, other, blur, slope, along, total, final, bricks, out_sems):
    column = lanes() % 64
    first_y = column == 0
    last_y = column == 63

    def after(f):
        return jnp.where(last_y, 0.0, pltpu.roll(f, 127, 1))

    def before(f):
        return jnp.where(first_y, 0.0, pltpu.roll(f, 1, 1))

    def blur_y(f):
        return (f + after(f)) + (f + before(f))

    zero = jnp.zeros((8, 128), jnp.float32)

    def clear(field, plane):
        for step in range(1, STEPS + 1):
            field[plane, step] = zero

    def load(source, count, offset):
        @pl.loop(0, count // 2)
        def _(pair):
            for plane in (2 * pair, 2 * pair + 1):
                for step in range(STEPS):
                    image[plane + offset, step + 1] = source[plane, step]

    place = lax.axis_index("depth")
    low_end = place == 0
    high_end = place == lax.axis_size("depth") - 1

    def load_or_clear(source, offset, outside):
        @pl.when(jnp.logical_not(outside))
        def _():
            load(source, HALO, offset)

        @pl.when(outside)
        def _():
            for plane in range(HALO):
                clear(image, plane + offset)

    load_or_clear(lower, 0, low_end)
    load(own, PLANES, HALO)
    load_or_clear(upper, HALO + PLANES, high_end)

    def along_y(source, plane, step):
        if step == 0:
            cells = left_edge(source[plane, STEPS])
        elif step == STEPS + 1:
            cells = right_edge(source[plane, 1])
        else:
            cells = source[plane, step]
        if step in (0, STEPS + 1):
            source[plane, step] = cells
        up, down = after(cells), before(cells)
        blur[plane, step] = (cells + cells) + (up + down)
        slope[plane, step] = up - down

    def depth_blur(field, plane, step):
        deep = [field[plane - 1 + k, step] for k in range(GROUP + 2)]
        pairs = [deep[k] + deep[k + 1] for k in range(GROUP + 1)]
        return [pairs[k] + pairs[k + 1] for k in range(GROUP)], deep

    def depth_slope(deep):
        return [deep[k + 2] - deep[k] for k in range(GROUP)]

    def clear_outside(*fields):
        for outside, edge in ((low_end, HALO - 1), (high_end, HALO + PLANES)):

            @pl.when(outside)
            def _():
                for field in fields:
                    clear(field, edge)

    for sweep in range(ITERS):
        source = image if sweep % 2 == 0 else other
        target = other if sweep % 2 == 0 else image
        margin = 2 * sweep + 1
        start, stop = margin, DEEP - margin

        for k in range(GROUP + 1):
            for step in range(STEPS + 2):
                along_y(source, start - 1 + k, step)

        @pl.loop(0, (stop - start) // GROUP)
        def _(group):
            plane = start + group * GROUP
            norm_z, norm_x, norm_y = coefs[0], coefs[1], coefs[2]

            flat, steep, wide = {}, {}, {}

            def prepare(step):
                for k in range(GROUP):
                    along_y(source, plane + GROUP + k, step)
                flat[step], deep = depth_blur(blur, plane, step)
                steep[step] = depth_slope(deep)
                wide[step], _ = depth_blur(slope, plane, step)

            prepare(0)
            prepare(1)
            steep_pair = [steep[0][k] + steep[1][k] for k in range(GROUP)]
            wide_pair = [wide[0][k] + wide[1][k] for k in range(GROUP)]
            for step in range(1, STEPS + 1):
                prepare(step + 1)
                for k in range(GROUP):
                    steep_next = steep[step][k] + steep[step + 1][k]
                    wide_next = wide[step][k] + wide[step + 1][k]
                    grad_z = steep_pair[k] + steep_next
                    grad_x = flat[step + 1][k] - flat[step - 1][k]
                    grad_y = wide_pair[k] + wide_next
                    steep_pair[k], wide_pair[k] = steep_next, wide_next
                    aligned = norm_z * grad_z + norm_x * grad_x + norm_y * grad_y
                    aligned = aligned * aligned
                    whole = grad_z * grad_z + grad_x * grad_x + grad_y * grad_y
                    along[plane + k, step] = aligned
                    total[plane + k, step] = whole

        clear_outside(along, total)

        margin += 1
        begin, finish = margin, DEEP - margin

        @pl.loop(0, (finish - begin) // GROUP)
        def _(group):
            plane = begin + group * GROUP
            c_mid, c_zz, c_xx, c_yy, c_zx, c_zy, c_xy = [coefs[3 + i] for i in range(7)]
            a_cells, t_cells, deep, tilted = {}, {}, {}, {}

            def prepare(step):
                for field, cells in ((along, a_cells), (total, t_cells)):
                    if step == 0:
                        cells[0] = [left_edge(f) for f in depth_blur(field, plane, STEPS)[0]]
                        cells[STEPS + 1] = [right_edge(f) for f in depth_blur(field, plane, 1)[0]]
                    elif step <= STEPS:
                        cells[step], _ = depth_blur(field, plane, step)
                deep[step] = [source[plane - 1 + k, step] for k in range(GROUP + 2)]
                steep = depth_slope(deep[step])
                tilted[step] = [c_zx * steep[k] + c_xy * slope[plane + k, step] for k in range(GROUP)]

            prepare(0)
            prepare(1)
            a_pair = [a_cells[0][k] + a_cells[1][k] for k in range(GROUP)]
            t_pair = [t_cells[0][k] + t_cells[1][k] for k in range(GROUP)]
            for step in range(1, STEPS + 1):
                prepare(step + 1)
                lean = depth_slope([slope[plane - 1 + k, step] for k in range(GROUP + 2)])
                for k in range(GROUP):
                    a_new = a_cells[step][k] + a_cells[step + 1][k]
                    t_new = t_cells[step][k] + t_cells[step + 1][k]
                    aligned = blur_y(a_pair[k] + a_new)
                    whole = blur_y(t_pair[k] + t_new)
                    a_pair[k], t_pair[k] = a_new, t_new
                    weight = aligned / (whole + jnp.float32(TINY * 65536.0))
                    now = deep[step][k + 1]
                    change = (
                        (c_mid * now + c_zz * (deep[step][k] + deep[step][k + 2]))
                        + (c_xx * (deep[step - 1][k + 1] + deep[step + 1][k + 1]) + c_yy * blur[plane + k, step])
                        + ((tilted[step + 1][k] - tilted[step - 1][k]) + c_zy * lean[k])
                    )
                    new = now + weight * change
                    if sweep < ITERS - 1:
                        target[plane + k, step] = new
                    else:
                        base = pl.multiple_of((plane + k - HALO) * PITCH, 8) + (step - 1) * 8
                        final[pl.ds(base, 8), :] = new

        if sweep < ITERS - 1:
            clear_outside(target)

    low_half = lanes() < 64
    copies = [pltpu.make_async_copy(bricks.at[b], out.at[b], out_sems.at[b]) for b in range(4)]
    for b in range(4):
        for half in range(2):
            for k in range(8):
                base = k * 16 + b * 2 + half
                first = final[pl.ds(base, 8, stride=PITCH), :]
                second = final[pl.ds(base + 8, 8, stride=PITCH), :]
                tile = half * 16 + k
                bricks[b, :, tile * 128 : tile * 128 + 128] = jnp.where(low_half, first, pltpu.roll(second, 64, 1))
                tile += 8
                bricks[b, :, tile * 128 : tile * 128 + 128] = jnp.where(low_half, pltpu.roll(first, 64, 1), second)
        copies[b].start()
    for copy in copies:
        copy.wait()


def smooth(coefs, lower, own, upper, interpret=False):
    field = pltpu.VMEM((DEEP + GROUP, STEPS + 2, 8, 128), jnp.float32)
    vmem = pl.BlockSpec(memory_space=pltpu.VMEM)
    return pl.pallas_call(
        smooth_kernel,
        in_specs=[vmem] * 4,
        out_specs=pl.BlockSpec(memory_space=pltpu.HBM),
        out_shape=jax.ShapeDtypeStruct((4, PLANES, STEPS * 256), jnp.float32),
        scratch_shapes=[field] * 6
        + [
            pltpu.VMEM((PLANES * PITCH, 128), jnp.float32),
            pltpu.VMEM((4, PLANES, STEPS * 256), jnp.float32),
            pltpu.SemaphoreType.DMA((4,)),
        ],
        compiler_params=pltpu.CompilerParams(vmem_limit_bytes=32 << 20),
        name="smooth_image",
        interpret=interpret,
    )(coefs, lower, own, upper)


def local(partials, aperture, owner_map, dip_class):
    sent = pack(aperture, owner_map, partials, lax.axis_size("shots"))
    received = lax.all_to_all(sent, "shots", 0, 0, tiled=True)
    image = merge(received).reshape(PLANES, STEPS, 8, 128)
    depth_count = lax.axis_size("depth")
    lower = lax.ppermute(image[PLANES - HALO :], "depth", [(i, (i + 1) % depth_count) for i in range(depth_count)])
    upper = lax.ppermute(image[:HALO], "depth", [((i + 1) % depth_count, i) for i in range(depth_count)])
    coefs = factors(owner_map, dip_class, image[0, 0])
    return smooth(coefs, lower, image, upper)


def solution(mesh):
    placed = (P("shots", "depth", None), P("shots"), P(), P())
    return jax.shard_map(
        local, mesh=mesh, in_specs=placed, out_specs=P("shots", "depth", None), check_vma=False
    )
```
